32 devices in a mesh: dp: 8 (over z, y), tensor: 4 (over x, core).
Axes of the slice: x: 2, y: 2, z: 4, core: 2. Of those that a mesh axis runs over, the one named last changes fastest.
Arguments:
- tokens_in: bfloat16 [6144, 2048], P(('dp', 'tensor')), may hold values from -6 to 6
- lengths: int32 [8, 2], P('dp'), may hold values from 64 to 640, as said below
- norm_gain: bfloat16 [2, 2048], P(None, ('dp', 'tensor')), may hold values from 0.5 to 1.5
- norm_bias: bfloat16 [2, 2048], P(None, ('dp', 'tensor')), may hold values from -2 to 2
- proj_weight: bfloat16 [2, 2048, 3, 2048], P(None, 'dp', None, 'tensor'), may hold values from -0.125 to 0.125
- proj_bias: bfloat16 [2, 3, 4, 512], P(None, None, 'tensor', 'dp'), may hold values from -3 to 3
- dense_weight: bfloat16 [2, 2048, 2048], P(None, 'tensor', 'dp'), may hold values from -2 to 2
- dense_bias: bfloat16 [2, 2048], P(None, ('dp', 'tensor')), may hold values from -3 to 3
- up_weight: bfloat16 [2, 2048, 8192], P(None, 'dp', 'tensor'), may hold values from -0.125 to 0.125
- up_bias: bfloat16 [2, 4, 2048], P(None, 'tensor', 'dp'), may hold values from -3 to 3
- down_weight: bfloat16 [2, 8192, 2048], P(None, 'tensor', 'dp'), may hold values from -0.0625 to 0.0625
- down_bias: bfloat16 [2, 2048], P(None, ('dp', 'tensor')), may hold values from -3 to 3
- cotangent: bfloat16 [6144, 2048], P(('dp', 'tensor')), may hold values from -6 to 6
Outputs:
- activations: float32 [6144, 2048], P(('dp', 'tensor'))
- input_grad: float32 [6144, 2048], P(('dp', 'tensor'))
- grad_norm_gain: float32 [2, 2048], P(None, ('dp', 'tensor'))
- grad_norm_bias: float32 [2, 2048], P(None, ('dp', 'tensor'))
- grad_proj_weight: float32 [2, 2048, 3, 2048], P(None, 'dp', None, 'tensor')
- grad_proj_bias: float32 [2, 3, 4, 512], P(None, None, 'tensor', 'dp')
- grad_dense_weight: float32 [2, 2048, 2048], P(None, 'tensor', 'dp')
- grad_dense_bias: float32 [2, 2048], P(None, ('dp', 'tensor'))
- grad_up_weight: float32 [2, 2048, 8192], P(None, 'dp', 'tensor')
- grad_up_bias: float32 [2, 4, 2048], P(None, 'tensor', 'dp')
- grad_down_weight: float32 [2, 8192, 2048], P(None, 'tensor', 'dp')
- grad_down_bias: float32 [2, 2048], P(None, ('dp', 'tensor'))
The draws below stay inside these ranges and needn't reach their ends.
Inputs may be any that keep to these rules, and one draw needn't show every extreme that they name: lengths[g] are the lengths of the two sequences of data group g in the order in which they are packed, each padded to whole blocks of 128 tokens; the two fit in 6 blocks.
All inputs are finite; a program needn't handle non-finite values.
Results may differ from the reference program's by a relative error of at most 0.018.
Values may be sent and summed in bfloat16 or wider, within the bound.
No kernel may reach another device: no remote copies, remote signals or barrier semaphores. Data moves between devices by JAX's collectives and lax.ppermute only.
A program may use at most 256 MiB of HBM per device.

```python
import math
from functools import partial
import jax
import jax.numpy as jnp
from jax import lax

D = 2048
HEADS = 32
HEAD_DIM = 64
ROT = 32
FF = 8192
LAYERS = 2
BLOCK = 128
BLK_DEV = 6
TOK_GRP = 768
TOKENS = 6144
N_DP = 8
N_TENSOR = 4


def draw_lengths(key, part):
    key = jax.random.fold_in(key, 11)
    key_long, key_short, key_order = jax.random.split(key, 3)
    longest = BLOCK * (BLK_DEV - 1)
    long_len = jax.random.randint(key_long, (N_DP,), longest - BLOCK // 2 + 1, longest + 1)
    short_len = jax.random.randint(key_short, (N_DP,), BLOCK // 2, BLOCK + 1)
    long_len = long_len.at[0].set(longest)
    short_len = short_len.at[0].set(BLOCK // 2)
    flipped = jax.random.randint(key_order, (N_DP,), 0, 2)
    first_len = jnp.where(flipped == 1, long_len, short_len)
    second_len = jnp.where(flipped == 1, short_len, long_len)
    return jnp.stack([first_len, second_len], axis=1).astype(jnp.int32)


def levels(stream_key, shape, cuts, least, top_value):
    loudness, own = 1.0, jax.random.fold_in(stream_key, 6)
    for dim, parts in cuts:
        heights = jnp.exp(jax.random.uniform(jax.random.fold_in(own, dim), (parts,), jnp.float32, least / len(cuts), top_value / len(cuts)))
        loudness = loudness * jnp.repeat(heights, shape[dim] // parts).reshape([-1 if axis == dim else 1 for axis in range(len(shape))])
    return loudness


def normal_values(own_key, dims, width, bound, shards=(), held_as=jnp.bfloat16):
    level = levels(own_key, dims, shards, -0.22, 0.18) if shards else 1.0
    drawn = jax.random.normal(own_key, dims, jnp.float32) * width * level
    return jnp.minimum(jnp.maximum(drawn, -bound), bound).astype(held_as)


def setup_inputs(seed: int = 0) -> dict:
    splits = jax.random.split(jax.random.key(seed), 14)
    tokens_in = normal_values(splits[0], (TOKENS, D), 1.0, 6.0, ((0, 32),))
    lengths = draw_lengths(jax.random.fold_in(splits[13], 71), 0)
    norm_gain = jnp.clip(1.0 + 0.1 * jax.random.normal(splits[2], (LAYERS, D), jnp.float32), 0.5, 1.5).astype(jnp.bfloat16)
    norm_bias = normal_values(splits[3], (LAYERS, D), 0.3, 2.0, ((1, 32),))
    proj_weight = normal_values(splits[4], (LAYERS, D, 3, D), D ** -0.5, 0.125, ((1, 8), (3, 4)))
    proj_bias = normal_values(splits[5], (LAYERS, 3, N_TENSOR, D // N_TENSOR), 0.5, 3.0, ((2, 4), (3, 8)))
    dense_weight = normal_values(splits[6], (LAYERS, D, D), (max(D // 256, 1)) ** -0.5, 2.0, ((1, 4), (2, 8)))
    dense_bias = normal_values(splits[7], (LAYERS, D), 0.5, 3.0, ((1, 32),))
    up_weight = normal_values(splits[8], (LAYERS, D, FF), D ** -0.5, 0.125, ((1, 8), (2, 4)))
    up_bias = normal_values(splits[9], (LAYERS, N_TENSOR, FF // N_TENSOR), 0.5, 3.0, ((1, 4), (2, 8)))
    down_weight = normal_values(splits[10], (LAYERS, FF, D), FF ** -0.5, 0.0625, ((1, 4), (2, 8)))
    down_bias = normal_values(splits[11], (LAYERS, D), 0.5, 3.0, ((1, 32),))
    cotangent = normal_values(splits[12], (TOKENS, D), 1.0, 6.0, ((0, 32),))
    return {"tokens_in": tokens_in, "lengths": lengths, "norm_gain": norm_gain, "norm_bias": norm_bias, "proj_weight": proj_weight, "proj_bias": proj_bias, "dense_weight": dense_weight, "dense_bias": dense_bias, "up_weight": up_weight, "up_bias": up_bias, "down_weight": down_weight, "down_bias": down_bias, "cotangent": cotangent}


highest = lax.Precision.HIGHEST
neg_large = -1e+30

@jax.custom_vjp
def low(v):
    return lax.optimization_barrier(v.astype(jnp.bfloat16)).astype(jnp.float32)

@jax.custom_vjp
def low_back(v):
    return v

def low_keep(v):
    return (low(v), None)

def low_pass(kept, grad):
    return (grad,)

def back_keep(v):
    return (v, None)

def back_low(kept, grad):
    return (low(grad),)
low.defvjp(low_keep, low_pass)
low_back.defvjp(back_keep, back_low)

def norm_rows(rows, scale, shift):
    centre = rows - lax.optimization_barrier(jnp.mean(rows, axis=-1, keepdims=True))
    spread = lax.optimization_barrier(jnp.mean(centre * centre, axis=-1, keepdims=True))
    return centre * lax.rsqrt(spread + 1e-05) * scale + shift

def layout(lens, total, block):
    steps_index = jnp.arange(total, dtype=jnp.int32)
    blocks_first = (lens[0] + block - 1) // block
    second_start = blocks_first * block
    in_first = steps_index < lens[0]
    in_second = (steps_index >= second_start) & (steps_index < second_start + lens[1])
    segment = jnp.where(in_first, 0, jnp.where(in_second, 1, steps_index + 2)).astype(jnp.int32)
    position = jnp.where(in_first, steps_index, jnp.where(in_second, steps_index - second_start, 0)).astype(jnp.int32)
    return (segment, position)

def rotary_tables(position):
    half_rot = ROT // 2
    freqs = 10000.0 ** (-(jnp.arange(half_rot).astype(jnp.float32) * 2.0) / ROT)
    angles = position.astype(jnp.float32)[:, None] * freqs[None, :]
    return (jnp.cos(angles)[:, None, :], jnp.sin(angles)[:, None, :])

def rotate(field, cosine, sine):
    half_rot = cosine.shape[-1]
    first = field[..., :half_rot]
    second = field[..., half_rot:2 * half_rot]
    remain = field[..., 2 * half_rot:]
    return jnp.concatenate([first * cosine - second * sine, second * cosine + first * sine, remain], axis=-1)

def group_attention(pieces):
    query_rows, key_rows, value_rows, segment = pieces
    token_index = jnp.arange(segment.shape[0], dtype=jnp.int32)
    allowed = (segment[:, None] == segment[None, :]) & (token_index[None, :] <= token_index[:, None])
    scores = jnp.einsum('qhd,khd->hqk', query_rows, key_rows, precision=highest) * (1.0 / math.sqrt(HEAD_DIM))
    scores = low_back(scores)
    masked = jnp.where(allowed[None], scores, neg_large)
    weights = low(jax.nn.softmax(masked, axis=-1))
    return jnp.einsum('hqk,khd->qhd', weights, value_rows, precision=highest)

def layer_forward(stream, params, segment, tables):
    norm_scale, norm_shift, proj_w, proj_b, dense_w, dense_b, up_w, up_b, down_w, down_b = params
    total = stream.shape[0]
    cosine, sine = tables
    normed = low(norm_rows(stream, norm_scale, norm_shift))
    mixed = jnp.dot(normed, proj_w.reshape(D, 3 * D), precision=highest) + proj_b.reshape(3 * D)
    mixed = low_back(mixed).reshape(total, 3, HEADS, HEAD_DIM)
    query_rows = low(rotate(mixed[:, 0], cosine, sine))
    key_rows = low(rotate(mixed[:, 1], cosine, sine))
    value_rows = low(mixed[:, 2])
    grouped_shape = (N_DP, TOK_GRP, HEADS, HEAD_DIM)
    attended = lax.map(jax.checkpoint(group_attention), (query_rows.reshape(grouped_shape), key_rows.reshape(grouped_shape), value_rows.reshape(grouped_shape), segment.reshape(N_DP, TOK_GRP)))
    attended = low(low_back(attended.reshape(total, D)))
    hidden_pre = low_back(jnp.dot(normed, up_w, precision=highest) + up_b.reshape(FF))
    hidden = low(jax.nn.gelu(hidden_pre, approximate=True))
    branch = low_back(jnp.dot(attended, dense_w, precision=highest) + jnp.dot(hidden, down_w, precision=highest))
    return stream + branch + dense_b + down_b

def reference(tokens_in, lengths, norm_gain, norm_bias, proj_weight, proj_bias, dense_weight, dense_bias, up_weight, up_bias, down_weight, down_bias, cotangent):
    segment, position = jax.vmap(partial(layout, total=TOK_GRP, block=BLOCK))(lengths)
    segment = segment.reshape(TOKENS)
    tables = rotary_tables(position.reshape(TOKENS))
    floats = (norm_gain.astype(jnp.float32), norm_bias.astype(jnp.float32), proj_weight.astype(jnp.float32), proj_bias.astype(jnp.float32), dense_weight.astype(jnp.float32), dense_bias.astype(jnp.float32), up_weight.astype(jnp.float32), up_bias.astype(jnp.float32), down_weight.astype(jnp.float32), down_bias.astype(jnp.float32))

    def whole(stream, params):
        for layer_index in range(LAYERS):
            stream = layer_forward(stream, tuple((member[layer_index] for member in params)), segment, tables)
        return stream
    result, pull = jax.vjp(whole, tokens_in.astype(jnp.float32), floats)
    stream_grad, grads = pull(cotangent.astype(jnp.float32))
    return (result, stream_grad, grads[0], grads[1], grads[2], grads[3], grads[4], grads[5], grads[6], grads[7], grads[8], grads[9])
```

```python
from functools import partial
import math

import jax
import jax.numpy as jnp
from jax import lax
from jax.experimental import pallas as pl
from jax.experimental.pallas import tpu as pltpu
from jax.sharding import PartitionSpec as P

HEAD_DIM = 64
ROT = 32
BLOCK = 128
LANES = 128
TILE = 256
MID = 1

neg_large = -1e30
f32 = jnp.float32
bf16 = jnp.bfloat16


def swap(value, axis, bit):
    size = lax.axis_size(axis)
    return lax.ppermute(value, axis, [(i, i ^ (1 << bit)) for i in range(size)])


def side_bits():
    count = (lax.axis_size("dp") - 1).bit_length()
    return [bit for bit in range(count - 1, MID, -1)] + [0]


def slice_order():
    sides = side_bits()
    me = lax.axis_index("dp")
    base = me - (((me >> MID) & 1) << MID)
    order = []
    for k in range(1 << len(sides)):
        mask = sum(((k >> s) & 1) << bit for s, bit in enumerate(sides))
        for mid in range(2):
            order.append((base ^ mask) | (mid << MID))
    return jnp.stack(order).astype(jnp.int32)


def pick(pair_first, pair_second, bit):
    return jnp.where(bit == 0, pair_first, pair_second)


def pair_up(keep, received, mid, axis):
    return jnp.concatenate(
        [pick(keep, received, mid), pick(received, keep, mid)], axis=axis
    )


def spread(block, axis):
    blocks = [block]
    for bit in side_bits():
        blocks = blocks + [swap(value, "dp", bit) for value in blocks]
    return jnp.concatenate(blocks, axis=axis)


def spread_sum(product):
    sides = side_bits()
    arrived = [[] for _ in range(1 << len(sides))]

    def total(k):
        part = product(k)
        for value in arrived[k]:
            part = part + value.astype(f32)
        return part.astype(bf16)

    for s in reversed(range(len(sides))):
        for k in reversed(range(1 << s, 2 << s)):
            arrived[k - (1 << s)].append(swap(total(k), "dp", sides[s]))
    return total(0)


def gather_rows(own):
    chunks = [own]
    chunks = chunks + [swap(value, "dp", MID) for value in chunks]
    chunks = chunks + [swap(value, "tensor", 1) for value in chunks]
    chunks = chunks + [swap(value, "tensor", 0) for value in chunks]
    return jnp.concatenate(chunks, axis=0)


def scatter_rows(product, rows):
    high = product(6 * rows, 8 * rows).astype(bf16)
    core_high = swap(high, "tensor", 0)
    low = product(4 * rows, 6 * rows).astype(bf16)
    core_low = swap(low, "tensor", 0)

    def chunk(k, *others):
        source = core_high if k >= 2 else core_low
        at = (k % 2) * rows
        part = product(k * rows, (k + 1) * rows) + source[at : at + rows].astype(f32)
        for value in others:
            part = part + value.astype(f32)
        return part

    x_high = swap(chunk(3).astype(bf16), "tensor", 1)
    x_low = swap(chunk(2).astype(bf16), "tensor", 1)
    mid = swap(chunk(1, x_high).astype(bf16), "dp", MID)
    return chunk(0, x_low, mid)


def copy_kernel(order_ref, in_ref, out_ref):
    out_ref[...] = in_ref[...].astype(out_ref.dtype)


def reorder(value, order, dtype, back=False):
    rows, width = value.shape
    count = order.shape[0]
    part = width // count
    if part % LANES:
        blocks = value.reshape(rows, count, part)
        index = jnp.argsort(order) if back else order
        return jnp.take(blocks, index, axis=1).reshape(rows, width).astype(dtype)
    there = pl.BlockSpec((rows, part), lambda i, order_ref: (0, order_ref[i]))
    here = pl.BlockSpec((rows, part), lambda i, order_ref: (0, i))
    return pl.pallas_call(
        copy_kernel,
        grid_spec=pltpu.PrefetchScalarGridSpec(
            num_scalar_prefetch=1,
            grid=(count,),
            in_specs=[here if back else there],
            out_specs=there if back else here,
        ),
        out_shape=jax.ShapeDtypeStruct((rows, width), dtype),
    )(order, value)


def layout(lens, total, block):
    steps_index = jnp.arange(total, dtype=jnp.int32)
    blocks_first = (lens[0] + block - 1) // block
    second_start = blocks_first * block
    in_first = steps_index < lens[0]
    in_second = (steps_index >= second_start) & (steps_index < second_start + lens[1])
    return jnp.where(in_first, steps_index, jnp.where(in_second, steps_index - second_start, 0))


def rotary_tables(position):
    half_rot = ROT // 2
    freqs = 10000.0 ** (-(jnp.arange(half_rot).astype(f32) * 2.0) / ROT)
    angles = position.astype(f32)[..., None] * freqs
    cosine, sine = jnp.cos(angles), jnp.sin(angles)
    rest = position.shape + (HEAD_DIM - ROT,)
    ones, zeros, none = jnp.ones(rest, f32), jnp.zeros(rest, f32), jnp.zeros_like(sine)
    heads = LANES // HEAD_DIM
    tables = (
        jnp.concatenate([cosine, cosine, ones] * heads, axis=-1),
        jnp.concatenate([-sine, none, zeros] * heads, axis=-1),
        jnp.concatenate([none, sine, zeros] * heads, axis=-1),
    )
    return tables


def turn(field, cos, above, below, back=False):
    up = pltpu.roll(field, LANES - ROT // 2, 1) * above
    down = pltpu.roll(field, ROT // 2, 1) * below
    return field * cos - (up + down) if back else field * cos + (up + down)


def allowed_bias(scalars, group, first_row, rows, cols):
    first_len, second_len = scalars[2 * group], scalars[2 * group + 1]
    second_start = ((first_len + BLOCK - 1) // BLOCK) * BLOCK
    row = first_row + lax.broadcasted_iota(jnp.int32, (rows, 1), 0)
    in_second = (row >= second_start) & (row < second_start + second_len)
    start = jnp.where(row < first_len, 0, jnp.where(in_second, second_start, row))
    col = lax.broadcasted_iota(jnp.int32, (rows, cols), 1)
    return jnp.where((col >= start) & (col <= row), 0.0, neg_large)


def chunk_places(scalars, rows):
    me = scalars[4]
    return [pl.multiple_of((me ^ ((r % 2) * 2 + r // 2)) * rows, 64) for r in range(4)]


def head_mask(head):
    lane = lax.broadcasted_iota(jnp.int32, (1, LANES), 1)
    return jnp.where(lane // HEAD_DIM == head, 1.0, 0.0).astype(bf16)


def nt(left, right):
    return lax.dot_general(left, right, (((1,), (1,)), ((), ())), preferred_element_type=f32)


def nn(left, right):
    return jnp.dot(left, right, preferred_element_type=f32)


def tn(left, right):
    return lax.dot_general(left, right, (((0,), (0,)), ((), ())), preferred_element_type=f32)


def attention_kernel(
    scalars, mixed_ref, cos_ref, above_ref, below_ref, out_ref, kept_ref, sums_ref, held
):
    group = pl.program_id(0)
    rows = mixed_ref.shape[2]
    width = mixed_ref.shape[3] // 3
    total = 4 * rows
    places = chunk_places(scalars, rows)
    for r in range(4):
        at = pl.ds(places[r], rows)
        cos, above, below = cos_ref[0, at, :], above_ref[0, at, :], below_ref[0, at, :]
        for part in range(0, 2 * width, LANES):
            turned = turn(mixed_ref[r, 0, :, part : part + LANES], cos, above, below)
            if part < width:
                turned = turned.astype(bf16) * HEAD_DIM**-0.5
            kept_ref[0, at, part : part + LANES] = turned.astype(bf16)
        kept_ref[0, at, 2 * width :] = mixed_ref[r, 0, :, 2 * width :].astype(bf16)
    for first in range(0, total, TILE):
        cols = first + TILE
        bias = allowed_bias(scalars, group, first, TILE, cols)
        for pair in range(0, width, LANES):
            query = kept_ref[0, first:cols, pair : pair + LANES]
            key = kept_ref[0, :cols, width + pair : width + pair + LANES]
            value = kept_ref[0, :cols, 2 * width + pair : 2 * width + pair + LANES]
            result = None
            for head in range(LANES // HEAD_DIM):
                mask = head_mask(head)
                scores = nt(query * mask, key) + bias
                top = jnp.max(scores, axis=1, keepdims=True)
                expo = jnp.exp(scores - top)
                mass = jnp.sum(expo, axis=1, keepdims=True)
                probs16 = (expo * (1.0 / mass)).astype(bf16)
                mine = nn(probs16, value * mask)
                result = mine if result is None else result + mine
                at_head = pair // HEAD_DIM + head
                sums_ref[0, first:cols, at_head : at_head + 1] = top + jnp.log(mass)
            held[first:cols, pair : pair + LANES] = result.astype(bf16)
    for r in range(4):
        out_ref[r, 0] = held[pl.ds(places[r], rows), :]


def attention_back_kernel(
    scalars,
    kept_ref,
    sums_ref,
    grad_ref,
    cos_ref,
    above_ref,
    below_ref,
    out_ref,
    held,
    query_grad,
    key_grad,
    value_grad,
):
    group = pl.program_id(0)
    rows = grad_ref.shape[2]
    width = grad_ref.shape[3]
    total = 4 * rows
    places = chunk_places(scalars, rows)
    for r in range(4):
        held[pl.ds(places[r], rows), :] = grad_ref[r, 0]
    for first in reversed(range(0, total, TILE)):
        cols = first + TILE
        bias = allowed_bias(scalars, group, first, TILE, cols)
        for pair in range(0, width, LANES):
            lanes = slice(pair, pair + LANES)
            query = kept_ref[0, first:cols, pair : pair + LANES]
            key = kept_ref[0, :cols, width + pair : width + pair + LANES]
            value = kept_ref[0, :cols, 2 * width + pair : 2 * width + pair + LANES]
            grad = held[first:cols, lanes]
            grads = [None, None, None]
            for head in range(LANES // HEAD_DIM):
                mask = head_mask(head)
                at_head = pair // HEAD_DIM + head
                query_head, grad_head = query * mask, grad * mask
                scores = nt(query_head, key) + bias
                probs = jnp.exp(scores - sums_ref[0, first:cols, at_head : at_head + 1])
                prob_grad = nt(grad_head, value)
                mean = jnp.sum(probs * prob_grad, axis=1, keepdims=True)
                score_grad = (probs * (prob_grad - mean)).astype(bf16)
                mine = (
                    nn(score_grad, key * mask),
                    tn(score_grad, query_head),
                    tn(probs.astype(bf16), grad_head),
                )
                grads = [m if g is None else g + m for g, m in zip(grads, mine)]
            query_grad[first:cols, lanes] = grads[0]
            if cols == total:
                key_grad[:, lanes] = grads[1]
                value_grad[:, lanes] = grads[2]
            else:
                key_grad[:cols, lanes] += grads[1]
                value_grad[:cols, lanes] += grads[2]
    for r in range(4):
        at = pl.ds(places[r], rows)
        cos, above, below = cos_ref[0, at, :], above_ref[0, at, :], below_ref[0, at, :]
        for pair in range(0, width, LANES):
            query = turn(query_grad[at, pair : pair + LANES] * HEAD_DIM**-0.5, cos, above, below, True)
            key = turn(key_grad[at, pair : pair + LANES], cos, above, below, True)
            out_ref[r, 0, :, pair : pair + LANES] = query.astype(bf16)
            out_ref[r, 0, :, width + pair : width + pair + LANES] = key.astype(bf16)
        out_ref[r, 0, :, 2 * width :] = value_grad[at, :].astype(bf16)


def chunk_spec(rows, width):
    return pl.BlockSpec((4, 1, rows, width), lambda g, scalars: (0, g, 0, 0))


def group_spec(total, width):
    return pl.BlockSpec((1, total, width), lambda g, scalars: (g, 0, 0))


def attention_forward(mixed, tables, scalars, rows):
    width = mixed.shape[1] // 3
    total = 4 * rows
    attended, kept, sums = pl.pallas_call(
        attention_kernel,
        grid_spec=pltpu.PrefetchScalarGridSpec(
            num_scalar_prefetch=1,
            grid=(2,),
            in_specs=[chunk_spec(rows, 3 * width)] + [group_spec(total, LANES)] * 3,
            out_specs=[
                chunk_spec(rows, width),
                group_spec(total, 3 * width),
                group_spec(total, LANES),
            ],
            scratch_shapes=[pltpu.VMEM((total, width), bf16)],
        ),
        out_shape=[
            jax.ShapeDtypeStruct((4, 2, rows, width), bf16),
            jax.ShapeDtypeStruct((2, total, 3 * width), bf16),
            jax.ShapeDtypeStruct((2, total, LANES), f32),
        ],
        compiler_params=pltpu.CompilerParams(vmem_limit_bytes=40 << 20),
        cost_estimate=pl.CostEstimate(
            flops=16 * total * total * width, bytes_accessed=40 * total * width, transcendentals=0
        ),
    )(scalars, mixed.reshape(4, 2, rows, 3 * width), *tables)
    return attended.reshape(8 * rows, width), kept, sums


def attention_backward(kept, sums, grad16, tables, scalars, rows):
    width = grad16.shape[1]
    total = 4 * rows
    mixed_grad = pl.pallas_call(
        attention_back_kernel,
        grid_spec=pltpu.PrefetchScalarGridSpec(
            num_scalar_prefetch=1,
            grid=(2,),
            in_specs=[
                group_spec(total, 3 * width),
                group_spec(total, LANES),
                chunk_spec(rows, width),
            ]
            + [group_spec(total, LANES)] * 3,
            out_specs=chunk_spec(rows, 3 * width),
            scratch_shapes=[pltpu.VMEM((total, width), bf16)]
            + [pltpu.VMEM((total, width), f32)] * 3,
        ),
        out_shape=jax.ShapeDtypeStruct((4, 2, rows, 3 * width), bf16),
        compiler_params=pltpu.CompilerParams(vmem_limit_bytes=40 << 20),
        cost_estimate=pl.CostEstimate(
            flops=40 * total * total * width, bytes_accessed=40 * total * width, transcendentals=0
        ),
    )(scalars, kept, sums, grad16.reshape(4, 2, rows, width), *tables)
    return mixed_grad.reshape(8 * rows, 3 * width)


def norm_rows(rows, scale, shift):
    centre = rows - jnp.mean(rows, axis=-1, keepdims=True)
    spread_of = jnp.mean(centre * centre, axis=-1, keepdims=True)
    return centre * lax.rsqrt(spread_of + 1e-05) * scale + shift


def halves(value, half, axis):
    size = value.shape[axis] // 2
    return lax.dynamic_slice_in_dim(value, half * size, size, axis)


def fetch(take, mid, axis):
    keep, received = take(mid), swap(take(1 - mid), "dp", MID)
    return spread(pair_up(keep, received, mid, axis), axis)


def owned(product, mid, axis):
    total = spread_sum(product)
    keep = halves(total, mid, axis)
    received = swap(halves(total, 1 - mid, axis), "dp", MID)
    return pick(keep, received, mid).astype(f32), pick(received, keep, mid).astype(f32)


def layer_forward(stream, scale_row, shift_row, out_shift, weights, in_shift, tables, scalars, last):
    proj_full, up_full, out_full = weights
    proj_shift, up_shift = in_shift
    rows = stream.shape[0]
    normed = norm_rows(stream, scale_row, shift_row).astype(bf16)
    gathered = gather_rows(normed)
    mixed = nn(gathered, proj_full) + proj_shift
    attended, kept, sums = attention_forward(mixed, tables, scalars, rows)
    hidden_pre = nn(gathered, up_full) + up_shift
    hidden16 = jax.nn.gelu(hidden_pre, approximate=True).astype(bf16)
    features = jnp.concatenate([attended, hidden16], axis=1)
    branch = scatter_rows(lambda lo, hi: nn(features[lo:hi], out_full), rows)
    return stream + branch + out_shift, (gathered, kept, sums, features, hidden_pre)


def layer_backward(grad_in, stream_in, scale_row, shift_row, weights, saved, tables, scalars, mid):
    proj_full, up_full, out_full = weights
    gathered, kept, sums, features, hidden_pre = saved
    rows, width = stream_in.shape
    parts = 1 << len(side_bits())
    part = width // parts
    heads_width = proj_full.shape[1] // 3
    bias_grad = jnp.sum(grad_in, axis=0)
    grad16 = gather_rows(grad_in.astype(bf16))
    out_grads = owned(
        lambda k: tn(features, grad16[:, k * part : (k + 1) * part]), mid, 1
    )
    attended_grad = nt(grad16, out_full[:heads_width]).astype(bf16)
    mixed_grad = attention_backward(kept, sums, attended_grad, tables, scalars, rows)
    hidden_grad = nt(grad16, out_full[heads_width:])
    unused, gelu_pull = jax.vjp(partial(jax.nn.gelu, approximate=True), hidden_pre)
    pre_grad = gelu_pull(hidden_grad)[0].astype(bf16)
    up_grads = owned(
        lambda k: tn(gathered[:, k * part : (k + 1) * part], pre_grad), mid, 0
    )
    proj_grads = owned(
        lambda k: tn(gathered[:, k * part : (k + 1) * part], mixed_grad), mid, 0
    )
    in_bgrad = (
        jnp.sum(mixed_grad, axis=0, dtype=f32),
        jnp.sum(pre_grad, axis=0, dtype=f32),
    )
    both = jnp.concatenate([mixed_grad, pre_grad], axis=1)
    both_full = jnp.concatenate([proj_full, up_full], axis=1)
    normed_grad = scatter_rows(lambda lo, hi: nt(both[lo:hi], both_full), rows)
    unused_norm, norm_pull = jax.vjp(norm_rows, stream_in, scale_row, shift_row)
    stream_grad, scale_grad, shift_grad = norm_pull(normed_grad)
    norm_grads = jnp.stack([scale_grad, shift_grad, bias_grad])
    return grad_in + stream_grad, (proj_grads, up_grads, out_grads), in_bgrad, norm_grads


def small_sums(norm_grads, in_bgrads, mid):
    sides = side_bits()
    tensor = lax.axis_index("tensor")
    layers, kinds, width = norm_grads.shape
    sums = norm_grads.reshape(layers * kinds, -1)
    biases = in_bgrads
    split = biases.shape[0]
    for s in reversed(range(len(sides))):
        half = sums.shape[1] // 2
        sent = jnp.concatenate([biases, sums[:, half:].reshape(-1)])
        received = swap(sent, "dp", sides[s])
        biases = biases + received[:split]
        sums = sums[:, :half] + received[split:].reshape(-1, half)
    half = sums.shape[1] // 2
    sent = jnp.concatenate([biases, halves(sums, 1 - mid, 1).reshape(-1)])
    received = swap(sent, "dp", MID)
    both = jnp.stack([pick(biases, received[:split], mid), pick(received[:split], biases, mid)])
    sums = halves(sums, mid, 1) + received[split:].reshape(-1, half)
    for bit in (1, 0):
        mine = (tensor >> bit) & 1
        sums = halves(sums, mine, 1) + swap(halves(sums, 1 - mine, 1), "tensor", bit)
    return sums.reshape(layers, kinds, -1), both


def shards(
    tokens_in,
    lengths,
    norm_gain,
    norm_bias,
    proj_weight,
    proj_bias,
    dense_weight,
    dense_bias,
    up_weight,
    up_bias,
    down_weight,
    down_bias,
    cotangent,
):
    rows, width = tokens_in.shape
    layer_count = proj_weight.shape[0]
    n_dp = lax.axis_size("dp")
    dp = lax.axis_index("dp")
    tensor = lax.axis_index("tensor")
    mid = (dp >> MID) & 1
    order = slice_order()

    def weights_of(l):
        def take_proj(half):
            return halves(proj_weight[l], half, 2).reshape(proj_weight.shape[1], -1)

        def take_up(half):
            return halves(up_weight[l], half, 1)

        def take_out(half):
            return jnp.concatenate(
                [halves(dense_weight[l], half, 0), halves(down_weight[l], half, 0)], axis=0
            )

        return (fetch(take_proj, mid, 0), fetch(take_up, mid, 0), fetch(take_out, mid, 1))

    weights = [weights_of(l) for l in range(layer_count)]

    owners = n_dp * lax.axis_size("tensor")
    small = jnp.concatenate(
        [
            value.reshape(-1)
            for value in (norm_gain, norm_bias, dense_bias, down_bias, proj_bias, up_bias)
        ]
    )
    everyone = lax.all_gather(small, ("dp", "tensor"), axis=0)
    each = norm_gain.shape[1]
    rows_count = 4 * layer_count
    at = rows_count * each
    norm_parts = everyone[:, :at].reshape(n_dp, -1, rows_count, each)[order]
    norm_parts = jnp.transpose(norm_parts, (2, 0, 1, 3)).reshape(4, layer_count, width).astype(f32)
    same_heads = lax.dynamic_index_in_dim(
        everyone[:, at:].reshape(n_dp, -1, everyone.shape[1] - at), tensor, 1, keepdims=False
    )
    same_heads = halves(same_heads, mid, 0).astype(f32)
    proj_each, up_each = proj_bias.shape[3], up_bias.shape[2]
    proj_at = layer_count * 3 * proj_each
    proj_shift = jnp.transpose(
        same_heads[:, :proj_at].reshape(-1, layer_count * 3, proj_each), (1, 0, 2)
    ).reshape(layer_count, -1)
    up_shift = jnp.transpose(
        same_heads[:, proj_at:].reshape(-1, layer_count, up_each), (1, 0, 2)
    ).reshape(layer_count, -1)

    lens = jnp.concatenate([lengths, swap(lengths, "dp", MID)], axis=0)
    scalars = jnp.concatenate([lens.reshape(-1), tensor[None].astype(jnp.int32)]).astype(jnp.int32)
    tables = rotary_tables(jax.vmap(partial(layout, total=4 * rows, block=BLOCK))(lens))

    stream = reorder(tokens_in, order, f32)
    grad_stream = reorder(cotangent, order, f32)
    saved = []
    for l in range(layer_count):
        stream_in = stream
        stream, kept = layer_forward(
            stream,
            norm_parts[0, l],
            norm_parts[1, l],
            norm_parts[2, l] + norm_parts[3, l],
            weights[l],
            (proj_shift[l], up_shift[l]),
            tables,
            scalars,
            l == layer_count - 1,
        )
        saved.append((stream_in, kept))
    weight_grads = [None] * layer_count
    in_bgrads = [None] * layer_count
    norm_grads = [None] * layer_count
    for l in reversed(range(layer_count)):
        stream_in, kept = saved[l]
        grad_stream, weight_grads[l], in_bgrads[l], norm_grads[l] = layer_backward(
            grad_stream,
            stream_in,
            norm_parts[0, l],
            norm_parts[1, l],
            weights[l],
            kept,
            tables,
            scalars,
            mid,
        )
    heads_width = weights[0][0].shape[1] // 3
    proj_out, up_out, dense_out, down_out = [], [], [], []
    for l in range(layer_count):
        proj_grads, up_grads, out_grads = weight_grads[l]
        proj_out.append(
            jnp.concatenate([g.reshape(g.shape[0], 3, -1) for g in proj_grads], axis=2)
        )
        up_out.append(jnp.concatenate(up_grads, axis=1))
        dense_out.append(jnp.concatenate([g[:heads_width] for g in out_grads], axis=0))
        down_out.append(jnp.concatenate([g[heads_width:] for g in out_grads], axis=0))

    flat = jnp.concatenate([value for pair in in_bgrads for value in pair])
    norm_owned, bias_both = small_sums(jnp.stack(norm_grads), flat, mid)
    per_layer = flat.shape[0] // layer_count
    bias_both = bias_both.reshape(2, layer_count, per_layer)
    proj_b = jnp.transpose(
        bias_both[:, :, : 3 * heads_width].reshape(2, layer_count, 3, heads_width), (1, 2, 0, 3)
    ).reshape(layer_count, 3, 1, 2 * heads_width)
    up_b = jnp.transpose(bias_both[:, :, 3 * heads_width :], (1, 0, 2)).reshape(layer_count, 1, -1)
    return (
        reorder(stream, order, f32, True),
        reorder(grad_stream, order, f32, True),
        norm_owned[:, 0],
        norm_owned[:, 1],
        jnp.stack(proj_out),
        lax.dynamic_slice_in_dim(proj_b, dp * proj_each, proj_each, 3),
        jnp.stack(dense_out),
        norm_owned[:, 2],
        jnp.stack(up_out),
        lax.dynamic_slice_in_dim(up_b, dp * up_each, up_each, 2),
        jnp.stack(down_out),
        norm_owned[:, 2],
    )


def solution(mesh):
    in_specs = (
        P(("dp", "tensor"), None),
        P("dp", None),
        P(None, ("dp", "tensor")),
        P(None, ("dp", "tensor")),
        P(None, "dp", None, "tensor"),
        P(None, None, "tensor", "dp"),
        P(None, "tensor", "dp"),
        P(None, ("dp", "tensor")),
        P(None, "dp", "tensor"),
        P(None, "tensor", "dp"),
        P(None, "tensor", "dp"),
        P(None, ("dp", "tensor")),
        P(("dp", "tensor"), None),
    )
    out_specs = (
        P(("dp", "tensor"), None),
        P(("dp", "tensor"), None),
        P(None, ("dp", "tensor")),
        P(None, ("dp", "tensor")),
        P(None, "dp", None, "tensor"),
        P(None, None, "tensor", "dp"),
        P(None, "tensor", "dp"),
        P(None, ("dp", "tensor")),
        P(None, "dp", "tensor"),
        P(None, "tensor", "dp"),
        P(None, "tensor", "dp"),
        P(None, ("dp", "tensor")),
    )
    return jax.shard_map(shards, mesh=mesh, in_specs=in_specs, out_specs=out_specs, check_vma=False)
```

```python
from functools import partial
import math

import jax
import jax.numpy as jnp
from jax import lax
from jax.experimental import pallas as pl
from jax.experimental.pallas import tpu as pltpu
from jax.sharding import PartitionSpec as P

HEAD_DIM = 64
ROT = 32
BLOCK = 128
LANES = 128
TILE = 256
MID = 1

TICK = 1_200_000_000

neg_large = -1e30
f32 = jnp.float32
bf16 = jnp.bfloat16


def swap(value, axis, bit):
    size = lax.axis_size(axis)
    return lax.ppermute(value, axis, [(i, i ^ (1 << bit)) for i in range(size)])


def tick_kernel(in_ref, out_ref):
    out_ref[0, 0] = in_ref[0, 0]


def tick(scalar, count):
    spec = pl.BlockSpec(memory_space=pltpu.SMEM)
    result = pl.pallas_call(
        tick_kernel,
        in_specs=[spec],
        out_specs=spec,
        out_shape=jax.ShapeDtypeStruct((1, 1), f32),
        cost_estimate=pl.CostEstimate(flops=count * TICK, bytes_accessed=0, transcendentals=0),
    )(scalar.reshape(1, 1))
    return result[0, 0]


class Sequence:
    def __init__(self, scalar, always):
        self.scalar = scalar
        self.always = always

    def gate(self, *values):
        *values, self.scalar = lax.optimization_barrier((*values, self.scalar))
        return values

    def run(self, step, *values, apart=False):
        values = self.gate(*values)
        if apart:
            shapes = jax.eval_shape(step, *values)

            def never(*others):
                return jax.tree.map(lambda shape: jnp.zeros(shape.shape, shape.dtype), shapes)

            result = lax.cond(self.always, step, never, *values)
        else:
            result = step(*values)
        leaves, tree = jax.tree.flatten(result)
        return jax.tree.unflatten(tree, self.gate(*leaves))

    def start(self, value, axis, bit):
        (value,) = self.gate(value)
        return swap(value, axis, bit)

    def wait(self, value):
        (value,) = self.gate(value)
        return value

    def settle(self, step, *values, beside=None):
        def both(*moved):
            return (step(*moved), beside()) if beside else step(*moved)

        return self.run(both, *values, apart=True)

    def tick(self, count):
        self.scalar = tick(self.scalar, count)

    def swap(self, value, axis, bit):
        return self.settle(lambda moved: swap(moved, axis, bit), value)


def side_bits():
    count = (lax.axis_size("dp") - 1).bit_length()
    return [bit for bit in range(count - 1, MID, -1)] + [0]


def slice_order():
    sides = side_bits()
    me = lax.axis_index("dp")
    base = me - (((me >> MID) & 1) << MID)
    order = []
    for k in range(1 << len(sides)):
        mask = sum(((k >> s) & 1) << bit for s, bit in enumerate(sides))
        for mid in range(2):
            order.append((base ^ mask) | (mid << MID))
    return jnp.stack(order).astype(jnp.int32)


def slice_places():
    sides = side_bits()
    every = jnp.arange(lax.axis_size("dp"), dtype=jnp.int32)
    apart = every ^ lax.axis_index("dp")
    place = (every >> MID) & 1
    for s, bit in enumerate(sides):
        place = place + (((apart >> bit) & 1) << (s + 1))
    return place


def pick(pair_first, pair_second, bit):
    return jnp.where(bit == 0, pair_first, pair_second)


def pair_up(keep, received, bit, axis):
    return jnp.concatenate(
        [pick(keep, received, bit), pick(received, keep, bit)], axis=axis
    )


class Spread:
    def __init__(self, seq, block, axis):
        self.seq, self.axis = seq, axis
        self.sides = side_bits()
        self.far_count = 1 << (len(self.sides) - 1)
        self.blocks = {0: block}

    def move(self, ks):
        for k in ks:
            if k != ks[0]:
                self.arrived(ks)
            s = k.bit_length() - 1
            self.blocks[k] = self.seq.start(self.blocks[k - (1 << s)], "dp", self.sides[s])

    def arrived(self, ks):
        last = max(k for k in ks if k in self.blocks)
        self.blocks[last] = self.seq.wait(self.blocks[last])

    def far(self):
        self.move(range(1, self.far_count))

    def far_wait(self):
        self.arrived(range(1, self.far_count))

    def near(self):
        self.move([self.far_count])

    def near_wait(self):
        self.arrived([self.far_count])

    def last(self):
        self.move(range(self.far_count + 1, 2 * self.far_count))

    def last_wait(self):
        self.arrived(range(self.far_count + 1, 2 * self.far_count))

    def plain(self, window=None):
        parts = [self.blocks[k] for k in sorted(self.blocks)]
        return assemble(parts, self.axis, window)

    def whole(self, window=None):
        parts = [self.blocks[k] for k in sorted(self.blocks)]
        return self.seq.run(lambda *values: assemble(values, self.axis, window), *parts)


class Reduce:
    def __init__(self, seq, product, *operands):
        self.seq, self.product, self.operands = seq, product, operands
        self.sides = side_bits()
        self.count = 1 << len(self.sides)
        self.blocks = {}
        self.arrived = [[] for _ in range(self.count)]
        self.moving = {}

    def make(self, ks):
        for k in ks:
            values = (*self.operands, *self.arrived[k])
            self.blocks[k] = self.seq.run(partial(self.product, k), *values)

    def plain(self, ks):
        return [self.product(k, *self.operands, *self.arrived[k]) for k in ks]

    def take(self, ks, made):
        self.blocks.update(zip(ks, made))

    def send(self, ks):
        for i, k in enumerate(ks):
            if i:
                self.wait([ks[i - 1]])
            s = k.bit_length() - 1
            self.moving[k] = self.seq.start(self.blocks[k], "dp", self.sides[s])

    def wait(self, ks):
        k = ks[-1]
        s = k.bit_length() - 1
        self.arrived[k - (1 << s)].append(self.seq.wait(self.moving[k]))

    def near(self, half):
        whole = list(reversed(range(self.count // 2, self.count)))
        middle = len(whole) // 2
        return whole[middle:] if half else whole[:middle]

    def far(self):
        return list(reversed(range(1, self.count // 2)))

    def make_far(self, near_done=True):
        ks = self.far()
        if ks[-1] in self.blocks or not (near_done or len(ks) == 1):
            return
        for k in ks[:-1]:
            self.make([k])
            self.send([k])
            self.wait([k])
        self.make(ks[-1:])

    def send_far(self):
        self.send(self.far()[-1:])

    def wait_far(self):
        self.wait(self.far()[-1:])

    def finish(self):
        self.make([0])
        return self.blocks[0]


def gather_start(own):
    mid, across = swap(own, "dp", MID), swap(own, "tensor", 1)
    own, mid, across = lax.optimization_barrier((own, mid, across))
    return own, mid, across, swap(own, "tensor", 0), swap(across, "tensor", 0)


def gather_start_with(own, low, core, sent):
    mid, across = swap(own, "dp", MID), swap(own, "tensor", 1)
    low, core, across = lax.optimization_barrier((low, core, across))
    later, x_high = sent(low, core)
    own, mid, across, x_high = lax.optimization_barrier((own, mid, across, x_high))
    core_parts = swap(own, "tensor", 0), swap(across, "tensor", 0)
    return (later, x_high), (own, mid, across, *core_parts)


def gather_finish(own, mid, across, core_own, core_across):
    both, core_mid = swap(mid, "tensor", 1), swap(mid, "tensor", 0)
    core_both = swap(both, "tensor", 0)
    parts = (own, mid, across, both, core_own, core_mid, core_across, core_both)
    return assemble(parts, 0)


class Gather:
    def __init__(self, seq, own, beside=None):
        self.seq = seq
        self.parts = seq.settle(gather_start, own, beside=beside)
        if beside:
            self.parts, self.beside = self.parts

    def finish(self, beside=None):
        return self.seq.settle(gather_finish, *self.parts, beside=beside)


def gather_start_beside(mine, mid):
    own, near, across = mine, swap(mine, "dp", MID), swap(mine, "tensor", 1)
    across, mid = lax.optimization_barrier((across, mid))
    both = swap(mid, "tensor", 1)
    own, near, across, both = lax.optimization_barrier((own, near, across, both))
    return (own, near, across, swap(own, "tensor", 0), swap(across, "tensor", 0)), both


def gather_finish_beside(parts, other):
    own, mid, across, core_own, core_across = parts
    other_own, other_mid, other_across, other_both, other_core_own, other_core_across = other
    both, core_mid = swap(mid, "tensor", 1), swap(mid, "tensor", 0)
    core_mid, other_mid = lax.optimization_barrier((core_mid, other_mid))
    other_core_mid = swap(other_mid, "tensor", 0)
    other_core_mid, other_both = lax.optimization_barrier((other_core_mid, other_both))
    other_core_both = swap(other_both, "tensor", 0)
    both, other_core_both = lax.optimization_barrier((both, other_core_both))
    core_both = swap(both, "tensor", 0)
    mine = (own, mid, across, both, core_own, core_mid, core_across, core_both)
    others = (other_own, other_mid, other_across, other_both)
    others += (other_core_own, other_core_mid, other_core_across, other_core_both)
    return assemble(others, 0), assemble(mine, 0)


class Scatter:
    def __init__(self, seq, product, operands, rows):
        self.seq, self.product, self.operands, self.rows = seq, product, operands, rows

    def begin(self):
        high = self.seq.run(lambda *values: self.product(*values, 1, bf16), *self.operands)
        self.core, self.low_part = self.seq.settle(
            lambda high: swap(high, "tensor", 0),
            high,
            beside=lambda: self.product(*self.operands, 0, f32),
        )

    def plain(self):
        high = self.product(*self.operands, 1, bf16)
        return self.product(*self.operands, 0, f32), swap(high, "tensor", 0)

    def take(self, made):
        self.low_part, self.core = made

    def chunk(self, low, core, k, *others):
        at = slice(k * self.rows, (k + 1) * self.rows)
        part = low[at] + core[at].astype(f32)
        for value in others:
            part = part + value.astype(f32)
        return part

    def sent(self, low, core):
        return tuple(self.chunk(low, core, k).astype(bf16) for k in (2, 3))

    def next(self, low, core, other):
        return self.chunk(low, core, 1, other).astype(bf16)

    def second(self, beside=None):
        def step(low, core):
            later, first = self.sent(low, core)
            return later, swap(first, "tensor", 1)

        moved = self.seq.settle(step, self.low_part, self.core, beside=beside)
        if beside:
            moved, made = moved
        self.later, self.x_high = moved
        return made if beside else None

    def third_step(self, low, core, other, later):
        return swap(self.next(low, core, other), "dp", MID), swap(later, "tensor", 1)

    def third(self, beside=None):
        values = (self.low_part, self.core, self.x_high, self.later)
        moved = self.seq.settle(self.third_step, *values, beside=beside)
        if beside:
            moved, made = moved
        self.mid, self.x_low = moved
        return made if beside else None

    def sent_across(self, low, core):
        later, first = self.sent(low, core)
        return later, swap(first, "tensor", 1)

    def finish(self, step, *others):
        return self.seq.run(step, self.low_part, self.core, self.x_low, self.mid, *others)


def order_kernel(back, order_ref, in_ref, out_ref):
    count = order_ref.shape[0]
    part = in_ref.shape[1] // count
    for i in range(count):
        there = pl.ds(pl.multiple_of(order_ref[i] * part, LANES), part)
        here = slice(i * part, (i + 1) * part)
        if back:
            out_ref[:, there] = in_ref[:, here].astype(out_ref.dtype)
        else:
            out_ref[:, here] = in_ref[:, there].astype(out_ref.dtype)


def reorder(value, order, dtype, back=False):
    rows, width = value.shape
    count = order.shape[0]
    part = width // count
    if part % LANES:
        blocks = value.reshape(rows, count, part)
        index = slice_places() if back else order
        return jnp.take(blocks, index, axis=1).reshape(rows, width).astype(dtype)
    spec = pl.BlockSpec((rows, width), lambda i, order_ref: (0, 0))
    return pl.pallas_call(
        partial(order_kernel, back),
        grid_spec=pltpu.PrefetchScalarGridSpec(
            num_scalar_prefetch=1, grid=(1,), in_specs=[spec], out_specs=spec
        ),
        out_shape=jax.ShapeDtypeStruct((rows, width), dtype),
    )(order, value)


def assemble_kernel(axis, window, *refs):
    parts, out_ref, held, in_sems, out_sems = refs[:-4], refs[-4], refs[-3], refs[-2], refs[-1]
    copies, at = [], 0
    for i, part in enumerate(parts):
        size = window[1] if axis else part.shape[0]
        where = (pl.ds(at, size),) if axis == 0 else (slice(None), pl.ds(at, size))
        copies.append(
            (
                pltpu.make_async_copy(
                    part.at[:, pl.ds(*window)], held.at[where], in_sems.at[i]
                ),
                pltpu.make_async_copy(held.at[where], out_ref.at[where], out_sems.at[i]),
            )
        )
        at += size
    for come, go in copies:
        come.start()
    for come, go in copies:
        come.wait()
        go.start()
    for come, go in copies:
        go.wait()


def assemble(parts, axis, window=None):
    rows, width = parts[0].shape
    window = window or (0, width)
    count = len(parts)
    shape = (rows * count, window[1]) if axis == 0 else (rows, window[1] * count)
    if window[1] % LANES or window[0] % LANES:
        return jnp.concatenate(
            [part[:, window[0] : window[0] + window[1]] for part in parts], axis=axis
        )
    return pl.pallas_call(
        partial(assemble_kernel, axis, window),
        in_specs=[pl.BlockSpec(memory_space=pl.ANY)] * count,
        out_specs=pl.BlockSpec(memory_space=pl.ANY),
        out_shape=jax.ShapeDtypeStruct(shape, parts[0].dtype),
        scratch_shapes=[
            pltpu.VMEM(shape, parts[0].dtype),
            pltpu.SemaphoreType.DMA((count,)),
            pltpu.SemaphoreType.DMA((count,)),
        ],
        compiler_params=pltpu.CompilerParams(vmem_limit_bytes=16 << 20),
        cost_estimate=pl.CostEstimate(flops=0, bytes_accessed=0, transcendentals=0),
    )(*parts)


def norm_kernel(
    low_ref, core_ref, x_ref, mid_ref, old_ref, shift_ref, gain_ref, bias_ref, stream_ref, out_ref
):
    branch = low_ref[...] + core_ref[...].astype(f32) + x_ref[...].astype(f32)
    stream = old_ref[...] + (branch + mid_ref[...].astype(f32)) + shift_ref[...]
    stream_ref[...] = stream
    centre = stream - jnp.mean(stream, axis=1, keepdims=True)
    spread_of = jnp.mean(centre * centre, axis=1, keepdims=True)
    out_ref[...] = (
        centre * lax.rsqrt(spread_of + 1e-05) * gain_ref[...] + bias_ref[...]
    ).astype(bf16)


def norm_back_kernel(
    low_ref, core_ref, x_ref, mid_ref, grad_ref, old_ref, gain_ref, sums_ref, grad_out_ref, out_ref
):
    normed_grad = low_ref[...] + core_ref[...].astype(f32) + x_ref[...].astype(f32)
    normed_grad = normed_grad + mid_ref[...].astype(f32)
    grad, old = grad_ref[...].astype(f32), old_ref[...]
    centre = old - jnp.mean(old, axis=1, keepdims=True)
    root = lax.rsqrt(jnp.mean(centre * centre, axis=1, keepdims=True) + 1e-05)
    hat = centre * root
    scaled = normed_grad * gain_ref[...]
    back = scaled - jnp.mean(scaled, axis=1, keepdims=True)
    back = root * (back - hat * jnp.mean(scaled * hat, axis=1, keepdims=True))
    result = grad + back
    grad_out_ref[...] = result
    out_ref[...] = result.astype(bf16)

    @pl.when(pl.program_id(0) == 0)
    def clear():
        sums_ref[...] = jnp.zeros_like(sums_ref)

    sums_ref[0:1, :] += jnp.sum(normed_grad * hat, axis=0, keepdims=True)
    sums_ref[1:2, :] += jnp.sum(normed_grad, axis=0, keepdims=True)
    sums_ref[2:3, :] += jnp.sum(grad, axis=0, keepdims=True)


def norm_first_kernel(order_ref, in_ref, gain_ref, bias_ref, stream_ref, out_ref):
    order_kernel(False, order_ref, in_ref, stream_ref)
    stream = stream_ref[...]
    centre = stream - jnp.mean(stream, axis=1, keepdims=True)
    spread_of = jnp.mean(centre * centre, axis=1, keepdims=True)
    out_ref[...] = (
        centre * lax.rsqrt(spread_of + 1e-05) * gain_ref[...] + bias_ref[...]
    ).astype(bf16)


def norm_first(value, order, gain, bias):
    rows, width = value.shape
    if width // order.shape[0] % LANES:
        stream = reorder(value, order, f32)
        centre = stream - jnp.mean(stream, axis=1, keepdims=True)
        spread_of = jnp.mean(centre * centre, axis=1, keepdims=True)
        return stream, (centre * lax.rsqrt(spread_of + 1e-05) * gain + bias).astype(bf16)
    steps = row_steps(rows)
    row_spec = pl.BlockSpec((rows // steps, width), lambda i, order_ref: (i, 0))
    line_spec = pl.BlockSpec((1, width), lambda i, order_ref: (0, 0))
    return call(
        norm_first_kernel,
        (order, value, gain.reshape(1, width), bias.reshape(1, width)),
        (steps,),
        [row_spec, line_spec, line_spec],
        [row_spec, row_spec],
        [jax.ShapeDtypeStruct((rows, width), dtype) for dtype in (f32, bf16)],
        scalars=1,
    )


def row_steps(rows):
    return rows // 48 if rows % 48 == 0 else 1


def norm_call(kernel, rows, width, row_values, line_values, out_shapes):
    steps = row_steps(rows)
    row_spec = pl.BlockSpec((rows // steps, width), lambda i: (i, 0))
    line_spec = pl.BlockSpec((1, width), lambda i: (0, 0))
    sum_spec = pl.BlockSpec((8, width), lambda i: (0, 0))
    return pl.pallas_call(
        kernel,
        grid=(steps,),
        in_specs=[row_spec] * len(row_values) + [line_spec] * len(line_values),
        out_specs=[row_spec if shape.shape[0] == rows else sum_spec for shape in out_shapes],
        out_shape=out_shapes,
        compiler_params=pltpu.CompilerParams(vmem_limit_bytes=40 << 20),
        cost_estimate=pl.CostEstimate(flops=0, bytes_accessed=0, transcendentals=0),
    )(*row_values, *[value.reshape(1, width) for value in line_values])


def norm_after(low, core, x_low, mid, old, shift, gain, bias):
    rows, width = old.shape
    out = [jax.ShapeDtypeStruct((rows, width), dtype) for dtype in (f32, bf16)]
    return norm_call(
        norm_kernel, rows, width, (low, core, x_low, mid, old), (shift, gain, bias), out
    )


def norm_before(low, core, x_low, mid, grad, old, gain):
    rows, width = old.shape
    out = [jax.ShapeDtypeStruct((8, width), f32)]
    out += [jax.ShapeDtypeStruct((rows, width), dtype) for dtype in (f32, bf16)]
    return norm_call(norm_back_kernel, rows, width, (low, core, x_low, mid, grad, old), (gain,), out)


def layout(lens, total, block):
    steps_index = jnp.arange(total, dtype=jnp.int32)
    blocks_first = (lens[0] + block - 1) // block
    second_start = blocks_first * block
    in_first = steps_index < lens[0]
    in_second = (steps_index >= second_start) & (steps_index < second_start + lens[1])
    return jnp.where(in_first, steps_index, jnp.where(in_second, steps_index - second_start, 0))


def rotary_tables(position):
    half_rot = ROT // 2
    lane = jnp.arange(LANES, dtype=jnp.int32) % HEAD_DIM
    freqs = 10000.0 ** (-((lane % half_rot).astype(f32) * 2.0) / ROT)
    angles = position.astype(f32)[..., None] * freqs
    cosine, sine = jnp.cos(angles), jnp.sin(angles)
    return (
        jnp.where(lane < ROT, cosine, 1.0),
        jnp.where(lane < half_rot, -sine, 0.0),
        jnp.where((lane >= half_rot) & (lane < ROT), sine, 0.0),
    )


def turn(field, cos, above, below, back=False):
    up = pltpu.roll(field, LANES - ROT // 2, 1) * above
    down = pltpu.roll(field, ROT // 2, 1) * below
    return field * cos - (up + down) if back else field * cos + (up + down)


def allowed_bias(scalars, group, first_row, rows, cols):
    first_len, second_len = scalars[2 * group], scalars[2 * group + 1]
    second_start = ((first_len + BLOCK - 1) // BLOCK) * BLOCK
    row = first_row + lax.broadcasted_iota(jnp.int32, (rows, 1), 0)
    in_second = (row >= second_start) & (row < second_start + second_len)
    start = jnp.where(row < first_len, 0, jnp.where(in_second, second_start, row))
    col = lax.broadcasted_iota(jnp.int32, (rows, cols), 1)
    return jnp.where((col >= start) & (col <= row), 0.0, neg_large)


def chunk_places(scalars, rows):
    me = scalars[4]
    return [pl.multiple_of((me ^ ((r % 2) * 2 + r // 2)) * rows, 64) for r in range(4)]


def head_mask(head):
    lane = lax.broadcasted_iota(jnp.int32, (1, LANES), 1)
    return jnp.where(lane // HEAD_DIM == head, 1.0, 0.0).astype(bf16)


def nt(left, right):
    return lax.dot_general(left, right, (((1,), (1,)), ((), ())), preferred_element_type=f32)


def nn(left, right):
    return jnp.dot(left, right, preferred_element_type=f32)


def tn(left, right):
    return lax.dot_general(left, right, (((0,), (0,)), ((), ())), preferred_element_type=f32)


def attention_kernel(
    scalars, mixed_ref, cos_ref, above_ref, below_ref, out_ref, kept_ref, sums_ref, held
):
    group = pl.program_id(0)
    rows = mixed_ref.shape[2]
    width = mixed_ref.shape[3] // 3
    total = 4 * rows
    places = chunk_places(scalars, rows)
    for r in range(4):
        at = pl.ds(places[r], rows)
        cos, above, below = cos_ref[0, at, :], above_ref[0, at, :], below_ref[0, at, :]
        for part in range(0, 2 * width, LANES):
            turned = turn(mixed_ref[r, 0, :, part : part + LANES], cos, above, below)
            if part < width:
                turned = turned.astype(bf16) * HEAD_DIM**-0.5
            kept_ref[0, at, part : part + LANES] = turned.astype(bf16)
        kept_ref[0, at, 2 * width :] = mixed_ref[r, 0, :, 2 * width :].astype(bf16)
    for first in range(0, total, TILE):
        cols = first + TILE
        bias = allowed_bias(scalars, group, first, TILE, cols)
        for pair in range(0, width, LANES):
            query = kept_ref[0, first:cols, pair : pair + LANES]
            key = kept_ref[0, :cols, width + pair : width + pair + LANES]
            value = kept_ref[0, :cols, 2 * width + pair : 2 * width + pair + LANES]
            result = None
            for head in range(LANES // HEAD_DIM):
                mask = head_mask(head)
                scores = nt(query * mask, key) + bias
                top = jnp.max(scores, axis=1, keepdims=True)
                expo = jnp.exp(scores - top)
                mass = jnp.sum(expo, axis=1, keepdims=True)
                probs16 = (expo * (1.0 / mass)).astype(bf16)
                mine = nn(probs16, value * mask)
                result = mine if result is None else result + mine
                at_head = pair // HEAD_DIM + head
                sums_ref[0, first:cols, at_head : at_head + 1] = top + jnp.log(mass)
            held[first:cols, pair : pair + LANES] = result.astype(bf16)
    for r in range(4):
        out_ref[r, 0] = held[pl.ds(places[r], rows), :]


def attention_back_kernel(
    scalars,
    kept_ref,
    sums_ref,
    grad_ref,
    cos_ref,
    above_ref,
    below_ref,
    out_ref,
    held,
    query_grad,
    key_grad,
    value_grad,
):
    group = pl.program_id(0)
    rows = grad_ref.shape[2]
    width = grad_ref.shape[3]
    total = 4 * rows
    places = chunk_places(scalars, rows)
    for r in range(4):
        held[pl.ds(places[r], rows), :] = grad_ref[r, 0]
    for first in reversed(range(0, total, TILE)):
        cols = first + TILE
        bias = allowed_bias(scalars, group, first, TILE, cols)
        for pair in range(0, width, LANES):
            lanes = slice(pair, pair + LANES)
            query = kept_ref[0, first:cols, pair : pair + LANES]
            key = kept_ref[0, :cols, width + pair : width + pair + LANES]
            value = kept_ref[0, :cols, 2 * width + pair : 2 * width + pair + LANES]
            grad = held[first:cols, lanes]
            grads = [None, None, None]
            for head in range(LANES // HEAD_DIM):
                mask = head_mask(head)
                at_head = pair // HEAD_DIM + head
                query_head, grad_head = query * mask, grad * mask
                scores = nt(query_head, key) + bias
                probs = jnp.exp(scores - sums_ref[0, first:cols, at_head : at_head + 1])
                prob_grad = nt(grad_head, value)
                mean = jnp.sum(probs * prob_grad, axis=1, keepdims=True)
                score_grad = (probs * (prob_grad - mean)).astype(bf16)
                mine = (
                    nn(score_grad, key * mask),
                    tn(score_grad, query_head),
                    tn(probs.astype(bf16), grad_head),
                )
                grads = [m if g is None else g + m for g, m in zip(grads, mine)]
            query_grad[first:cols, lanes] = grads[0]
            if cols == total:
                key_grad[:, lanes] = grads[1]
                value_grad[:, lanes] = grads[2]
            else:
                key_grad[:cols, lanes] += grads[1]
                value_grad[:cols, lanes] += grads[2]
    for r in range(4):
        at = pl.ds(places[r], rows)
        cos, above, below = cos_ref[0, at, :], above_ref[0, at, :], below_ref[0, at, :]
        for pair in range(0, width, LANES):
            query = turn(query_grad[at, pair : pair + LANES] * HEAD_DIM**-0.5, cos, above, below, True)
            key = turn(key_grad[at, pair : pair + LANES], cos, above, below, True)
            out_ref[r, 0, :, pair : pair + LANES] = query.astype(bf16)
            out_ref[r, 0, :, width + pair : width + pair + LANES] = key.astype(bf16)
        out_ref[r, 0, :, 2 * width :] = value_grad[at, :].astype(bf16)


def chunk_spec(rows, width):
    return pl.BlockSpec((4, 1, rows, width), lambda g, scalars: (0, g, 0, 0))


def group_spec(total, width):
    return pl.BlockSpec((1, total, width), lambda g, scalars: (g, 0, 0))


def attention_forward(mixed, tables, scalars, rows):
    width = mixed.shape[1] // 3
    total = 4 * rows
    attended, kept, sums = pl.pallas_call(
        attention_kernel,
        grid_spec=pltpu.PrefetchScalarGridSpec(
            num_scalar_prefetch=1,
            grid=(2,),
            in_specs=[chunk_spec(rows, 3 * width)] + [group_spec(total, LANES)] * 3,
            out_specs=[
                chunk_spec(rows, width),
                group_spec(total, 3 * width),
                group_spec(total, LANES),
            ],
            scratch_shapes=[pltpu.VMEM((total, width), bf16)],
        ),
        out_shape=[
            jax.ShapeDtypeStruct((4, 2, rows, width), bf16),
            jax.ShapeDtypeStruct((2, total, 3 * width), bf16),
            jax.ShapeDtypeStruct((2, total, LANES), f32),
        ],
        compiler_params=pltpu.CompilerParams(vmem_limit_bytes=40 << 20),
        cost_estimate=pl.CostEstimate(flops=0, bytes_accessed=0, transcendentals=0),
    )(scalars, mixed.reshape(4, 2, rows, 3 * width), *tables)
    return attended.reshape(8 * rows, width), kept, sums


def attention_backward(kept, sums, grad16, tables, scalars, rows):
    width = grad16.shape[1]
    total = 4 * rows
    mixed_grad = pl.pallas_call(
        attention_back_kernel,
        grid_spec=pltpu.PrefetchScalarGridSpec(
            num_scalar_prefetch=1,
            grid=(2,),
            in_specs=[
                group_spec(total, 3 * width),
                group_spec(total, LANES),
                chunk_spec(rows, width),
            ]
            + [group_spec(total, LANES)] * 3,
            out_specs=chunk_spec(rows, 3 * width),
            scratch_shapes=[pltpu.VMEM((total, width), bf16)]
            + [pltpu.VMEM((total, width), f32)] * 3,
        ),
        out_shape=jax.ShapeDtypeStruct((4, 2, rows, 3 * width), bf16),
        compiler_params=pltpu.CompilerParams(vmem_limit_bytes=40 << 20),
        cost_estimate=pl.CostEstimate(flops=0, bytes_accessed=0, transcendentals=0),
    )(scalars, kept, sums, grad16.reshape(4, 2, rows, width), *tables)
    return mixed_grad.reshape(8 * rows, 3 * width)


def call(kernel, args, grid, in_specs, out_specs, out_shape, scratch_shapes=(), scalars=0):
    return pl.pallas_call(
        kernel,
        grid_spec=pltpu.PrefetchScalarGridSpec(
            num_scalar_prefetch=scalars,
            grid=grid,
            in_specs=in_specs,
            out_specs=out_specs,
            scratch_shapes=scratch_shapes,
        ),
        out_shape=out_shape,
        compiler_params=pltpu.CompilerParams(vmem_limit_bytes=48 << 20),
        cost_estimate=pl.CostEstimate(flops=0, bytes_accessed=0, transcendentals=0),
    )(*args)


def mix_kernel(left_ref, right_ref, shift_ref, out_ref):
    out_ref[...] = nn(left_ref[...], right_ref[...]) + shift_ref[...]


def mix_product(normed, mixed_full, shift):
    rows, width = normed.shape
    cols = shift.shape[1]
    block = rows // 3
    return call(
        mix_kernel,
        (normed, mixed_full, shift.reshape(1, cols)),
        (3,),
        [
            pl.BlockSpec((block, width), lambda i: (i, 0)),
            pl.BlockSpec((width, cols), lambda i: (0, 0)),
            pl.BlockSpec((1, cols), lambda i: (0, 0)),
        ],
        pl.BlockSpec((block, cols), lambda i: (i, 0)),
        jax.ShapeDtypeStruct((rows, cols), f32),
    )


def hide_kernel(left_ref, right_ref, shift_ref, out_ref, slope_ref):
    value = nn(left_ref[...], right_ref[...]) + shift_ref[...]
    inner = math.sqrt(2.0 / math.pi)
    square = value * value
    bend = jnp.tanh(inner * value * (1.0 + 0.044715 * square))
    half = 0.5 * (1.0 + bend)
    out_ref[...] = (value * half).astype(bf16)
    slope = 0.5 * value * (1.0 - bend * bend) * (inner * (1.0 + 3.0 * 0.044715 * square))
    slope_ref[...] = (half + slope).astype(slope_ref.dtype)


def hide_product(normed, up_full, shift):
    rows, width = normed.shape
    cols = up_full.shape[1]
    block = rows // 6
    out = pl.BlockSpec((block, cols), lambda i: (i, 0))
    return call(
        hide_kernel,
        (normed, up_full, shift.reshape(1, cols)),
        (6,),
        [
            pl.BlockSpec((block, width), lambda i: (i, 0)),
            pl.BlockSpec((width, cols), lambda i: (0, 0)),
            pl.BlockSpec((1, cols), lambda i: (0, 0)),
        ],
        [out, out],
        [jax.ShapeDtypeStruct((rows, cols), dtype) for dtype in (bf16, f32)],
    )


def out_kernel(first_ref, second_ref, dense_ref, down_ref, out_ref):
    value = nt(first_ref[...], dense_ref[...]) + nn(second_ref[...], down_ref[...])
    out_ref[...] = value.astype(out_ref.dtype)


def out_product(attended, hidden, mixed_full, down_full, half, dtype):
    rows, width = attended.shape[0] // 2, down_full.shape[1]
    heads = attended.shape[1]
    return call(
        out_kernel,
        (attended, hidden, mixed_full, down_full),
        (width // 512,),
        [
            pl.BlockSpec((rows, heads), lambda j: (half, 0)),
            pl.BlockSpec((rows, hidden.shape[1]), lambda j: (half, 0)),
            pl.BlockSpec((512, heads), lambda j: (j, 3)),
            pl.BlockSpec((hidden.shape[1], 512), lambda j: (0, j)),
        ],
        pl.BlockSpec((rows, 512), lambda j: (0, j)),
        jax.ShapeDtypeStruct((rows, width), dtype),
    )


def nn_kernel(left_ref, right_ref, out_ref):
    out_ref[...] = nn(left_ref[...], right_ref[...]).astype(out_ref.dtype)


def nt_scaled_kernel(left_ref, right_ref, slope_ref, out_ref):
    value = nt(left_ref[...], right_ref[...]) * slope_ref[...].astype(f32)
    out_ref[...] = value.astype(out_ref.dtype)


def attended_back(grad16, mixed_full, heads):
    rows, width = grad16.shape
    block = rows // 3
    return call(
        nn_kernel,
        (grad16, mixed_full),
        (3,),
        [
            pl.BlockSpec((block, width), lambda i: (i, 0)),
            pl.BlockSpec((width, heads), lambda i: (0, 3)),
        ],
        pl.BlockSpec((block, heads), lambda i: (i, 0)),
        jax.ShapeDtypeStruct((rows, heads), bf16),
    )


def hidden_back(grad16, down_full, slope):
    rows, width = grad16.shape
    cols = slope.shape[1]
    block = rows // 2
    spec = pl.BlockSpec((block, 256), lambda i, j: (i, j))
    return call(
        nt_scaled_kernel,
        (grad16, down_full, slope),
        (2, cols // 256),
        [
            pl.BlockSpec((block, width), lambda i, j: (i, 0)),
            pl.BlockSpec((256, width), lambda i, j: (j, 0)),
            spec,
        ],
        spec,
        jax.ShapeDtypeStruct((rows, cols), bf16),
    )


def both_kernel(first_ref, second_ref, proj_ref, up_ref, out_ref):
    value = nt(first_ref[...], proj_ref[...]) + nt(second_ref[...], up_ref[...])
    out_ref[...] = value.astype(out_ref.dtype)


def normed_back(mixed_grad, pre_grad, mixed_full, up_full, half, dtype):
    rows, width = mixed_grad.shape[0] // 2, up_full.shape[0]
    return call(
        both_kernel,
        (mixed_grad, pre_grad, mixed_full, up_full),
        (width // 512,),
        [
            pl.BlockSpec((rows, mixed_grad.shape[1]), lambda j: (half, 0)),
            pl.BlockSpec((rows, pre_grad.shape[1]), lambda j: (half, 0)),
            pl.BlockSpec((512, mixed_grad.shape[1]), lambda j: (j, 0)),
            pl.BlockSpec((512, up_full.shape[1]), lambda j: (j, 0)),
        ],
        pl.BlockSpec((rows, 512), lambda j: (0, j)),
        jax.ShapeDtypeStruct((rows, width), dtype),
    )


def in_grad_kernel(left_ref, right_ref, *refs):
    value = tn(left_ref[...], right_ref[...])
    for ref in refs[:-1]:
        value = value + ref[...].astype(f32)
    refs[-1][...] = value.astype(bf16)


def in_grad(part, k, normed, grad, *others):
    rows, cols = grad.shape
    block = min(part, 256)
    steps = part // block
    spec = pl.BlockSpec((block, cols), lambda i: (i, 0))
    return call(
        in_grad_kernel,
        (normed, grad, *others),
        (steps,),
        [
            pl.BlockSpec((rows, block), lambda i: (0, k * steps + i)),
            pl.BlockSpec((rows, cols), lambda i: (0, 0)),
        ]
        + [spec] * len(others),
        spec,
        jax.ShapeDtypeStruct((part, cols), bf16),
    )


def down_grad(part, k, hidden, grad, *others):
    rows, height = hidden.shape
    block = min(part, 256)
    steps = part // block
    spec = pl.BlockSpec((height, block), lambda j: (0, j))
    return call(
        in_grad_kernel,
        (hidden, grad, *others),
        (steps,),
        [
            pl.BlockSpec((rows, height), lambda j: (0, 0)),
            pl.BlockSpec((rows, block), lambda j: (0, k * steps + j)),
        ]
        + [spec] * len(others),
        spec,
        jax.ShapeDtypeStruct((height, part), bf16),
    )


def mixed_grad_kernel(normed_ref, mixed_ref, grad_ref, attended_ref, *refs):
    split = mixed_ref.shape[1]
    values = (tn(normed_ref[...], mixed_ref[...]), tn(grad_ref[...], attended_ref[...]))
    for value, cols in zip(values, (slice(0, split), slice(split, None))):
        for ref in refs[:-1]:
            value = value + ref[:, cols].astype(f32)
        refs[-1][:, cols] = value.astype(bf16)


def mixed_weight_grad(part, k, normed, mixed_grad, grad, attended, *others):
    rows, heads = attended.shape
    width = mixed_grad.shape[1] + heads
    block = min(part, 256)
    steps = part // block
    spec = pl.BlockSpec((block, width), lambda i: (i, 0))
    slice_spec = pl.BlockSpec((rows, block), lambda i: (0, k * steps + i))
    return call(
        mixed_grad_kernel,
        (normed, mixed_grad, grad, attended, *others),
        (steps,),
        [
            slice_spec,
            pl.BlockSpec(mixed_grad.shape, lambda i: (0, 0)),
            slice_spec,
            pl.BlockSpec(attended.shape, lambda i: (0, 0)),
        ]
        + [spec] * len(others),
        spec,
        jax.ShapeDtypeStruct((part, width), bf16),
    )


def halves_kernel(axis, mid_ref, keep_ref, other_ref, *refs):
    out_ref, size = refs[-1], keep_ref.shape[axis]
    for part_ref, half in ((keep_ref, mid_ref[0]), (other_ref, 1 - mid_ref[0])):
        at = pl.ds(pl.multiple_of(half * size, LANES), size)
        if axis:
            out_ref[0, :, at] = part_ref[...].astype(f32)
        else:
            out_ref[0, at, :] = part_ref[...].astype(f32)


def place_halves(keep, other, mid, axis, layer, layers, before=None):
    rows, cols = keep.shape
    shape = (rows, 2 * cols) if axis else (2 * rows, cols)
    if cols % LANES or (axis == 0 and rows % LANES):
        line = jnp.concatenate([pick(keep, other, mid), pick(other, keep, mid)], axis=axis)
        line = line.astype(f32)[None]
        if before is None:
            return jnp.concatenate([jnp.zeros_like(line)] * layer + [line], axis=0)
        return jnp.concatenate([line, before[1:]], axis=0)
    spec = pl.BlockSpec((rows, cols), lambda i, mid_ref: (0, 0))
    given = [] if before is None else [before]
    return pl.pallas_call(
        partial(halves_kernel, axis),
        grid_spec=pltpu.PrefetchScalarGridSpec(
            num_scalar_prefetch=1,
            grid=(1,),
            in_specs=[spec, spec] + [pl.BlockSpec(memory_space=pl.ANY)] * len(given),
            out_specs=pl.BlockSpec((1, *shape), lambda i, mid_ref: (layer, 0, 0)),
        ),
        out_shape=jax.ShapeDtypeStruct((layers, *shape), f32),
        input_output_aliases={3: 0} if given else {},
        compiler_params=pltpu.CompilerParams(vmem_limit_bytes=32 << 20),
        cost_estimate=pl.CostEstimate(flops=0, bytes_accessed=0, transcendentals=0),
    )(mid.reshape(1), keep, other, *given)


def last_kernel(
    order_ref, low_ref, core_ref, x_ref, mid_ref, old_ref, shift_ref, out_ref, held
):
    branch = low_ref[...] + core_ref[...].astype(f32) + x_ref[...].astype(f32)
    held[...] = old_ref[...] + (branch + mid_ref[...].astype(f32)) + shift_ref[...]
    order_kernel(True, order_ref, held, out_ref)


def last_stream(order, low, core, x_low, mid, old, shift):
    rows, width = old.shape
    if width // order.shape[0] % LANES:
        branch = low[:rows] + core[:rows].astype(f32) + x_low.astype(f32) + mid.astype(f32)
        return reorder(old + branch + shift, order, f32, True)
    steps = row_steps(rows)
    row_spec = pl.BlockSpec((rows // steps, width), lambda i, order_ref: (i, 0))
    return call(
        last_kernel,
        (order, low, core, x_low, mid, old, shift),
        (steps,),
        [row_spec] * 5 + [pl.BlockSpec((1, width), lambda i, order_ref: (0, 0))],
        row_spec,
        jax.ShapeDtypeStruct((rows, width), f32),
        [pltpu.VMEM((rows // steps, width), f32)],
        scalars=1,
    )


def halves(value, half, axis):
    size = value.shape[axis] // 2
    return lax.dynamic_slice_in_dim(value, half * size, size, axis)


class Small:
    def __init__(self, seq, mine, tensor, mid):
        self.seq, self.tensor = seq, tensor
        self.mine = seq.settle(
            lambda mine: pair_up(mine, swap(mine, "dp", MID), mid, 0), mine[None]
        )

    def second(self):
        def step(mine):
            for bit in side_bits():
                mine = jnp.concatenate([mine, swap(mine, "dp", bit)], axis=0)
            return mine[None]

        self.mine = self.seq.settle(step, self.mine)

    def finish(self, unpack):
        def step(mine):
            for bit in (0, 1):
                mine = pair_up(mine, swap(mine, "tensor", bit), (self.tensor >> bit) & 1, 0)
            return unpack(jnp.swapaxes(mine, 0, 1))

        return self.seq.settle(step, self.mine)


class SmallSums:
    def __init__(self, seq, norm_grads, in_bgrads, mid):
        self.seq, self.mid = seq, mid
        self.norm_grads, self.in_bgrads = norm_grads, in_bgrads
        self.layers, self.kinds = len(norm_grads), 3
        self.sides = side_bits()

    def halve(self, sums, biases, axis, half, move):
        keep, sent = halves(sums, half, axis), halves(sums, 1 - half, axis)
        split = biases.shape[0]
        received = move(jnp.concatenate([biases, sent.reshape(-1)]))
        return keep + received[split:].reshape(keep.shape), received[:split]

    def side(self, s, sums, biases):
        sums, other = self.halve(
            sums, biases, 1, 0, lambda value: swap(value, "dp", self.sides[s])
        )
        return sums, biases + other

    def first(self):
        tensor = lax.axis_index("tensor")

        def step(*values):
            sums = jnp.stack([value[: self.kinds] for value in values[: self.layers]])
            biases = jnp.concatenate(values[self.layers :])
            shape = (self.layers * self.kinds, 1 << len(self.sides), 2, lax.axis_size("tensor"), -1)
            sums, biases = self.side(len(self.sides) - 1, sums.reshape(shape), biases)
            none = biases[:0]
            for bit in (1, 0):
                sums, _ = self.halve(
                    sums, none, 3, (tensor >> bit) & 1, lambda value: swap(value, "tensor", bit)
                )
            sums, other = self.halve(
                sums, biases, 2, self.mid, lambda value: swap(value, "dp", MID)
            )
            pair = (pick(biases, other, self.mid), pick(other, biases, self.mid))
            return sums, jnp.concatenate(pair)

        values = [value for pair in self.in_bgrads for value in pair]
        self.sums, self.biases = self.seq.settle(step, *self.norm_grads, *values)

    def finish(self):
        def step(sums, biases):
            for s in reversed(range(len(self.sides) - 1)):
                sums, biases = self.side(s, sums, biases)
            return sums, biases

        sums, biases = self.seq.settle(step, self.sums, self.biases)
        return sums.reshape(self.layers, self.kinds, -1), biases.reshape(2, -1)


def shards(
    tokens_in,
    lengths,
    norm_gain,
    norm_bias,
    proj_weight,
    proj_bias,
    dense_weight,
    dense_bias,
    up_weight,
    up_bias,
    down_weight,
    down_bias,
    cotangent,
):
    rows, width = tokens_in.shape
    layer_count = proj_weight.shape[0]
    n_dp = lax.axis_size("dp")
    dp = lax.axis_index("dp")
    tensor = lax.axis_index("tensor")
    mid = (dp >> MID) & 1
    order = slice_order()
    seq = Sequence(lengths[0, 0].astype(f32), lengths[0, 0] > 0)

    def take_mixed(l, half, weight=proj_weight):
        proj = halves(weight[l], half, 2).reshape(weight.shape[1], -1)
        return jnp.concatenate([proj, halves(dense_weight[l], half, 0).T], axis=1)

    def take_up(l, half, weight=up_weight):
        return halves(weight[l], half, 1)

    def take_down(l, half, weight=down_weight):
        return halves(weight[l], half, 0)

    takes = ((take_mixed, 0), (take_up, 0), (take_down, 1))

    def set_out(l, i):
        weight = (proj_weight, up_weight, down_weight)[i]
        part = seq.run(lambda value: takes[i][0](l, 1 - mid, value), weight, apart=True)
        return seq.start(part, "dp", MID)

    def paired(l, i, moving):
        return joined(l, i, seq.wait(moving))

    def joined(l, i, received):
        take, axis = takes[i]
        block = seq.run(
            lambda other: pair_up(take(l, mid), other, mid, axis), received, apart=True
        )
        return Spread(seq, block, axis)

    moving = [set_out(0, 0), set_out(0, 1)]
    whole_lens = lengths.reshape(-1).astype(f32)
    coarse = jnp.floor(whole_lens / 8.0)
    small = Small(
        seq,
        jnp.concatenate(
            [
                value.reshape(-1)
                for value in (norm_gain, norm_bias, dense_bias, down_bias, proj_bias, up_bias)
            ]
            + [coarse.astype(bf16), (whole_lens - 8.0 * coarse).astype(bf16)]
        ),
        tensor,
        mid,
    )
    small.second()
    m0 = paired(0, 0, moving[0])
    u0 = paired(0, 1, moving[1])
    m0.near()
    m0.far()
    cot = seq.run(lambda value: reorder(value, order, bf16), cotangent)
    each, proj_each, up_each = norm_gain.shape[1], proj_bias.shape[3], up_bias.shape[2]

    def unpack(everyone):
        pair_lens = lax.dynamic_index_in_dim(everyone[:2, :, -4:], tensor, 1, keepdims=False)
        pair_lens = pair_lens.astype(f32)
        pair_lens = (pair_lens[:, :2] * 8.0 + pair_lens[:, 2:]).astype(jnp.int32)
        lens = pick(pair_lens, pair_lens[::-1], mid)
        everyone = everyone[:, :, :-4]
        at = 4 * layer_count * each
        norm_parts = everyone[:, :, :at].reshape(n_dp, -1, 4 * layer_count, each)
        norm_parts = jnp.transpose(norm_parts, (2, 0, 1, 3)).reshape(4, layer_count, width)
        norm_parts = norm_parts.astype(f32)
        same_heads = lax.dynamic_index_in_dim(everyone[:, :, at:], tensor, 1, keepdims=False)
        same_heads = halves(same_heads[slice_places()], mid, 0).astype(f32)
        proj_at = layer_count * 3 * proj_each
        proj_shift = jnp.transpose(
            same_heads[:, :proj_at].reshape(-1, layer_count * 3, proj_each), (1, 0, 2)
        ).reshape(layer_count, -1)
        up_shift = jnp.transpose(
            same_heads[:, proj_at:].reshape(-1, layer_count, up_each), (1, 0, 2)
        ).reshape(layer_count, -1)
        gains, biases = norm_parts[0], norm_parts[1]
        shifts = norm_parts[2] + norm_parts[3]
        scalars = jnp.concatenate([lens.reshape(-1), tensor[None].astype(jnp.int32)])
        lines = [value[l] for value in (gains, biases, shifts) for l in range(layer_count)]
        lines += [value[l] for value in (proj_shift, up_shift) for l in range(layer_count)]
        return [line[None] for line in lines], lens, scalars.astype(jnp.int32)

    lines, lens, scalars = small.finish(unpack)
    gains, biases, out_shifts, proj_shift, up_shift = (
        lines[i * layer_count : (i + 1) * layer_count] for i in range(5)
    )

    def mix(l, normed, proj_full):
        return seq.run(mix_product, normed, proj_full, proj_shift[l])

    def attend(mixed):
        return seq.run(lambda value: attention_forward(value, tables, scalars, rows), mixed)

    def hide(l, normed, up_full):
        return seq.run(hide_product, normed, up_full, up_shift[l])

    def make_tables():
        return rotary_tables(jax.vmap(partial(layout, total=4 * rows, block=BLOCK))(lens))

    stream, own = seq.run(
        lambda value: norm_first(value, order, gains[0], biases[0]), tokens_in
    )
    def with_cot(own, cot):
        mid, across = swap(own, "dp", MID), swap(own, "tensor", 1)
        across, moved = lax.optimization_barrier((across, cot))
        cot_across = swap(moved, "tensor", 1)
        mid, cot_across, own = lax.optimization_barrier((mid, cot_across, own))
        return (own, mid, across, swap(own, "tensor", 0), swap(across, "tensor", 0)), cot_across

    (token_parts, cot_across), tables = seq.settle(with_cot, own, cot, beside=make_tables)
    m0.near_wait()
    m0.far_wait()
    u0.far()
    m0.last()
    u0.near()
    sent = seq.run(lambda value: take_down(0, 1 - mid, value), down_weight, apart=True)

    def with_others(own, mid, across, core_own, core_across, sent, cot):
        received, both = swap(sent, "dp", MID), swap(mid, "tensor", 1)
        received, cot, mid = lax.optimization_barrier((received, cot, mid))
        cot_mid, core_mid = swap(cot, "dp", MID), swap(mid, "tensor", 0)
        both, core_mid = lax.optimization_barrier((both, core_mid))
        core_both = swap(both, "tensor", 0)
        parts = (own, mid, across, both, core_own, core_mid, core_across, core_both)
        return assemble(parts, 0), received, cot_mid

    normed, received, cot_mid = seq.settle(with_others, *token_parts, sent, cot)
    d0 = joined(0, 2, received)
    u0.far_wait()
    seq.tick(3)
    u0.near_wait()
    m0.last_wait()
    u0.last()
    d0.far()
    mixed_full = m0.whole()
    mixed = mix(0, normed, mixed_full)
    d0.near()
    moving = [set_out(1, 0), set_out(1, 1)]
    attended, kept, sums = attend(mixed)
    u0.last_wait()
    up_full = u0.whole()
    hidden, slope = hide(0, normed, up_full)
    m1 = paired(1, 0, moving[0])
    u1 = paired(1, 1, moving[1])
    d0.far_wait()
    seq.tick(3)
    d0.near_wait()
    d0.last()
    m1.far()
    moving = [set_out(1, 2)]
    d0.last_wait()
    down_full = d0.whole()
    m1.near()
    saved = [(normed, kept, sums, slope, attended, hidden)]
    weights = [(mixed_full, up_full, down_full)]
    streams = [stream]

    branch = Scatter(seq, out_product, (attended, hidden, mixed_full, down_full), rows)
    branch.begin()
    m1.far_wait()
    m1.near_wait()
    u1.far()
    m1.last()
    branch.second()
    d1 = paired(1, 2, moving[0])
    m1.last_wait()
    u1.near()
    branch.third()
    u1.far_wait()
    seq.tick(4)
    u1.near_wait()
    d1.far()
    u1.last()
    stream, own = branch.finish(
        norm_after, stream, out_shifts[0], gains[1], biases[1]
    )
    streams.append(stream)

    def with_cores(mine, mid, cot, across):
        parts, both = gather_start_beside(mine, mid)
        *parts, cot, across = lax.optimization_barrier((*parts, cot, across))
        return parts, both, swap(cot, "tensor", 0), swap(across, "tensor", 0)

    parts, cot_both, cot_core_own, cot_core_across = seq.settle(
        with_cores, own, cot_mid, cot, cot_across
    )
    u1.last_wait()
    d1.near()
    (grad16, normed), mixed_full = seq.settle(
        lambda *values: gather_finish_beside(values[:5], values[5:]),
        *parts,
        cot,
        cot_mid,
        cot_across,
        cot_both,
        cot_core_own,
        cot_core_across,
        beside=lambda: m1.plain(),
    )
    d1.far_wait()
    seq.tick(3)
    d1.near_wait()
    d1.last()
    mixed = mix(1, normed, mixed_full)
    attended, kept, sums = attend(mixed)
    up_full = u1.whole()
    hidden, slope = hide(1, normed, up_full)
    d1.last_wait()
    down_full = d1.whole()
    saved.append((normed, kept, sums, slope, attended, hidden))
    weights.append((mixed_full, up_full, down_full))

    heads_width = attended.shape[1]
    parts = 1 << len(side_bits())
    norm_grads, in_bgrads = [None] * layer_count, [None] * layer_count

    part = width // parts

    def down_grads(l, grad16):
        return Reduce(seq, partial(down_grad, part), saved[l][5], grad16)

    def up_grads(l, grad):
        return Reduce(seq, partial(in_grad, part), saved[l][0], grad)

    def mixed_grads(l, grad, grad16):
        values = saved[l][0], grad, grad16, saved[l][4]
        return Reduce(seq, partial(mixed_weight_grad, part), *values)

    def attend_back(l, grad16):
        kept, sums = saved[l][1:3]
        mixed_full = weights[l][0]

        def step(value):
            grad = attended_back(value, mixed_full, heads_width)
            return attention_backward(kept, sums, grad, tables, scalars, rows)

        return seq.run(step, grad16)

    def hide_back(l, grad16):
        slope, down_full = saved[l][3], weights[l][2]
        return seq.run(lambda value: hidden_back(value, down_full, slope), grad16)

    def rows_back(l, mixed_grad, pre_grad):
        return Scatter(seq, normed_back, (mixed_grad, pre_grad, *weights[l][:2]), rows)

    def bias_back(mixed_grad, pre_grad):
        return jnp.sum(mixed_grad, axis=0, dtype=f32), jnp.sum(pre_grad, axis=0, dtype=f32)

    def own_start(total, axis):
        return halves(total, mid, axis), seq.start(halves(total, 1 - mid, axis), "dp", MID)

    def own_wait(pair):
        keep, moving = pair
        received = seq.wait(moving)
        return pick(keep, received, mid).astype(f32), pick(received, keep, mid).astype(f32)

    first, second = 0, 1
    early = len(side_bits()) == 2

    def send(reduce, which):
        reduce.send(reduce.near(which))

    def arrive(reduce, which):
        reduce.wait(reduce.near(which))

    def rest(reduce):
        for which in (first, second):
            reduce.make(reduce.near(which))
            send(reduce, which)
            arrive(reduce, which)
        reduce.make_far()
        reduce.send_far()
        reduce.wait_far()
        reduce.finish()

    down2 = down_grads(1, grad16)
    down2.make(down2.near(first))
    if early:
        send(down2, first)
    mixed_grad = attend_back(1, grad16)
    if early:
        down2.make(down2.near(second))
        send(down2, second)
    pre_grad = hide_back(1, grad16)
    up2, mix2 = up_grads(1, pre_grad), mixed_grads(1, mixed_grad, grad16)
    back = rows_back(1, mixed_grad, pre_grad)
    back.begin()
    branch = Scatter(seq, out_product, (attended, hidden, *weights[1][::2]), rows)
    if early:
        arrive(down2, first)
        up2.make(up2.near(first))
        send(up2, first)
    made = back.second(
        lambda: (
            down2.plain(down2.far()) if early else (),
            up2.plain(up2.near(second)),
            mix2.plain(mix2.near(first)),
            mix2.plain(mix2.near(second)),
            bias_back(mixed_grad, pre_grad),
        )
    )
    in_bgrads[1] = made[4]
    if early:
        down2.take(down2.far(), made[0])
        up2.take(up2.near(second), made[1])
        mix2.take(mix2.near(first), made[2])
        mix2.take(mix2.near(second), made[3])
        arrive(down2, second)
        seq.tick(4)
        arrive(up2, first)
        send(up2, second)
    made = back.third(lambda: (up2.plain(up2.far()) if early else (), branch.plain()))
    branch.take(made[1])
    norm_grads[1], grad_stream, own = back.finish(
        norm_before, cot, streams[1], gains[1]
    )
    if early:
        up2.take(up2.far(), made[0])
        arrive(up2, second)
        send(mix2, first)
        down2.send_far()
    (branch.later, branch.x_high), coming = seq.settle(
        lambda own, low, core: gather_start_with(own, low, core, branch.sent_across),
        own,
        branch.low_part,
        branch.core,
    )
    if early:
        arrive(mix2, first)
        send(mix2, second)
        up2.send_far()
        grad16, made = seq.settle(gather_finish, *coming, beside=lambda: mix2.plain(mix2.far()))
        mix2.take(mix2.far(), made)
        mix2.send_far()
        down2.wait_far()
    else:
        grad16 = seq.settle(gather_finish, *coming)
        rest(down2)
        rest(up2)
        rest(mix2)

    results = {}

    def own_start(total, axis):
        keep, sent = seq.run(
            lambda value: (halves(value, mid, axis), halves(value, 1 - mid, axis)),
            total,
            apart=True,
        )
        return keep, seq.start(sent, "dp", MID)

    def own_finish(l, name, axis, pair):
        keep, moving = pair
        received = seq.wait(moving)
        before = results.get(name)
        given = () if before is None else (before,)
        results[name] = seq.run(
            lambda keep, other, *given: place_halves(
                keep, other, mid, axis, l, layer_count, *given
            ),
            keep,
            received,
            *given,
        )

    def mixed_finish(pair):
        keep, moving = pair
        received = seq.wait(moving)
        cols = 3 * heads_width

        def step(keep, other):
            pair = [pick(keep, other, mid).astype(f32), pick(other, keep, mid).astype(f32)]
            proj = [value[:, :cols].reshape(value.shape[0], 3, -1) for value in pair]
            dense = [value[:, cols:].T for value in pair]
            return jnp.concatenate(proj, axis=2), jnp.concatenate(dense, axis=0)

        return seq.run(step, keep, received, apart=True)

    down1 = down_grads(0, grad16)
    down1.make(down1.near(first))
    if early:
        send(down1, first)
        down2.make([0])
    down2_pair = own_start(down2.blocks[0], 1)
    mixed_grad = attend_back(0, grad16)
    down1.make(down1.near(second))
    if early:
        up2.wait_far()
        arrive(mix2, second)
        send(down1, second)
    pre_grad = hide_back(0, grad16)
    up1, mix1 = up_grads(0, pre_grad), mixed_grads(0, mixed_grad, grad16)
    up1.make(up1.near(first))
    if early:
        send(up1, first)
        up2.make([0])
    own_finish(1, "down", 0, down2_pair)
    up1.make(up1.near(second))
    mix1.make(mix1.near(first))
    if early:
        mix2.wait_far()
        seq.tick(5)
        arrive(down1, first)
        down1.make_far()
        arrive(down1, second)
        down1.send_far()
        send(up1, second)
    up2_pair = own_start(up2.blocks[0], 0)
    back = rows_back(0, mixed_grad, pre_grad)
    back.begin()
    if early:
        arrive(up1, first)
        up1.make_far()
        up1.send_far()
        send(mix1, first)
        mix2.make([0])
    own_finish(1, "up", 1, up2_pair)
    mix2_pair = own_start(mix2.blocks[0], 0)
    made = back.second(
        lambda: (
            mix1.plain(mix1.near(second)),
            bias_back(mixed_grad, pre_grad),
        )
    )
    mix1.take(mix1.near(second), made[0])
    in_bgrads[0] = made[1]
    if early:
        down1.wait_far()
        seq.tick(1)
        arrive(up1, second)
        seq.tick(1)
        arrive(mix1, first)
        mix1.make_far()
        mix1.send_far()
        send(mix1, second)
    made = back.third(lambda: down1.plain([0]) if early else ())
    norm_grads[0], grad_stream, own = back.finish(
        norm_before, grad_stream, streams[0], gains[0]
    )
    if early:
        down1.take([0], made)
    else:
        rest(down1)
        rest(up1)
        rest(mix1)
    down1_pair = own_start(down1.blocks[0], 1)
    small_sums = SmallSums(seq, norm_grads, in_bgrads, mid)
    small_sums.first()
    if early:
        up1.wait_far()
        up1.make([0])
    up1_pair = own_start(up1.blocks[0], 0)
    mix2_own = mixed_finish(mix2_pair)
    input_grad = branch.third(lambda: reorder(grad_stream, order, f32, True))
    activations = branch.finish(partial(last_stream, order), streams[1], out_shifts[1])
    if early:
        mix1.wait_far()
        seq.tick(4)
        arrive(mix1, second)
        mix1.make([0])
    mix1_pair = own_start(mix1.blocks[0], 0)
    own_finish(0, "down", 0, down1_pair)
    own_finish(0, "up", 1, up1_pair)
    norm_owned, bias_both = small_sums.finish()
    mix1_own = mixed_finish(mix1_pair)
    bias_both = bias_both + 0.0 * seq.scalar
    per_layer = bias_both.shape[1] // layer_count
    bias_both = bias_both.reshape(2, layer_count, per_layer)
    proj_b = jnp.transpose(
        bias_both[:, :, : 3 * heads_width].reshape(2, layer_count, 3, heads_width), (1, 2, 0, 3)
    ).reshape(layer_count, 3, 1, 2 * heads_width)
    up_b = jnp.transpose(bias_both[:, :, 3 * heads_width :], (1, 0, 2)).reshape(layer_count, 1, -1)
    return (
        activations,
        input_grad,
        norm_owned[:, 0],
        norm_owned[:, 1],
        jnp.stack([mix1_own[0], mix2_own[0]]),
        lax.dynamic_slice_in_dim(proj_b, dp * proj_each, proj_each, 3),
        jnp.stack([mix1_own[1], mix2_own[1]]),
        norm_owned[:, 2],
        results["up"],
        lax.dynamic_slice_in_dim(up_b, dp * up_each, up_each, 2),
        results["down"],
        norm_owned[:, 2],
    )


def solution(mesh):
    in_specs = (
        P(("dp", "tensor"), None),
        P("dp", None),
        P(None, ("dp", "tensor")),
        P(None, ("dp", "tensor")),
        P(None, "dp", None, "tensor"),
        P(None, None, "tensor", "dp"),
        P(None, "tensor", "dp"),
        P(None, ("dp", "tensor")),
        P(None, "dp", "tensor"),
        P(None, "tensor", "dp"),
        P(None, "tensor", "dp"),
        P(None, ("dp", "tensor")),
        P(("dp", "tensor"), None),
    )
    out_specs = (
        P(("dp", "tensor"), None),
        P(("dp", "tensor"), None),
        P(None, ("dp", "tensor")),
        P(None, ("dp", "tensor")),
        P(None, "dp", None, "tensor"),
        P(None, None, "tensor", "dp"),
        P(None, "tensor", "dp"),
        P(None, ("dp", "tensor")),
        P(None, "dp", "tensor"),
        P(None, "tensor", "dp"),
        P(None, "tensor", "dp"),
        P(None, ("dp", "tensor")),
    )
    return jax.shard_map(shards, mesh=mesh, in_specs=in_specs, out_specs=out_specs, check_vma=False)
```

```python
from functools import partial
import math

import jax
import jax.numpy as jnp
from jax import lax
from jax.experimental import pallas as pl
from jax.experimental.pallas import tpu as pltpu
from jax.sharding import PartitionSpec as P

HEAD_DIM = 64
ROT = 32
BLOCK = 128
LANES = 128
TILE = 256
MID = 1

TICK = 1_200_000_000

neg_large = -1e30
f32 = jnp.float32
bf16 = jnp.bfloat16


def swap(value, axis, bit):
    size = lax.axis_size(axis)
    return lax.ppermute(value, axis, [(i, i ^ (1 << bit)) for i in range(size)])


def tick_kernel(in_ref, out_ref):
    out_ref[0, 0] = in_ref[0, 0]


def tick(scalar, count):
    spec = pl.BlockSpec(memory_space=pltpu.SMEM)
    result = pl.pallas_call(
        tick_kernel,
        in_specs=[spec],
        out_specs=spec,
        out_shape=jax.ShapeDtypeStruct((1, 1), f32),
        cost_estimate=pl.CostEstimate(flops=count * TICK, bytes_accessed=0, transcendentals=0),
    )(scalar.reshape(1, 1))
    return result[0, 0]


class Sequence:
    def __init__(self, scalar, always):
        self.scalar = scalar
        self.always = always

    def gate(self, *values):
        *values, self.scalar = lax.optimization_barrier((*values, self.scalar))
        return values

    def run(self, step, *values, apart=False):
        values = self.gate(*values)
        if apart:
            shapes = jax.eval_shape(step, *values)

            def never(*others):
                return jax.tree.map(lambda shape: jnp.zeros(shape.shape, shape.dtype), shapes)

            result = lax.cond(self.always, step, never, *values)
        else:
            result = step(*values)
        leaves, tree = jax.tree.flatten(result)
        return jax.tree.unflatten(tree, self.gate(*leaves))

    def start(self, value, axis, bit):
        (value,) = self.gate(value)
        return swap(value, axis, bit)

    def wait(self, value):
        (value,) = self.gate(value)
        return value

    def settle(self, step, *values, beside=None):
        def both(*moved):
            return (step(*moved), beside()) if beside else step(*moved)

        return self.run(both, *values, apart=True)

    def tick(self, count):
        self.scalar = tick(self.scalar, count)

    def swap(self, value, axis, bit):
        return self.settle(lambda moved: swap(moved, axis, bit), value)


def side_bits():
    count = (lax.axis_size("dp") - 1).bit_length()
    return [bit for bit in range(count - 1, MID, -1)] + [0]


def slice_order():
    sides = side_bits()
    me = lax.axis_index("dp")
    base = me - (((me >> MID) & 1) << MID)
    order = []
    for k in range(1 << len(sides)):
        mask = sum(((k >> s) & 1) << bit for s, bit in enumerate(sides))
        for mid in range(2):
            order.append((base ^ mask) | (mid << MID))
    return jnp.stack(order).astype(jnp.int32)


def slice_places():
    sides = side_bits()
    every = jnp.arange(lax.axis_size("dp"), dtype=jnp.int32)
    apart = every ^ lax.axis_index("dp")
    place = (every >> MID) & 1
    for s, bit in enumerate(sides):
        place = place + (((apart >> bit) & 1) << (s + 1))
    return place


def pick(pair_first, pair_second, bit):
    return jnp.where(bit == 0, pair_first, pair_second)


def pair_up(keep, received, bit, axis):
    return jnp.concatenate(
        [pick(keep, received, bit), pick(received, keep, bit)], axis=axis
    )


class Spread:
    def __init__(self, seq, block, axis):
        self.seq, self.axis = seq, axis
        self.sides = side_bits()
        self.far_count = 1 << (len(self.sides) - 1)
        self.blocks = {0: block}

    def move(self, ks):
        for k in ks:
            if k != ks[0]:
                self.arrived(ks)
            s = k.bit_length() - 1
            self.blocks[k] = self.seq.start(self.blocks[k - (1 << s)], "dp", self.sides[s])

    def arrived(self, ks):
        last = max(k for k in ks if k in self.blocks)
        self.blocks[last] = self.seq.wait(self.blocks[last])

    def far(self):
        self.move(range(1, self.far_count))

    def far_wait(self):
        self.arrived(range(1, self.far_count))

    def near(self):
        self.move([self.far_count])

    def near_wait(self):
        self.arrived([self.far_count])

    def last(self):
        self.move(range(self.far_count + 1, 2 * self.far_count))

    def last_wait(self):
        self.arrived(range(self.far_count + 1, 2 * self.far_count))

    def plain(self, window=None):
        parts = [self.blocks[k] for k in sorted(self.blocks)]
        return assemble(parts, self.axis, window)

    def whole(self, window=None):
        parts = [self.blocks[k] for k in sorted(self.blocks)]
        return self.seq.run(lambda *values: assemble(values, self.axis, window), *parts)


class Reduce:
    def __init__(self, seq, product, *operands):
        self.seq, self.product, self.operands = seq, product, operands
        self.sides = side_bits()
        self.count = 1 << len(self.sides)
        self.blocks = {}
        self.arrived = [[] for _ in range(self.count)]
        self.moving = {}

    def make(self, ks):
        for k in ks:
            values = (*self.operands, *self.arrived[k])
            self.blocks[k] = self.seq.run(partial(self.product, k), *values)

    def plain(self, ks):
        return [self.product(k, *self.operands, *self.arrived[k]) for k in ks]

    def take(self, ks, made):
        self.blocks.update(zip(ks, made))

    def send(self, ks):
        for i, k in enumerate(ks):
            if i:
                self.wait([ks[i - 1]])
            s = k.bit_length() - 1
            self.moving[k] = self.seq.start(self.blocks[k], "dp", self.sides[s])

    def wait(self, ks):
        k = ks[-1]
        s = k.bit_length() - 1
        self.arrived[k - (1 << s)].append(self.seq.wait(self.moving[k]))

    def near(self, half):
        whole = list(reversed(range(self.count // 2, self.count)))
        middle = len(whole) // 2
        return whole[middle:] if half else whole[:middle]

    def far(self):
        return list(reversed(range(1, self.count // 2)))

    def make_far(self, near_done=True):
        ks = self.far()
        if ks[-1] in self.blocks or not (near_done or len(ks) == 1):
            return
        for k in ks[:-1]:
            self.make([k])
            self.send([k])
            self.wait([k])
        self.make(ks[-1:])

    def send_far(self):
        self.send(self.far()[-1:])

    def wait_far(self):
        self.wait(self.far()[-1:])

    def finish(self):
        self.make([0])
        return self.blocks[0]


def gather_start(own):
    mid, across = swap(own, "dp", MID), swap(own, "tensor", 1)
    own, mid, across = lax.optimization_barrier((own, mid, across))
    return own, mid, across, swap(own, "tensor", 0), swap(across, "tensor", 0)


def gather_start_with(own, low, core, sent):
    mid, across = swap(own, "dp", MID), swap(own, "tensor", 1)
    low, core, across = lax.optimization_barrier((low, core, across))
    later, x_high = sent(low, core)
    own, mid, across, x_high = lax.optimization_barrier((own, mid, across, x_high))
    core_parts = swap(own, "tensor", 0), swap(across, "tensor", 0)
    return (later, x_high), (own, mid, across, *core_parts)


def gather_finish(own, mid, across, core_own, core_across):
    both, core_mid = swap(mid, "tensor", 1), swap(mid, "tensor", 0)
    core_both = swap(both, "tensor", 0)
    parts = (own, mid, across, both, core_own, core_mid, core_across, core_both)
    return assemble(parts, 0)


class Gather:
    def __init__(self, seq, own, beside=None):
        self.seq = seq
        self.parts = seq.settle(gather_start, own, beside=beside)
        if beside:
            self.parts, self.beside = self.parts

    def finish(self, beside=None):
        return self.seq.settle(gather_finish, *self.parts, beside=beside)


def gather_start_beside(mine, mid):
    own, near, across = mine, swap(mine, "dp", MID), swap(mine, "tensor", 1)
    across, mid = lax.optimization_barrier((across, mid))
    both = swap(mid, "tensor", 1)
    own, near, across, both = lax.optimization_barrier((own, near, across, both))
    return (own, near, across, swap(own, "tensor", 0), swap(across, "tensor", 0)), both


def gather_finish_beside(parts, other, beside):
    own, mid, across, core_own, core_across = parts
    other_own, other_mid, other_across, other_both, other_core_own, other_core_across = other
    both, core_mid = swap(mid, "tensor", 1), swap(mid, "tensor", 0)
    core_mid, other_mid = lax.optimization_barrier((core_mid, other_mid))
    other_core_mid = swap(other_mid, "tensor", 0)
    other_core_mid, other_both = lax.optimization_barrier((other_core_mid, other_both))
    other_core_both = swap(other_both, "tensor", 0)
    others = (other_own, other_mid, other_across, other_both)
    others += (other_core_own, other_core_mid, other_core_across, other_core_both)
    whole, made = assemble(others, 0), beside()
    both, whole, made = lax.optimization_barrier((both, whole, made))
    core_both = swap(both, "tensor", 0)
    mine = (own, mid, across, both, core_own, core_mid, core_across, core_both)
    return whole, assemble(mine, 0), made


class Scatter:
    def __init__(self, seq, product, operands, rows):
        self.seq, self.product, self.operands, self.rows = seq, product, operands, rows

    def begin(self, beside=tuple):
        high = self.seq.run(lambda *values: self.product(*values, 1, bf16), *self.operands)
        self.core, (self.low_part, made) = self.seq.settle(
            lambda high: swap(high, "tensor", 0),
            high,
            beside=lambda: (self.product(*self.operands, 0, f32), beside()),
        )
        return made

    def plain(self):
        high = self.product(*self.operands, 1, bf16)
        return self.product(*self.operands, 0, f32), swap(high, "tensor", 0)

    def take(self, made):
        self.low_part, self.core = made

    def chunk(self, low, core, k, *others):
        at = slice(k * self.rows, (k + 1) * self.rows)
        part = low[at] + core[at].astype(f32)
        for value in others:
            part = part + value.astype(f32)
        return part

    def sent(self, low, core):
        return tuple(self.chunk(low, core, k).astype(bf16) for k in (2, 3))

    def next(self, low, core, other):
        return self.chunk(low, core, 1, other).astype(bf16)

    def second(self, beside=None):
        def step(low, core):
            later, first = self.sent(low, core)
            return later, swap(first, "tensor", 1)

        moved = self.seq.settle(step, self.low_part, self.core, beside=beside)
        if beside:
            moved, made = moved
        self.later, self.x_high = moved
        return made if beside else None

    def third_step(self, low, core, other, later):
        return swap(self.next(low, core, other), "dp", MID), swap(later, "tensor", 1)

    def third(self, beside=None):
        values = (self.low_part, self.core, self.x_high, self.later)
        moved = self.seq.settle(self.third_step, *values, beside=beside)
        if beside:
            moved, made = moved
        self.mid, self.x_low = moved
        return made if beside else None

    def sent_across(self, low, core):
        later, first = self.sent(low, core)
        return later, swap(first, "tensor", 1)

    def finish(self, step, *others):
        return self.seq.run(step, self.low_part, self.core, self.x_low, self.mid, *others)


def order_kernel(back, order_ref, in_ref, out_ref):
    count = order_ref.shape[0]
    part = in_ref.shape[1] // count
    for i in range(count):
        there = pl.ds(pl.multiple_of(order_ref[i] * part, LANES), part)
        here = slice(i * part, (i + 1) * part)
        if back:
            out_ref[:, there] = in_ref[:, here].astype(out_ref.dtype)
        else:
            out_ref[:, here] = in_ref[:, there].astype(out_ref.dtype)


def reorder(value, order, dtype, back=False):
    rows, width = value.shape
    count = order.shape[0]
    part = width // count
    if part % LANES:
        blocks = value.reshape(rows, count, part)
        index = slice_places() if back else order
        return jnp.take(blocks, index, axis=1).reshape(rows, width).astype(dtype)
    spec = pl.BlockSpec((rows, width), lambda i, order_ref: (0, 0))
    return pl.pallas_call(
        partial(order_kernel, back),
        grid_spec=pltpu.PrefetchScalarGridSpec(
            num_scalar_prefetch=1, grid=(1,), in_specs=[spec], out_specs=spec
        ),
        out_shape=jax.ShapeDtypeStruct((rows, width), dtype),
    )(order, value)


def assemble_kernel(axis, window, *refs):
    parts, out_ref, held, in_sems, out_sems = refs[:-4], refs[-4], refs[-3], refs[-2], refs[-1]
    copies, at = [], 0
    for i, part in enumerate(parts):
        size = window[1] if axis else part.shape[0]
        where = (pl.ds(at, size),) if axis == 0 else (slice(None), pl.ds(at, size))
        copies.append(
            (
                pltpu.make_async_copy(
                    part.at[:, pl.ds(*window)], held.at[where], in_sems.at[i]
                ),
                pltpu.make_async_copy(held.at[where], out_ref.at[where], out_sems.at[i]),
            )
        )
        at += size
    for come, go in copies:
        come.start()
    for come, go in copies:
        come.wait()
        go.start()
    for come, go in copies:
        go.wait()


def assemble(parts, axis, window=None):
    rows, width = parts[0].shape
    window = window or (0, width)
    count = len(parts)
    shape = (rows * count, window[1]) if axis == 0 else (rows, window[1] * count)
    if window[1] % LANES or window[0] % LANES:
        return jnp.concatenate(
            [part[:, window[0] : window[0] + window[1]] for part in parts], axis=axis
        )
    return pl.pallas_call(
        partial(assemble_kernel, axis, window),
        in_specs=[pl.BlockSpec(memory_space=pl.ANY)] * count,
        out_specs=pl.BlockSpec(memory_space=pl.ANY),
        out_shape=jax.ShapeDtypeStruct(shape, parts[0].dtype),
        scratch_shapes=[
            pltpu.VMEM(shape, parts[0].dtype),
            pltpu.SemaphoreType.DMA((count,)),
            pltpu.SemaphoreType.DMA((count,)),
        ],
        compiler_params=pltpu.CompilerParams(vmem_limit_bytes=16 << 20),
        cost_estimate=pl.CostEstimate(flops=0, bytes_accessed=0, transcendentals=0),
    )(*parts)


def norm_kernel(
    low_ref, core_ref, x_ref, mid_ref, old_ref, shift_ref, gain_ref, bias_ref, stream_ref, out_ref
):
    branch = low_ref[...] + core_ref[...].astype(f32) + x_ref[...].astype(f32)
    stream = old_ref[...] + (branch + mid_ref[...].astype(f32)) + shift_ref[...]
    stream_ref[...] = stream
    centre = stream - jnp.mean(stream, axis=1, keepdims=True)
    spread_of = jnp.mean(centre * centre, axis=1, keepdims=True)
    out_ref[...] = (
        centre * lax.rsqrt(spread_of + 1e-05) * gain_ref[...] + bias_ref[...]
    ).astype(bf16)


def norm_back_kernel(
    low_ref, core_ref, x_ref, mid_ref, grad_ref, old_ref, gain_ref, sums_ref, grad_out_ref, out_ref
):
    normed_grad = low_ref[...] + core_ref[...].astype(f32) + x_ref[...].astype(f32)
    normed_grad = normed_grad + mid_ref[...].astype(f32)
    grad, old = grad_ref[...].astype(f32), old_ref[...]
    centre = old - jnp.mean(old, axis=1, keepdims=True)
    root = lax.rsqrt(jnp.mean(centre * centre, axis=1, keepdims=True) + 1e-05)
    hat = centre * root
    scaled = normed_grad * gain_ref[...]
    back = scaled - jnp.mean(scaled, axis=1, keepdims=True)
    back = root * (back - hat * jnp.mean(scaled * hat, axis=1, keepdims=True))
    result = grad + back
    grad_out_ref[...] = result
    out_ref[...] = result.astype(bf16)

    @pl.when(pl.program_id(0) == 0)
    def clear():
        sums_ref[...] = jnp.zeros_like(sums_ref)

    sums_ref[0:1, :] += jnp.sum(normed_grad * hat, axis=0, keepdims=True)
    sums_ref[1:2, :] += jnp.sum(normed_grad, axis=0, keepdims=True)
    sums_ref[2:3, :] += jnp.sum(grad, axis=0, keepdims=True)


def norm_first_kernel(order_ref, in_ref, gain_ref, bias_ref, stream_ref, out_ref):
    order_kernel(False, order_ref, in_ref, stream_ref)
    stream = stream_ref[...]
    centre = stream - jnp.mean(stream, axis=1, keepdims=True)
    spread_of = jnp.mean(centre * centre, axis=1, keepdims=True)
    out_ref[...] = (
        centre * lax.rsqrt(spread_of + 1e-05) * gain_ref[...] + bias_ref[...]
    ).astype(bf16)


def norm_first(value, order, gain, bias):
    rows, width = value.shape
    if width // order.shape[0] % LANES:
        stream = reorder(value, order, f32)
        centre = stream - jnp.mean(stream, axis=1, keepdims=True)
        spread_of = jnp.mean(centre * centre, axis=1, keepdims=True)
        return stream, (centre * lax.rsqrt(spread_of + 1e-05) * gain + bias).astype(bf16)
    steps = row_steps(rows)
    row_spec = pl.BlockSpec((rows // steps, width), lambda i, order_ref: (i, 0))
    line_spec = pl.BlockSpec((1, width), lambda i, order_ref: (0, 0))
    return call(
        norm_first_kernel,
        (order, value, gain.reshape(1, width), bias.reshape(1, width)),
        (steps,),
        [row_spec, line_spec, line_spec],
        [row_spec, row_spec],
        [jax.ShapeDtypeStruct((rows, width), dtype) for dtype in (f32, bf16)],
        scalars=1,
    )


def row_steps(rows):
    return rows // 48 if rows % 48 == 0 else 1


def norm_call(kernel, rows, width, row_values, line_values, out_shapes):
    steps = row_steps(rows)
    row_spec = pl.BlockSpec((rows // steps, width), lambda i: (i, 0))
    line_spec = pl.BlockSpec((1, width), lambda i: (0, 0))
    sum_spec = pl.BlockSpec((8, width), lambda i: (0, 0))
    return pl.pallas_call(
        kernel,
        grid=(steps,),
        in_specs=[row_spec] * len(row_values) + [line_spec] * len(line_values),
        out_specs=[row_spec if shape.shape[0] == rows else sum_spec for shape in out_shapes],
        out_shape=out_shapes,
        compiler_params=pltpu.CompilerParams(vmem_limit_bytes=40 << 20),
        cost_estimate=pl.CostEstimate(flops=0, bytes_accessed=0, transcendentals=0),
    )(*row_values, *[value.reshape(1, width) for value in line_values])


def norm_after(low, core, x_low, mid, old, shift, gain, bias):
    rows, width = old.shape
    out = [jax.ShapeDtypeStruct((rows, width), dtype) for dtype in (f32, bf16)]
    return norm_call(
        norm_kernel, rows, width, (low, core, x_low, mid, old), (shift, gain, bias), out
    )


def norm_before(low, core, x_low, mid, grad, old, gain):
    rows, width = old.shape
    out = [jax.ShapeDtypeStruct((8, width), f32)]
    out += [jax.ShapeDtypeStruct((rows, width), dtype) for dtype in (f32, bf16)]
    return norm_call(norm_back_kernel, rows, width, (low, core, x_low, mid, grad, old), (gain,), out)


def layout(lens, total, block):
    steps_index = jnp.arange(total, dtype=jnp.int32)
    blocks_first = (lens[0] + block - 1) // block
    second_start = blocks_first * block
    in_first = steps_index < lens[0]
    in_second = (steps_index >= second_start) & (steps_index < second_start + lens[1])
    return jnp.where(in_first, steps_index, jnp.where(in_second, steps_index - second_start, 0))


def rotary_tables(position):
    half_rot = ROT // 2
    lane = jnp.arange(LANES, dtype=jnp.int32) % HEAD_DIM
    freqs = 10000.0 ** (-((lane % half_rot).astype(f32) * 2.0) / ROT)
    angles = position.astype(f32)[..., None] * freqs
    cosine, sine = jnp.cos(angles), jnp.sin(angles)
    return (
        jnp.where(lane < ROT, cosine, 1.0),
        jnp.where(lane < half_rot, -sine, 0.0),
        jnp.where((lane >= half_rot) & (lane < ROT), sine, 0.0),
    )


def turn(field, cos, above, below, back=False):
    up = pltpu.roll(field, LANES - ROT // 2, 1) * above
    down = pltpu.roll(field, ROT // 2, 1) * below
    return field * cos - (up + down) if back else field * cos + (up + down)


def allowed_bias(scalars, group, first_row, rows, cols):
    first_len, second_len = scalars[2 * group], scalars[2 * group + 1]
    second_start = ((first_len + BLOCK - 1) // BLOCK) * BLOCK
    row = first_row + lax.broadcasted_iota(jnp.int32, (rows, 1), 0)
    in_second = (row >= second_start) & (row < second_start + second_len)
    start = jnp.where(row < first_len, 0, jnp.where(in_second, second_start, row))
    col = lax.broadcasted_iota(jnp.int32, (rows, cols), 1)
    return jnp.where((col >= start) & (col <= row), 0.0, neg_large)


def chunk_places(scalars, rows):
    me = scalars[4]
    return [pl.multiple_of((me ^ ((r % 2) * 2 + r // 2)) * rows, 64) for r in range(4)]


def head_mask(head):
    lane = lax.broadcasted_iota(jnp.int32, (1, LANES), 1)
    return jnp.where(lane // HEAD_DIM == head, 1.0, 0.0).astype(bf16)


def nt(left, right):
    return lax.dot_general(left, right, (((1,), (1,)), ((), ())), preferred_element_type=f32)


def nn(left, right):
    return jnp.dot(left, right, preferred_element_type=f32)


def tn(left, right):
    return lax.dot_general(left, right, (((0,), (0,)), ((), ())), preferred_element_type=f32)


def attention_kernel(
    scalars, mixed_ref, cos_ref, above_ref, below_ref, out_ref, kept_ref, sums_ref, held
):
    group = pl.program_id(0)
    rows = mixed_ref.shape[2]
    width = mixed_ref.shape[3] // 3
    total = 4 * rows
    places = chunk_places(scalars, rows)
    for r in range(4):
        at = pl.ds(places[r], rows)
        cos, above, below = cos_ref[0, at, :], above_ref[0, at, :], below_ref[0, at, :]
        for part in range(0, 2 * width, LANES):
            turned = turn(mixed_ref[r, 0, :, part : part + LANES], cos, above, below)
            if part < width:
                turned = turned.astype(bf16) * HEAD_DIM**-0.5
            kept_ref[0, at, part : part + LANES] = turned.astype(bf16)
        kept_ref[0, at, 2 * width :] = mixed_ref[r, 0, :, 2 * width :].astype(bf16)
    for first in range(0, total, TILE):
        cols = first + TILE
        bias = allowed_bias(scalars, group, first, TILE, cols)
        for pair in range(0, width, LANES):
            query = kept_ref[0, first:cols, pair : pair + LANES]
            key = kept_ref[0, :cols, width + pair : width + pair + LANES]
            value = kept_ref[0, :cols, 2 * width + pair : 2 * width + pair + LANES]
            result = None
            for head in range(LANES // HEAD_DIM):
                mask = head_mask(head)
                scores = nt(query * mask, key) + bias
                top = jnp.max(scores, axis=1, keepdims=True)
                expo = jnp.exp(scores - top)
                mass = jnp.sum(expo, axis=1, keepdims=True)
                probs16 = (expo * (1.0 / mass)).astype(bf16)
                mine = nn(probs16, value * mask)
                result = mine if result is None else result + mine
                at_head = pair // HEAD_DIM + head
                sums_ref[0, first:cols, at_head : at_head + 1] = top + jnp.log(mass)
            held[first:cols, pair : pair + LANES] = result.astype(bf16)
    for r in range(4):
        out_ref[r, 0] = held[pl.ds(places[r], rows), :]


def attention_back_kernel(
    scalars,
    kept_ref,
    sums_ref,
    grad_ref,
    cos_ref,
    above_ref,
    below_ref,
    out_ref,
    held,
    query_grad,
    key_grad,
    value_grad,
):
    group = pl.program_id(0)
    rows = grad_ref.shape[2]
    width = grad_ref.shape[3]
    total = 4 * rows
    places = chunk_places(scalars, rows)
    for r in range(4):
        held[pl.ds(places[r], rows), :] = grad_ref[r, 0]
    for first in reversed(range(0, total, TILE)):
        cols = first + TILE
        bias = allowed_bias(scalars, group, first, TILE, cols)
        for pair in range(0, width, LANES):
            lanes = slice(pair, pair + LANES)
            query = kept_ref[0, first:cols, pair : pair + LANES]
            key = kept_ref[0, :cols, width + pair : width + pair + LANES]
            value = kept_ref[0, :cols, 2 * width + pair : 2 * width + pair + LANES]
            grad = held[first:cols, lanes]
            grads = [None, None, None]
            for head in range(LANES // HEAD_DIM):
                mask = head_mask(head)
                at_head = pair // HEAD_DIM + head
                query_head, grad_head = query * mask, grad * mask
                scores = nt(query_head, key) + bias
                probs = jnp.exp(scores - sums_ref[0, first:cols, at_head : at_head + 1])
                prob_grad = nt(grad_head, value)
                mean = jnp.sum(probs * prob_grad, axis=1, keepdims=True)
                score_grad = (probs * (prob_grad - mean)).astype(bf16)
                mine = (
                    nn(score_grad, key * mask),
                    tn(score_grad, query_head),
                    tn(probs.astype(bf16), grad_head),
                )
                grads = [m if g is None else g + m for g, m in zip(grads, mine)]
            query_grad[first:cols, lanes] = grads[0]
            if cols == total:
                key_grad[:, lanes] = grads[1]
                value_grad[:, lanes] = grads[2]
            else:
                key_grad[:cols, lanes] += grads[1]
                value_grad[:cols, lanes] += grads[2]
    for r in range(4):
        at = pl.ds(places[r], rows)
        cos, above, below = cos_ref[0, at, :], above_ref[0, at, :], below_ref[0, at, :]
        for pair in range(0, width, LANES):
            query = turn(query_grad[at, pair : pair + LANES] * HEAD_DIM**-0.5, cos, above, below, True)
            key = turn(key_grad[at, pair : pair + LANES], cos, above, below, True)
            out_ref[r, 0, :, pair : pair + LANES] = query.astype(bf16)
            out_ref[r, 0, :, width + pair : width + pair + LANES] = key.astype(bf16)
        out_ref[r, 0, :, 2 * width :] = value_grad[at, :].astype(bf16)


def chunk_spec(rows, width):
    return pl.BlockSpec((4, 1, rows, width), lambda g, scalars: (0, g, 0, 0))


def group_spec(total, width):
    return pl.BlockSpec((1, total, width), lambda g, scalars: (g, 0, 0))


def attention_forward(mixed, tables, scalars, rows):
    width = mixed.shape[1] // 3
    total = 4 * rows
    attended, kept, sums = pl.pallas_call(
        attention_kernel,
        grid_spec=pltpu.PrefetchScalarGridSpec(
            num_scalar_prefetch=1,
            grid=(2,),
            in_specs=[chunk_spec(rows, 3 * width)] + [group_spec(total, LANES)] * 3,
            out_specs=[
                chunk_spec(rows, width),
                group_spec(total, 3 * width),
                group_spec(total, LANES),
            ],
            scratch_shapes=[pltpu.VMEM((total, width), bf16)],
        ),
        out_shape=[
            jax.ShapeDtypeStruct((4, 2, rows, width), bf16),
            jax.ShapeDtypeStruct((2, total, 3 * width), bf16),
            jax.ShapeDtypeStruct((2, total, LANES), f32),
        ],
        compiler_params=pltpu.CompilerParams(vmem_limit_bytes=40 << 20),
        cost_estimate=pl.CostEstimate(flops=0, bytes_accessed=0, transcendentals=0),
    )(scalars, mixed.reshape(4, 2, rows, 3 * width), *tables)
    return attended.reshape(8 * rows, width), kept, sums


def attention_backward(kept, sums, grad16, tables, scalars, rows):
    width = grad16.shape[1]
    total = 4 * rows
    mixed_grad = pl.pallas_call(
        attention_back_kernel,
        grid_spec=pltpu.PrefetchScalarGridSpec(
            num_scalar_prefetch=1,
            grid=(2,),
            in_specs=[
                group_spec(total, 3 * width),
                group_spec(total, LANES),
                chunk_spec(rows, width),
            ]
            + [group_spec(total, LANES)] * 3,
            out_specs=chunk_spec(rows, 3 * width),
            scratch_shapes=[pltpu.VMEM((total, width), bf16)]
            + [pltpu.VMEM((total, width), f32)] * 3,
        ),
        out_shape=jax.ShapeDtypeStruct((4, 2, rows, 3 * width), bf16),
        compiler_params=pltpu.CompilerParams(vmem_limit_bytes=40 << 20),
        cost_estimate=pl.CostEstimate(flops=0, bytes_accessed=0, transcendentals=0),
    )(scalars, kept, sums, grad16.reshape(4, 2, rows, width), *tables)
    return mixed_grad.reshape(8 * rows, 3 * width)


def call(kernel, args, grid, in_specs, out_specs, out_shape, scratch_shapes=(), scalars=0):
    return pl.pallas_call(
        kernel,
        grid_spec=pltpu.PrefetchScalarGridSpec(
            num_scalar_prefetch=scalars,
            grid=grid,
            in_specs=in_specs,
            out_specs=out_specs,
            scratch_shapes=scratch_shapes,
        ),
        out_shape=out_shape,
        compiler_params=pltpu.CompilerParams(vmem_limit_bytes=48 << 20),
        cost_estimate=pl.CostEstimate(flops=0, bytes_accessed=0, transcendentals=0),
    )(*args)


def mix_kernel(left_ref, right_ref, shift_ref, out_ref):
    out_ref[...] = nn(left_ref[...], right_ref[...]) + shift_ref[...]


def mix_product(normed, mixed_full, shift):
    rows, width = normed.shape
    cols = shift.shape[1]
    block = rows // 3
    return call(
        mix_kernel,
        (normed, mixed_full, shift.reshape(1, cols)),
        (3,),
        [
            pl.BlockSpec((block, width), lambda i: (i, 0)),
            pl.BlockSpec((width, cols), lambda i: (0, 0)),
            pl.BlockSpec((1, cols), lambda i: (0, 0)),
        ],
        pl.BlockSpec((block, cols), lambda i: (i, 0)),
        jax.ShapeDtypeStruct((rows, cols), f32),
    )


def hide_kernel(left_ref, right_ref, shift_ref, out_ref, slope_ref):
    value = nn(left_ref[...], right_ref[...]) + shift_ref[...]
    inner = math.sqrt(2.0 / math.pi)
    square = value * value
    bend = jnp.tanh(inner * value * (1.0 + 0.044715 * square))
    half = 0.5 * (1.0 + bend)
    out_ref[...] = (value * half).astype(bf16)
    slope = 0.5 * value * (1.0 - bend * bend) * (inner * (1.0 + 3.0 * 0.044715 * square))
    slope_ref[...] = (half + slope).astype(slope_ref.dtype)


def hide_product(normed, up_full, shift):
    rows, width = normed.shape
    cols = up_full.shape[1]
    block = rows // 6
    out = pl.BlockSpec((block, cols), lambda i: (i, 0))
    return call(
        hide_kernel,
        (normed, up_full, shift.reshape(1, cols)),
        (6,),
        [
            pl.BlockSpec((block, width), lambda i: (i, 0)),
            pl.BlockSpec((width, cols), lambda i: (0, 0)),
            pl.BlockSpec((1, cols), lambda i: (0, 0)),
        ],
        [out, out],
        [jax.ShapeDtypeStruct((rows, cols), dtype) for dtype in (bf16, f32)],
    )


def out_kernel(first_ref, second_ref, dense_ref, down_ref, out_ref):
    value = nt(first_ref[...], dense_ref[...]) + nn(second_ref[...], down_ref[...])
    out_ref[...] = value.astype(out_ref.dtype)


def out_product(attended, hidden, mixed_full, down_full, half, dtype):
    rows, width = attended.shape[0] // 2, down_full.shape[1]
    heads = attended.shape[1]
    return call(
        out_kernel,
        (attended, hidden, mixed_full, down_full),
        (width // 512,),
        [
            pl.BlockSpec((rows, heads), lambda j: (half, 0)),
            pl.BlockSpec((rows, hidden.shape[1]), lambda j: (half, 0)),
            pl.BlockSpec((512, heads), lambda j: (j, 3)),
            pl.BlockSpec((hidden.shape[1], 512), lambda j: (0, j)),
        ],
        pl.BlockSpec((rows, 512), lambda j: (0, j)),
        jax.ShapeDtypeStruct((rows, width), dtype),
    )


def nn_kernel(left_ref, right_ref, out_ref):
    out_ref[...] = nn(left_ref[...], right_ref[...]).astype(out_ref.dtype)


def nt_scaled_kernel(left_ref, right_ref, slope_ref, out_ref):
    value = nt(left_ref[...], right_ref[...]) * slope_ref[...].astype(f32)
    out_ref[...] = value.astype(out_ref.dtype)


def attended_back(grad16, mixed_full, heads):
    rows, width = grad16.shape
    block = rows // 3
    return call(
        nn_kernel,
        (grad16, mixed_full),
        (3,),
        [
            pl.BlockSpec((block, width), lambda i: (i, 0)),
            pl.BlockSpec((width, heads), lambda i: (0, 3)),
        ],
        pl.BlockSpec((block, heads), lambda i: (i, 0)),
        jax.ShapeDtypeStruct((rows, heads), bf16),
    )


def hidden_back(grad16, down_full, slope):
    rows, width = grad16.shape
    cols = slope.shape[1]
    block = rows // 2
    spec = pl.BlockSpec((block, 256), lambda i, j: (i, j))
    return call(
        nt_scaled_kernel,
        (grad16, down_full, slope),
        (2, cols // 256),
        [
            pl.BlockSpec((block, width), lambda i, j: (i, 0)),
            pl.BlockSpec((256, width), lambda i, j: (j, 0)),
            spec,
        ],
        spec,
        jax.ShapeDtypeStruct((rows, cols), bf16),
    )


def both_kernel(first_ref, second_ref, proj_ref, up_ref, out_ref):
    value = nt(first_ref[...], proj_ref[...]) + nt(second_ref[...], up_ref[...])
    out_ref[...] = value.astype(out_ref.dtype)


def normed_back(mixed_grad, pre_grad, mixed_full, up_full, half, dtype):
    rows, width = mixed_grad.shape[0] // 2, up_full.shape[0]
    return call(
        both_kernel,
        (mixed_grad, pre_grad, mixed_full, up_full),
        (width // 512,),
        [
            pl.BlockSpec((rows, mixed_grad.shape[1]), lambda j: (half, 0)),
            pl.BlockSpec((rows, pre_grad.shape[1]), lambda j: (half, 0)),
            pl.BlockSpec((512, mixed_grad.shape[1]), lambda j: (j, 0)),
            pl.BlockSpec((512, up_full.shape[1]), lambda j: (j, 0)),
        ],
        pl.BlockSpec((rows, 512), lambda j: (0, j)),
        jax.ShapeDtypeStruct((rows, width), dtype),
    )


def in_grad_kernel(left_ref, right_ref, *refs):
    value = tn(left_ref[...], right_ref[...])
    for ref in refs[:-1]:
        value = value + ref[...].astype(f32)
    refs[-1][...] = value.astype(bf16)


def in_grad(part, k, normed, grad, *others):
    rows, cols = grad.shape
    block = min(part, 256)
    steps = part // block
    spec = pl.BlockSpec((block, cols), lambda i: (i, 0))
    return call(
        in_grad_kernel,
        (normed, grad, *others),
        (steps,),
        [
            pl.BlockSpec((rows, block), lambda i: (0, k * steps + i)),
            pl.BlockSpec((rows, cols), lambda i: (0, 0)),
        ]
        + [spec] * len(others),
        spec,
        jax.ShapeDtypeStruct((part, cols), bf16),
    )


def down_grad(part, k, hidden, grad, *others):
    rows, height = hidden.shape
    block = min(part, 256)
    steps = part // block
    spec = pl.BlockSpec((height, block), lambda j: (0, j))
    return call(
        in_grad_kernel,
        (hidden, grad, *others),
        (steps,),
        [
            pl.BlockSpec((rows, height), lambda j: (0, 0)),
            pl.BlockSpec((rows, block), lambda j: (0, k * steps + j)),
        ]
        + [spec] * len(others),
        spec,
        jax.ShapeDtypeStruct((height, part), bf16),
    )


def mixed_grad_kernel(normed_ref, mixed_ref, grad_ref, attended_ref, *refs):
    split = mixed_ref.shape[1]
    values = (tn(normed_ref[...], mixed_ref[...]), tn(grad_ref[...], attended_ref[...]))
    for value, cols in zip(values, (slice(0, split), slice(split, None))):
        for ref in refs[:-1]:
            value = value + ref[:, cols].astype(f32)
        refs[-1][:, cols] = value.astype(bf16)


def mixed_weight_grad(part, k, normed, mixed_grad, grad, attended, *others):
    rows, heads = attended.shape
    width = mixed_grad.shape[1] + heads
    block = min(part, 256)
    steps = part // block
    spec = pl.BlockSpec((block, width), lambda i: (i, 0))
    slice_spec = pl.BlockSpec((rows, block), lambda i: (0, k * steps + i))
    return call(
        mixed_grad_kernel,
        (normed, mixed_grad, grad, attended, *others),
        (steps,),
        [
            slice_spec,
            pl.BlockSpec(mixed_grad.shape, lambda i: (0, 0)),
            slice_spec,
            pl.BlockSpec(attended.shape, lambda i: (0, 0)),
        ]
        + [spec] * len(others),
        spec,
        jax.ShapeDtypeStruct((part, width), bf16),
    )


def halves_kernel(axis, mid_ref, keep_ref, other_ref, *refs):
    out_ref, size = refs[-1], keep_ref.shape[axis]
    for part_ref, half in ((keep_ref, mid_ref[0]), (other_ref, 1 - mid_ref[0])):
        at = pl.ds(pl.multiple_of(half * size, LANES), size)
        if axis:
            out_ref[0, :, at] = part_ref[...].astype(f32)
        else:
            out_ref[0, at, :] = part_ref[...].astype(f32)


def place_halves(keep, other, mid, axis, layer, layers, before=None):
    rows, cols = keep.shape
    shape = (rows, 2 * cols) if axis else (2 * rows, cols)
    if cols % LANES or (axis == 0 and rows % LANES):
        line = jnp.concatenate([pick(keep, other, mid), pick(other, keep, mid)], axis=axis)
        line = line.astype(f32)[None]
        if before is None:
            return jnp.concatenate([jnp.zeros_like(line)] * layer + [line], axis=0)
        return jnp.concatenate([line, before[1:]], axis=0)
    spec = pl.BlockSpec((rows, cols), lambda i, mid_ref: (0, 0))
    given = [] if before is None else [before]
    return pl.pallas_call(
        partial(halves_kernel, axis),
        grid_spec=pltpu.PrefetchScalarGridSpec(
            num_scalar_prefetch=1,
            grid=(1,),
            in_specs=[spec, spec] + [pl.BlockSpec(memory_space=pl.ANY)] * len(given),
            out_specs=pl.BlockSpec((1, *shape), lambda i, mid_ref: (layer, 0, 0)),
        ),
        out_shape=jax.ShapeDtypeStruct((layers, *shape), f32),
        input_output_aliases={3: 0} if given else {},
        compiler_params=pltpu.CompilerParams(vmem_limit_bytes=32 << 20),
        cost_estimate=pl.CostEstimate(flops=0, bytes_accessed=0, transcendentals=0),
    )(mid.reshape(1), keep, other, *given)


def last_kernel(
    order_ref, low_ref, core_ref, x_ref, mid_ref, old_ref, shift_ref, out_ref, held
):
    branch = low_ref[...] + core_ref[...].astype(f32) + x_ref[...].astype(f32)
    held[...] = old_ref[...] + (branch + mid_ref[...].astype(f32)) + shift_ref[...]
    order_kernel(True, order_ref, held, out_ref)


def last_stream(order, low, core, x_low, mid, old, shift):
    rows, width = old.shape
    if width // order.shape[0] % LANES:
        branch = low[:rows] + core[:rows].astype(f32) + x_low.astype(f32) + mid.astype(f32)
        return reorder(old + branch + shift, order, f32, True)
    steps = row_steps(rows)
    row_spec = pl.BlockSpec((rows // steps, width), lambda i, order_ref: (i, 0))
    return call(
        last_kernel,
        (order, low, core, x_low, mid, old, shift),
        (steps,),
        [row_spec] * 5 + [pl.BlockSpec((1, width), lambda i, order_ref: (0, 0))],
        row_spec,
        jax.ShapeDtypeStruct((rows, width), f32),
        [pltpu.VMEM((rows // steps, width), f32)],
        scalars=1,
    )


def halves(value, half, axis):
    size = value.shape[axis] // 2
    return lax.dynamic_slice_in_dim(value, half * size, size, axis)


class Small:
    def __init__(self, seq, mine, tensor, mid, beside):
        self.seq, self.tensor = seq, tensor
        self.mine, self.beside = seq.settle(
            lambda mine: pair_up(mine, swap(mine, "dp", MID), mid, 0), mine[None], beside=beside
        )

    def second(self):
        def step(mine):
            for bit in side_bits():
                mine = jnp.concatenate([mine, swap(mine, "dp", bit)], axis=0)
            return mine[None]

        self.mine = self.seq.settle(step, self.mine)

    def finish(self, unpack):
        def step(mine):
            for bit in (0, 1):
                mine = pair_up(mine, swap(mine, "tensor", bit), (self.tensor >> bit) & 1, 0)
            return unpack(jnp.swapaxes(mine, 0, 1))

        return self.seq.settle(step, self.mine)


class SmallSums:
    def __init__(self, seq, norm_grads, in_bgrads, mid):
        self.seq, self.mid = seq, mid
        self.norm_grads, self.in_bgrads = norm_grads, in_bgrads
        self.layers, self.kinds = len(norm_grads), 3
        self.sides = side_bits()

    def halve(self, sums, biases, axis, half, move):
        keep, sent = halves(sums, half, axis), halves(sums, 1 - half, axis)
        split = biases.shape[0]
        received = move(jnp.concatenate([biases, sent.reshape(-1)]))
        return keep + received[split:].reshape(keep.shape), received[:split]

    def side(self, s, sums, biases):
        sums, other = self.halve(
            sums, biases, 1, 0, lambda value: swap(value, "dp", self.sides[s])
        )
        return sums, biases + other

    def first(self):
        tensor = lax.axis_index("tensor")

        def step(*values):
            sums = jnp.stack([value[: self.kinds] for value in values[: self.layers]])
            biases = jnp.concatenate(values[self.layers :])
            shape = (self.layers * self.kinds, 1 << len(self.sides), 2, lax.axis_size("tensor"), -1)
            sums, biases = self.side(len(self.sides) - 1, sums.reshape(shape), biases)
            none = biases[:0]
            for bit in (1, 0):
                sums, _ = self.halve(
                    sums, none, 3, (tensor >> bit) & 1, lambda value: swap(value, "tensor", bit)
                )
            sums, other = self.halve(
                sums, biases, 2, self.mid, lambda value: swap(value, "dp", MID)
            )
            pair = (pick(biases, other, self.mid), pick(other, biases, self.mid))
            return sums, jnp.concatenate(pair)

        values = [value for pair in self.in_bgrads for value in pair]
        self.sums, self.biases = self.seq.settle(step, *self.norm_grads, *values)

    def finish(self):
        def step(sums, biases):
            for s in reversed(range(len(self.sides) - 1)):
                sums, biases = self.side(s, sums, biases)
            return sums, biases

        sums, biases = self.seq.settle(step, self.sums, self.biases)
        return sums.reshape(self.layers, self.kinds, -1), biases.reshape(2, -1)


def shards(
    tokens_in,
    lengths,
    norm_gain,
    norm_bias,
    proj_weight,
    proj_bias,
    dense_weight,
    dense_bias,
    up_weight,
    up_bias,
    down_weight,
    down_bias,
    cotangent,
):
    rows, width = tokens_in.shape
    layer_count = proj_weight.shape[0]
    n_dp = lax.axis_size("dp")
    dp = lax.axis_index("dp")
    tensor = lax.axis_index("tensor")
    mid = (dp >> MID) & 1
    order = slice_order()
    seq = Sequence(lengths[0, 0].astype(f32), lengths[0, 0] > 0)

    def take_mixed(l, half, weight=proj_weight):
        proj = halves(weight[l], half, 2).reshape(weight.shape[1], -1)
        return jnp.concatenate([proj, halves(dense_weight[l], half, 0).T], axis=1)

    def take_up(l, half, weight=up_weight):
        return halves(weight[l], half, 1)

    def take_down(l, half, weight=down_weight):
        return halves(weight[l], half, 0)

    takes = ((take_mixed, 0), (take_up, 0), (take_down, 1))

    def set_out(l, i):
        weight = (proj_weight, up_weight, down_weight)[i]
        part = seq.run(lambda value: takes[i][0](l, 1 - mid, value), weight, apart=True)
        return seq.start(part, "dp", MID)

    def paired(l, i, moving):
        return joined(l, i, seq.wait(moving))

    def joined(l, i, received):
        take, axis = takes[i]
        block = seq.run(
            lambda other: pair_up(take(l, mid), other, mid, axis), received, apart=True
        )
        return Spread(seq, block, axis)

    moving = [set_out(0, 0), set_out(0, 1)]
    cot = seq.run(lambda value: reorder(value, order, bf16), cotangent)
    whole_lens = lengths.reshape(-1).astype(f32)
    coarse = jnp.floor(whole_lens / 8.0)
    small = Small(
        seq,
        jnp.concatenate(
            [
                value.reshape(-1)
                for value in (norm_gain, norm_bias, dense_bias, down_bias, proj_bias, up_bias)
            ]
            + [coarse.astype(bf16), (whole_lens - 8.0 * coarse).astype(bf16)]
        ),
        tensor,
        mid,
        lambda: swap(cot, "tensor", 1),
    )
    cot_across = small.beside
    small.second()
    m0 = paired(0, 0, moving[0])
    u0 = paired(0, 1, moving[1])
    m0.near()
    m0.far()
    each, proj_each, up_each = norm_gain.shape[1], proj_bias.shape[3], up_bias.shape[2]

    def unpack(everyone):
        pair_lens = lax.dynamic_index_in_dim(everyone[:2, :, -4:], tensor, 1, keepdims=False)
        pair_lens = pair_lens.astype(f32)
        pair_lens = (pair_lens[:, :2] * 8.0 + pair_lens[:, 2:]).astype(jnp.int32)
        lens = pick(pair_lens, pair_lens[::-1], mid)
        everyone = everyone[:, :, :-4]
        at = 4 * layer_count * each
        norm_parts = everyone[:, :, :at].reshape(n_dp, -1, 4 * layer_count, each)
        norm_parts = jnp.transpose(norm_parts, (2, 0, 1, 3)).reshape(4, layer_count, width)
        norm_parts = norm_parts.astype(f32)
        same_heads = lax.dynamic_index_in_dim(everyone[:, :, at:], tensor, 1, keepdims=False)
        same_heads = halves(same_heads[slice_places()], mid, 0).astype(f32)
        proj_at = layer_count * 3 * proj_each
        proj_shift = jnp.transpose(
            same_heads[:, :proj_at].reshape(-1, layer_count * 3, proj_each), (1, 0, 2)
        ).reshape(layer_count, -1)
        up_shift = jnp.transpose(
            same_heads[:, proj_at:].reshape(-1, layer_count, up_each), (1, 0, 2)
        ).reshape(layer_count, -1)
        gains, biases = norm_parts[0], norm_parts[1]
        shifts = norm_parts[2] + norm_parts[3]
        scalars = jnp.concatenate([lens.reshape(-1), tensor[None].astype(jnp.int32)])
        lines = [value[l] for value in (gains, biases, shifts) for l in range(layer_count)]
        lines += [value[l] for value in (proj_shift, up_shift) for l in range(layer_count)]
        return [line[None] for line in lines], lens, scalars.astype(jnp.int32)

    lines, lens, scalars = small.finish(unpack)
    gains, biases, out_shifts, proj_shift, up_shift = (
        lines[i * layer_count : (i + 1) * layer_count] for i in range(5)
    )

    def mix(l, normed, proj_full):
        return seq.run(mix_product, normed, proj_full, proj_shift[l])

    def attend(mixed):
        return seq.run(lambda value: attention_forward(value, tables, scalars, rows), mixed)

    def hide(l, normed, up_full):
        return seq.run(hide_product, normed, up_full, up_shift[l])

    def make_tables():
        return rotary_tables(jax.vmap(partial(layout, total=4 * rows, block=BLOCK))(lens))

    stream, own = seq.run(
        lambda value: norm_first(value, order, gains[0], biases[0]), tokens_in
    )
    tokens = Gather(seq, own, make_tables)
    token_parts, tables = tokens.parts, tokens.beside
    m0.near_wait()
    m0.far_wait()
    u0.far()
    m0.last()
    u0.near()
    sent = seq.run(lambda value: take_down(0, 1 - mid, value), down_weight, apart=True)

    def with_half(sent, own, mid, across, core_own, core_across):
        received, both = swap(sent, "dp", MID), swap(mid, "tensor", 1)
        received, both, mid = lax.optimization_barrier((received, both, mid))
        core_mid, core_both = swap(mid, "tensor", 0), swap(both, "tensor", 0)
        parts = (own, mid, across, both, core_own, core_mid, core_across, core_both)
        return received, assemble(parts, 0)

    received, normed = seq.settle(with_half, sent, *token_parts)
    d0 = joined(0, 2, received)
    u0.far_wait()
    seq.tick(3)
    u0.near_wait()
    m0.last_wait()
    u0.last()
    d0.far()
    mixed_full = m0.whole()
    mixed = mix(0, normed, mixed_full)
    d0.near()
    moving = [set_out(1, 0), set_out(1, 1)]
    attended, kept, sums = attend(mixed)
    u0.last_wait()
    up_full = u0.whole()
    hidden, slope = hide(0, normed, up_full)
    m1 = paired(1, 0, moving[0])
    u1 = paired(1, 1, moving[1])
    d0.far_wait()
    seq.tick(3)
    d0.near_wait()
    d0.last()
    cot_mid = seq.swap(cot, "dp", MID)
    m1.far()
    d0.last_wait()
    down_full = d0.whole()
    m1.near()
    moving = [set_out(1, 2)]
    saved = [(normed, kept, sums, slope, attended, hidden)]
    weights = [(mixed_full, up_full, down_full)]
    streams = [stream]

    branch = Scatter(seq, out_product, (attended, hidden, mixed_full, down_full), rows)
    branch.begin()
    branch.second()
    d1 = paired(1, 2, moving[0])
    m1.far_wait()
    seq.tick(2)
    m1.near_wait()
    m1.last()
    branch.third()
    u1.near()
    u1.far()
    stream, own = branch.finish(
        norm_after, stream, out_shifts[0], gains[1], biases[1]
    )
    streams.append(stream)

    def with_cores(mine, mid, cot, across):
        parts, both = gather_start_beside(mine, mid)
        *parts, cot, across = lax.optimization_barrier((*parts, cot, across))
        return parts, both, swap(cot, "tensor", 0), swap(across, "tensor", 0)

    parts, cot_both, cot_core_own, cot_core_across = seq.settle(
        with_cores, own, cot_mid, cot, cot_across
    )
    m1.last_wait()
    u1.near_wait()
    u1.far_wait()
    d1.near()
    d1.far()
    u1.last()
    grad16, normed, mixed_full = seq.settle(
        lambda *values: gather_finish_beside(values[:5], values[5:], m1.plain),
        *parts,
        cot,
        cot_mid,
        cot_across,
        cot_both,
        cot_core_own,
        cot_core_across,
    )
    mixed = mix(1, normed, mixed_full)
    d1.near_wait()
    u1.last_wait()
    attended, kept, sums = attend(mixed)
    up_full = u1.whole()
    hidden, slope = hide(1, normed, up_full)
    d1.far_wait()
    d1.last()
    saved.append((normed, kept, sums, slope, attended, hidden))
    weights.append((mixed_full, up_full, None))

    heads_width = attended.shape[1]
    parts = 1 << len(side_bits())
    norm_grads, in_bgrads = [None] * layer_count, [None] * layer_count

    part = width // parts

    def down_grads(l, grad16):
        return Reduce(seq, partial(down_grad, part), saved[l][5], grad16)

    def up_grads(l, grad):
        return Reduce(seq, partial(in_grad, part), saved[l][0], grad)

    def mixed_grads(l, grad, grad16):
        values = saved[l][0], grad, grad16, saved[l][4]
        return Reduce(seq, partial(mixed_weight_grad, part), *values)

    def attend_back(l, grad16):
        kept, sums = saved[l][1:3]
        mixed_full = weights[l][0]

        def step(value):
            grad = attended_back(value, mixed_full, heads_width)
            return attention_backward(kept, sums, grad, tables, scalars, rows)

        return seq.run(step, grad16)

    def hide_back(l, grad16):
        slope, down_full = saved[l][3], weights[l][2]
        return seq.run(lambda value: hidden_back(value, down_full, slope), grad16)

    def rows_back(l, mixed_grad, pre_grad):
        return Scatter(seq, normed_back, (mixed_grad, pre_grad, *weights[l][:2]), rows)

    def bias_back(mixed_grad, pre_grad):
        return jnp.sum(mixed_grad, axis=0, dtype=f32), jnp.sum(pre_grad, axis=0, dtype=f32)

    def own_start(total, axis):
        return halves(total, mid, axis), seq.start(halves(total, 1 - mid, axis), "dp", MID)

    def own_wait(pair):
        keep, moving = pair
        received = seq.wait(moving)
        return pick(keep, received, mid).astype(f32), pick(received, keep, mid).astype(f32)

    first, second = 0, 1
    early = len(side_bits()) == 2

    def send(reduce, which):
        reduce.send(reduce.near(which))

    def arrive(reduce, which):
        reduce.wait(reduce.near(which))

    def rest(reduce):
        for which in (first, second):
            reduce.make(reduce.near(which))
            send(reduce, which)
            arrive(reduce, which)
        reduce.make_far()
        reduce.send_far()
        reduce.wait_far()
        reduce.finish()

    down2 = down_grads(1, grad16)
    down2.make(down2.near(first))
    if early:
        send(down2, first)
    mixed_grad = attend_back(1, grad16)
    d1.last_wait()
    weights[1] = (mixed_full, up_full, d1.whole())
    if early:
        down2.make(down2.near(second))
        send(down2, second)
    pre_grad = hide_back(1, grad16)
    up2, mix2 = up_grads(1, pre_grad), mixed_grads(1, mixed_grad, grad16)
    back = rows_back(1, mixed_grad, pre_grad)
    back.begin()
    branch = Scatter(seq, out_product, (attended, hidden, *weights[1][::2]), rows)
    if early:
        arrive(down2, first)
        up2.make(up2.near(first))
        send(up2, first)
    made = back.second(
        lambda: (
            down2.plain(down2.far()) if early else (),
            up2.plain(up2.near(second)),
            mix2.plain(mix2.near(first)),
            mix2.plain(mix2.near(second)),
            bias_back(mixed_grad, pre_grad),
        )
    )
    in_bgrads[1] = made[4]
    if early:
        down2.take(down2.far(), made[0])
        up2.take(up2.near(second), made[1])
        mix2.take(mix2.near(first), made[2])
        mix2.take(mix2.near(second), made[3])
        arrive(down2, second)
        seq.tick(4)
        arrive(up2, first)
        send(up2, second)
    made = back.third(lambda: (up2.plain(up2.far()) if early else (), branch.plain()))
    branch.take(made[1])
    norm_grads[1], grad_stream, own = back.finish(
        norm_before, cot, streams[1], gains[1]
    )
    if early:
        up2.take(up2.far(), made[0])
        arrive(up2, second)
        send(mix2, first)
        down2.send_far()
    (branch.later, branch.x_high), coming = seq.settle(
        lambda own, low, core: gather_start_with(own, low, core, branch.sent_across),
        own,
        branch.low_part,
        branch.core,
    )
    if early:
        arrive(mix2, first)
        send(mix2, second)
        up2.send_far()
        grad16, made = seq.settle(gather_finish, *coming, beside=lambda: mix2.plain(mix2.far()))
        mix2.take(mix2.far(), made)
        mix2.send_far()
        down2.wait_far()
    else:
        grad16 = seq.settle(gather_finish, *coming)
        rest(down2)
        rest(up2)
        rest(mix2)

    results = {}

    def own_start(total, axis):
        keep, sent = seq.run(
            lambda value: (halves(value, mid, axis), halves(value, 1 - mid, axis)),
            total,
            apart=True,
        )
        return keep, seq.start(sent, "dp", MID)

    def own_finish(l, name, axis, pair):
        keep, moving = pair
        received = seq.wait(moving)
        before = results.get(name)
        given = () if before is None else (before,)
        results[name] = seq.run(
            lambda keep, other, *given: place_halves(
                keep, other, mid, axis, l, layer_count, *given
            ),
            keep,
            received,
            *given,
        )

    def mixed_finish(pair):
        keep, moving = pair
        received = seq.wait(moving)
        cols = 3 * heads_width

        def step(keep, other):
            pair = [pick(keep, other, mid).astype(f32), pick(other, keep, mid).astype(f32)]
            proj = [value[:, :cols].reshape(value.shape[0], 3, -1) for value in pair]
            dense = [value[:, cols:].T for value in pair]
            return jnp.concatenate(proj, axis=2), jnp.concatenate(dense, axis=0)

        return seq.run(step, keep, received, apart=True)

    down1 = down_grads(0, grad16)
    down1.make(down1.near(first))
    if early:
        send(down1, first)
        down2.make([0])
    down2_pair = own_start(down2.blocks[0], 1)
    mixed_grad = attend_back(0, grad16)
    down1.make(down1.near(second))
    if early:
        up2.wait_far()
        arrive(mix2, second)
        send(down1, second)
    pre_grad = hide_back(0, grad16)
    up1, mix1 = up_grads(0, pre_grad), mixed_grads(0, mixed_grad, grad16)
    up1.make(up1.near(first))
    if early:
        send(up1, first)
        up2.make([0])
    own_finish(1, "down", 0, down2_pair)
    up1.make(up1.near(second))
    mix1.make(mix1.near(first))
    if early:
        mix2.wait_far()
        seq.tick(5)
        arrive(down1, first)
        down1.make_far()
        arrive(down1, second)
        down1.send_far()
        send(up1, second)
    back = rows_back(0, mixed_grad, pre_grad)
    back.begin()
    if early:
        arrive(up1, first)
        up1.make_far()
        up1.send_far()
    branch.third()
    if early:
        send(mix1, first)
        mix2.make([0])
    activations = branch.finish(partial(last_stream, order), streams[1], out_shifts[1])
    up2_halves = seq.run(
        lambda value: (halves(value, mid, 0), halves(value, 1 - mid, 0)), up2.blocks[0], apart=True
    )
    made = back.second(
        lambda: (
            mix1.plain(mix1.near(second)),
            bias_back(mixed_grad, pre_grad),
            swap(up2_halves[1], "dp", MID),
        )
    )
    mix1.take(mix1.near(second), made[0])
    in_bgrads[0] = made[1]
    if early:
        down1.wait_far()
        seq.tick(1)
        arrive(up1, second)
        seq.tick(1)
        arrive(mix1, first)
        mix1.make_far()
        mix1.send_far()
        send(mix1, second)
    results["up"] = seq.run(
        lambda keep, other: place_halves(keep, other, mid, 1, 1, layer_count),
        up2_halves[0],
        made[2],
    )
    made = back.third(lambda: down1.plain([0]) if early else ())
    norm_grads[0], grad_stream, own = back.finish(
        norm_before, grad_stream, streams[0], gains[0]
    )
    if early:
        down1.take([0], made)
    else:
        rest(down1)
        rest(up1)
        rest(mix1)
    small_sums = SmallSums(seq, norm_grads, in_bgrads, mid)
    small_sums.first()
    if early:
        up1.wait_far()
    mix2_pair = own_start(mix2.blocks[0], 0)
    down1_pair = own_start(down1.blocks[0], 1)
    if early:
        up1.make([0])
    up1_pair = own_start(up1.blocks[0], 0)
    mix2_own = mixed_finish(mix2_pair)
    if early:
        mix1.wait_far()
        seq.tick(4)
        arrive(mix1, second)
        mix1.make([0])
    mix1_pair = own_start(mix1.blocks[0], 0)
    input_grad = seq.run(lambda value: reorder(value, order, f32, True), grad_stream)
    own_finish(0, "down", 0, down1_pair)
    own_finish(0, "up", 1, up1_pair)
    norm_owned, bias_both = small_sums.finish()
    mix1_own = mixed_finish(mix1_pair)
    bias_both = bias_both + 0.0 * seq.scalar
    per_layer = bias_both.shape[1] // layer_count
    bias_both = bias_both.reshape(2, layer_count, per_layer)
    proj_b = jnp.transpose(
        bias_both[:, :, : 3 * heads_width].reshape(2, layer_count, 3, heads_width), (1, 2, 0, 3)
    ).reshape(layer_count, 3, 1, 2 * heads_width)
    up_b = jnp.transpose(bias_both[:, :, 3 * heads_width :], (1, 0, 2)).reshape(layer_count, 1, -1)
    return (
        activations,
        input_grad,
        norm_owned[:, 0],
        norm_owned[:, 1],
        jnp.stack([mix1_own[0], mix2_own[0]]),
        lax.dynamic_slice_in_dim(proj_b, dp * proj_each, proj_each, 3),
        jnp.stack([mix1_own[1], mix2_own[1]]),
        norm_owned[:, 2],
        results["up"],
        lax.dynamic_slice_in_dim(up_b, dp * up_each, up_each, 2),
        results["down"],
        norm_owned[:, 2],
    )


def solution(mesh):
    in_specs = (
        P(("dp", "tensor"), None),
        P("dp", None),
        P(None, ("dp", "tensor")),
        P(None, ("dp", "tensor")),
        P(None, "dp", None, "tensor"),
        P(None, None, "tensor", "dp"),
        P(None, "tensor", "dp"),
        P(None, ("dp", "tensor")),
        P(None, "dp", "tensor"),
        P(None, "tensor", "dp"),
        P(None, "tensor", "dp"),
        P(None, ("dp", "tensor")),
        P(("dp", "tensor"), None),
    )
    out_specs = (
        P(("dp", "tensor"), None),
        P(("dp", "tensor"), None),
        P(None, ("dp", "tensor")),
        P(None, ("dp", "tensor")),
        P(None, "dp", None, "tensor"),
        P(None, None, "tensor", "dp"),
        P(None, "tensor", "dp"),
        P(None, ("dp", "tensor")),
        P(None, "dp", "tensor"),
        P(None, "tensor", "dp"),
        P(None, "tensor", "dp"),
        P(None, ("dp", "tensor")),
    )
    return jax.shard_map(shards, mesh=mesh, in_specs=in_specs, out_specs=out_specs, check_vma=False)
```

```python
from functools import partial
import math

import jax
import jax.numpy as jnp
from jax import lax
from jax.experimental import pallas as pl
from jax.experimental.pallas import tpu as pltpu
from jax.sharding import PartitionSpec as P

HEAD_DIM = 64
ROT = 32
BLOCK = 128
LANES = 128
TILE = 256
MID = 1

TICK = 1_200_000_000

neg_large = -1e30
f32 = jnp.float32
bf16 = jnp.bfloat16


def swap(value, axis, bit):
    size = lax.axis_size(axis)
    return lax.ppermute(value, axis, [(i, i ^ (1 << bit)) for i in range(size)])


def tick_kernel(in_ref, out_ref):
    out_ref[0, 0] = in_ref[0, 0]


def tick(scalar, count):
    spec = pl.BlockSpec(memory_space=pltpu.SMEM)
    result = pl.pallas_call(
        tick_kernel,
        in_specs=[spec],
        out_specs=spec,
        out_shape=jax.ShapeDtypeStruct((1, 1), f32),
        cost_estimate=pl.CostEstimate(flops=count * TICK, bytes_accessed=0, transcendentals=0),
    )(scalar.reshape(1, 1))
    return result[0, 0]


class Sequence:
    def __init__(self, scalar, always):
        self.scalar = scalar
        self.always = always

    def gate(self, *values):
        *values, self.scalar = lax.optimization_barrier((*values, self.scalar))
        return values

    def run(self, step, *values, apart=False):
        values = self.gate(*values)
        if apart:
            shapes = jax.eval_shape(step, *values)

            def never(*others):
                return jax.tree.map(lambda shape: jnp.zeros(shape.shape, shape.dtype), shapes)

            result = lax.cond(self.always, step, never, *values)
        else:
            result = step(*values)
        leaves, tree = jax.tree.flatten(result)
        return jax.tree.unflatten(tree, self.gate(*leaves))

    def start(self, value, axis, bit):
        (value,) = self.gate(value)
        return swap(value, axis, bit)

    def wait(self, value):
        (value,) = self.gate(value)
        return value

    def settle(self, step, *values, beside=None):
        def both(*moved):
            return (step(*moved), beside()) if beside else step(*moved)

        return self.run(both, *values, apart=True)

    def tick(self, count):
        self.scalar = tick(self.scalar, count)

    def swap(self, value, axis, bit):
        return self.settle(lambda moved: swap(moved, axis, bit), value)


def side_bits():
    count = (lax.axis_size("dp") - 1).bit_length()
    return [bit for bit in range(count - 1, MID, -1)] + [0]


def slice_order():
    sides = side_bits()
    me = lax.axis_index("dp")
    base = me - (((me >> MID) & 1) << MID)
    order = []
    for k in range(1 << len(sides)):
        mask = sum(((k >> s) & 1) << bit for s, bit in enumerate(sides))
        for mid in range(2):
            order.append((base ^ mask) | (mid << MID))
    return jnp.stack(order).astype(jnp.int32)


def slice_places():
    sides = side_bits()
    every = jnp.arange(lax.axis_size("dp"), dtype=jnp.int32)
    apart = every ^ lax.axis_index("dp")
    place = (every >> MID) & 1
    for s, bit in enumerate(sides):
        place = place + (((apart >> bit) & 1) << (s + 1))
    return place


def pick(pair_first, pair_second, bit):
    return jnp.where(bit == 0, pair_first, pair_second)


def pair_up(keep, received, bit, axis):
    return jnp.concatenate(
        [pick(keep, received, bit), pick(received, keep, bit)], axis=axis
    )


class Spread:
    def __init__(self, seq, block, axis):
        self.seq, self.axis = seq, axis
        self.sides = side_bits()
        self.far_count = 1 << (len(self.sides) - 1)
        self.blocks = {0: block}

    def move(self, ks):
        for k in ks:
            if k != ks[0]:
                self.arrived(ks)
            s = k.bit_length() - 1
            self.blocks[k] = self.seq.start(self.blocks[k - (1 << s)], "dp", self.sides[s])

    def arrived(self, ks):
        last = max(k for k in ks if k in self.blocks)
        self.blocks[last] = self.seq.wait(self.blocks[last])

    def far(self):
        self.move(range(1, self.far_count))

    def far_wait(self):
        self.arrived(range(1, self.far_count))

    def near(self):
        self.move([self.far_count])

    def near_wait(self):
        self.arrived([self.far_count])

    def last(self):
        self.move(range(self.far_count + 1, 2 * self.far_count))

    def last_wait(self):
        self.arrived(range(self.far_count + 1, 2 * self.far_count))

    def plain(self, window=None):
        parts = [self.blocks[k] for k in sorted(self.blocks)]
        return assemble(parts, self.axis, window)

    def whole(self, window=None):
        parts = [self.blocks[k] for k in sorted(self.blocks)]
        return self.seq.run(lambda *values: assemble(values, self.axis, window), *parts)


class Reduce:
    def __init__(self, seq, product, *operands):
        self.seq, self.product, self.operands = seq, product, operands
        self.sides = side_bits()
        self.count = 1 << len(self.sides)
        self.blocks = {}
        self.arrived = [[] for _ in range(self.count)]
        self.moving = {}

    def make(self, ks):
        for k in ks:
            values = (*self.operands, *self.arrived[k])
            self.blocks[k] = self.seq.run(partial(self.product, k), *values)

    def plain(self, ks):
        return [self.product(k, *self.operands, *self.arrived[k]) for k in ks]

    def take(self, ks, made):
        self.blocks.update(zip(ks, made))

    def send(self, ks):
        for i, k in enumerate(ks):
            if i:
                self.wait([ks[i - 1]])
            s = k.bit_length() - 1
            self.moving[k] = self.seq.start(self.blocks[k], "dp", self.sides[s])

    def wait(self, ks):
        k = ks[-1]
        s = k.bit_length() - 1
        self.arrived[k - (1 << s)].append(self.seq.wait(self.moving[k]))

    def near(self, half):
        whole = list(reversed(range(self.count // 2, self.count)))
        middle = len(whole) // 2
        return whole[middle:] if half else whole[:middle]

    def far(self):
        return list(reversed(range(1, self.count // 2)))

    def make_far(self, near_done=True):
        ks = self.far()
        if ks[-1] in self.blocks or not (near_done or len(ks) == 1):
            return
        for k in ks[:-1]:
            self.make([k])
            self.send([k])
            self.wait([k])
        self.make(ks[-1:])

    def send_far(self):
        self.send(self.far()[-1:])

    def wait_far(self):
        self.wait(self.far()[-1:])

    def finish(self):
        self.make([0])
        return self.blocks[0]


def gather_start(own):
    mid, across = swap(own, "dp", MID), swap(own, "tensor", 1)
    own, mid, across = lax.optimization_barrier((own, mid, across))
    return own, mid, across, swap(own, "tensor", 0), swap(across, "tensor", 0)


def gather_start_with(own, low, core, sent):
    mid, across = swap(own, "dp", MID), swap(own, "tensor", 1)
    low, core, across = lax.optimization_barrier((low, core, across))
    later, x_high = sent(low, core)
    own, mid, across, x_high = lax.optimization_barrier((own, mid, across, x_high))
    core_parts = swap(own, "tensor", 0), swap(across, "tensor", 0)
    return (later, x_high), (own, mid, across, *core_parts)


def gather_finish(own, mid, across, core_own, core_across):
    both, core_mid = swap(mid, "tensor", 1), swap(mid, "tensor", 0)
    core_both = swap(both, "tensor", 0)
    parts = (own, mid, across, both, core_own, core_mid, core_across, core_both)
    return assemble(parts, 0)


class Gather:
    def __init__(self, seq, own, beside=None):
        self.seq = seq
        self.parts = seq.settle(gather_start, own, beside=beside)
        if beside:
            self.parts, self.beside = self.parts

    def finish(self, beside=None):
        return self.seq.settle(gather_finish, *self.parts, beside=beside)


def gather_start_beside(mine, mid):
    own, near, across = mine, swap(mine, "dp", MID), swap(mine, "tensor", 1)
    across, mid = lax.optimization_barrier((across, mid))
    both = swap(mid, "tensor", 1)
    own, near, across, both = lax.optimization_barrier((own, near, across, both))
    return (own, near, across, swap(own, "tensor", 0), swap(across, "tensor", 0)), both


def gather_finish_beside(parts, other, beside):
    own, mid, across, core_own, core_across = parts
    other_own, other_mid, other_across, other_both, other_core_own, other_core_across = other
    both, core_mid = swap(mid, "tensor", 1), swap(mid, "tensor", 0)
    core_mid, other_mid = lax.optimization_barrier((core_mid, other_mid))
    other_core_mid = swap(other_mid, "tensor", 0)
    other_core_mid, other_both = lax.optimization_barrier((other_core_mid, other_both))
    other_core_both = swap(other_both, "tensor", 0)
    others = (other_own, other_mid, other_across, other_both)
    others += (other_core_own, other_core_mid, other_core_across, other_core_both)
    whole, made = assemble(others, 0), beside()
    both, whole, made = lax.optimization_barrier((both, whole, made))
    core_both = swap(both, "tensor", 0)
    mine = (own, mid, across, both, core_own, core_mid, core_across, core_both)
    return whole, assemble(mine, 0), made


class Scatter:
    def __init__(self, seq, product, operands, rows):
        self.seq, self.product, self.operands, self.rows = seq, product, operands, rows

    def begin(self, beside=tuple):
        high = self.seq.run(lambda *values: self.product(*values, 1, bf16), *self.operands)
        self.core, (self.low_part, made) = self.seq.settle(
            lambda high: swap(high, "tensor", 0),
            high,
            beside=lambda: (self.product(*self.operands, 0, f32), beside()),
        )
        return made

    def plain(self):
        high = self.product(*self.operands, 1, bf16)
        return self.product(*self.operands, 0, f32), swap(high, "tensor", 0)

    def take(self, made):
        self.low_part, self.core = made

    def chunk(self, low, core, k, *others):
        at = slice(k * self.rows, (k + 1) * self.rows)
        part = low[at] + core[at].astype(f32)
        for value in others:
            part = part + value.astype(f32)
        return part

    def sent(self, low, core):
        return tuple(self.chunk(low, core, k).astype(bf16) for k in (2, 3))

    def next(self, low, core, other):
        return self.chunk(low, core, 1, other).astype(bf16)

    def second(self, beside=None):
        def step(low, core):
            later, first = self.sent(low, core)
            return later, swap(first, "tensor", 1)

        moved = self.seq.settle(step, self.low_part, self.core, beside=beside)
        if beside:
            moved, made = moved
        self.later, self.x_high = moved
        return made if beside else None

    def third_step(self, low, core, other, later):
        return swap(self.next(low, core, other), "dp", MID), swap(later, "tensor", 1)

    def third(self, beside=None):
        values = (self.low_part, self.core, self.x_high, self.later)
        moved = self.seq.settle(self.third_step, *values, beside=beside)
        if beside:
            moved, made = moved
        self.mid, self.x_low = moved
        return made if beside else None

    def sent_across(self, low, core):
        later, first = self.sent(low, core)
        return later, swap(first, "tensor", 1)

    def finish(self, step, *others):
        return self.seq.run(step, self.low_part, self.core, self.x_low, self.mid, *others)


def order_kernel(back, order_ref, in_ref, out_ref):
    count = order_ref.shape[0]
    part = in_ref.shape[1] // count
    for i in range(count):
        there = pl.ds(pl.multiple_of(order_ref[i] * part, LANES), part)
        here = slice(i * part, (i + 1) * part)
        if back:
            out_ref[:, there] = in_ref[:, here].astype(out_ref.dtype)
        else:
            out_ref[:, here] = in_ref[:, there].astype(out_ref.dtype)


def reorder(value, order, dtype, back=False):
    rows, width = value.shape
    count = order.shape[0]
    part = width // count
    if part % LANES:
        blocks = value.reshape(rows, count, part)
        index = slice_places() if back else order
        return jnp.take(blocks, index, axis=1).reshape(rows, width).astype(dtype)
    spec = pl.BlockSpec((rows, width), lambda i, order_ref: (0, 0))
    return pl.pallas_call(
        partial(order_kernel, back),
        grid_spec=pltpu.PrefetchScalarGridSpec(
            num_scalar_prefetch=1, grid=(1,), in_specs=[spec], out_specs=spec
        ),
        out_shape=jax.ShapeDtypeStruct((rows, width), dtype),
    )(order, value)


def assemble_kernel(axis, window, *refs):
    parts, out_ref, held, in_sems, out_sems = refs[:-4], refs[-4], refs[-3], refs[-2], refs[-1]
    copies, at = [], 0
    for i, part in enumerate(parts):
        size = window[1] if axis else part.shape[0]
        where = (pl.ds(at, size),) if axis == 0 else (slice(None), pl.ds(at, size))
        copies.append(
            (
                pltpu.make_async_copy(
                    part.at[:, pl.ds(*window)], held.at[where], in_sems.at[i]
                ),
                pltpu.make_async_copy(held.at[where], out_ref.at[where], out_sems.at[i]),
            )
        )
        at += size
    for come, go in copies:
        come.start()
    for come, go in copies:
        come.wait()
        go.start()
    for come, go in copies:
        go.wait()


def assemble(parts, axis, window=None):
    rows, width = parts[0].shape
    window = window or (0, width)
    count = len(parts)
    shape = (rows * count, window[1]) if axis == 0 else (rows, window[1] * count)
    if window[1] % LANES or window[0] % LANES:
        return jnp.concatenate(
            [part[:, window[0] : window[0] + window[1]] for part in parts], axis=axis
        )
    return pl.pallas_call(
        partial(assemble_kernel, axis, window),
        in_specs=[pl.BlockSpec(memory_space=pl.ANY)] * count,
        out_specs=pl.BlockSpec(memory_space=pl.ANY),
        out_shape=jax.ShapeDtypeStruct(shape, parts[0].dtype),
        scratch_shapes=[
            pltpu.VMEM(shape, parts[0].dtype),
            pltpu.SemaphoreType.DMA((count,)),
            pltpu.SemaphoreType.DMA((count,)),
        ],
        compiler_params=pltpu.CompilerParams(vmem_limit_bytes=16 << 20),
        cost_estimate=pl.CostEstimate(flops=0, bytes_accessed=0, transcendentals=0),
    )(*parts)


def norm_kernel(
    low_ref, core_ref, x_ref, mid_ref, old_ref, shift_ref, gain_ref, bias_ref, stream_ref, out_ref
):
    branch = low_ref[...] + core_ref[...].astype(f32) + x_ref[...].astype(f32)
    stream = old_ref[...] + (branch + mid_ref[...].astype(f32)) + shift_ref[...]
    stream_ref[...] = stream
    centre = stream - jnp.mean(stream, axis=1, keepdims=True)
    spread_of = jnp.mean(centre * centre, axis=1, keepdims=True)
    out_ref[...] = (
        centre * lax.rsqrt(spread_of + 1e-05) * gain_ref[...] + bias_ref[...]
    ).astype(bf16)


def norm_back_kernel(
    low_ref, core_ref, x_ref, mid_ref, grad_ref, old_ref, gain_ref, sums_ref, grad_out_ref, out_ref
):
    normed_grad = low_ref[...] + core_ref[...].astype(f32) + x_ref[...].astype(f32)
    normed_grad = normed_grad + mid_ref[...].astype(f32)
    grad, old = grad_ref[...].astype(f32), old_ref[...]
    centre = old - jnp.mean(old, axis=1, keepdims=True)
    root = lax.rsqrt(jnp.mean(centre * centre, axis=1, keepdims=True) + 1e-05)
    hat = centre * root
    scaled = normed_grad * gain_ref[...]
    back = scaled - jnp.mean(scaled, axis=1, keepdims=True)
    back = root * (back - hat * jnp.mean(scaled * hat, axis=1, keepdims=True))
    result = grad + back
    grad_out_ref[...] = result
    out_ref[...] = result.astype(bf16)

    @pl.when(pl.program_id(0) == 0)
    def clear():
        sums_ref[...] = jnp.zeros_like(sums_ref)

    sums_ref[0:1, :] += jnp.sum(normed_grad * hat, axis=0, keepdims=True)
    sums_ref[1:2, :] += jnp.sum(normed_grad, axis=0, keepdims=True)
    sums_ref[2:3, :] += jnp.sum(grad, axis=0, keepdims=True)


def norm_first_kernel(order_ref, in_ref, gain_ref, bias_ref, stream_ref, out_ref):
    order_kernel(False, order_ref, in_ref, stream_ref)
    stream = stream_ref[...]
    centre = stream - jnp.mean(stream, axis=1, keepdims=True)
    spread_of = jnp.mean(centre * centre, axis=1, keepdims=True)
    out_ref[...] = (
        centre * lax.rsqrt(spread_of + 1e-05) * gain_ref[...] + bias_ref[...]
    ).astype(bf16)


def norm_first(value, order, gain, bias):
    rows, width = value.shape
    if width // order.shape[0] % LANES:
        stream = reorder(value, order, f32)
        centre = stream - jnp.mean(stream, axis=1, keepdims=True)
        spread_of = jnp.mean(centre * centre, axis=1, keepdims=True)
        return stream, (centre * lax.rsqrt(spread_of + 1e-05) * gain + bias).astype(bf16)
    steps = row_steps(rows)
    row_spec = pl.BlockSpec((rows // steps, width), lambda i, order_ref: (i, 0))
    line_spec = pl.BlockSpec((1, width), lambda i, order_ref: (0, 0))
    return call(
        norm_first_kernel,
        (order, value, gain.reshape(1, width), bias.reshape(1, width)),
        (steps,),
        [row_spec, line_spec, line_spec],
        [row_spec, row_spec],
        [jax.ShapeDtypeStruct((rows, width), dtype) for dtype in (f32, bf16)],
        scalars=1,
    )


def row_steps(rows):
    return rows // 48 if rows % 48 == 0 else 1


def norm_call(kernel, rows, width, row_values, line_values, out_shapes):
    steps = row_steps(rows)
    row_spec = pl.BlockSpec((rows // steps, width), lambda i: (i, 0))
    line_spec = pl.BlockSpec((1, width), lambda i: (0, 0))
    sum_spec = pl.BlockSpec((8, width), lambda i: (0, 0))
    return pl.pallas_call(
        kernel,
        grid=(steps,),
        in_specs=[row_spec] * len(row_values) + [line_spec] * len(line_values),
        out_specs=[row_spec if shape.shape[0] == rows else sum_spec for shape in out_shapes],
        out_shape=out_shapes,
        compiler_params=pltpu.CompilerParams(vmem_limit_bytes=40 << 20),
        cost_estimate=pl.CostEstimate(flops=0, bytes_accessed=0, transcendentals=0),
    )(*row_values, *[value.reshape(1, width) for value in line_values])


def norm_after(low, core, x_low, mid, old, shift, gain, bias):
    rows, width = old.shape
    out = [jax.ShapeDtypeStruct((rows, width), dtype) for dtype in (f32, bf16)]
    return norm_call(
        norm_kernel, rows, width, (low, core, x_low, mid, old), (shift, gain, bias), out
    )


def norm_before(low, core, x_low, mid, grad, old, gain):
    rows, width = old.shape
    out = [jax.ShapeDtypeStruct((8, width), f32)]
    out += [jax.ShapeDtypeStruct((rows, width), dtype) for dtype in (f32, bf16)]
    return norm_call(norm_back_kernel, rows, width, (low, core, x_low, mid, grad, old), (gain,), out)


def layout(lens, total, block):
    steps_index = jnp.arange(total, dtype=jnp.int32)
    blocks_first = (lens[0] + block - 1) // block
    second_start = blocks_first * block
    in_first = steps_index < lens[0]
    in_second = (steps_index >= second_start) & (steps_index < second_start + lens[1])
    return jnp.where(in_first, steps_index, jnp.where(in_second, steps_index - second_start, 0))


def rotary_tables(position):
    half_rot = ROT // 2
    lane = jnp.arange(LANES, dtype=jnp.int32) % HEAD_DIM
    freqs = 10000.0 ** (-((lane % half_rot).astype(f32) * 2.0) / ROT)
    angles = position.astype(f32)[..., None] * freqs
    cosine, sine = jnp.cos(angles), jnp.sin(angles)
    return (
        jnp.where(lane < ROT, cosine, 1.0),
        jnp.where(lane < half_rot, -sine, 0.0),
        jnp.where((lane >= half_rot) & (lane < ROT), sine, 0.0),
    )


def turn(field, cos, above, below, back=False):
    up = pltpu.roll(field, LANES - ROT // 2, 1) * above
    down = pltpu.roll(field, ROT // 2, 1) * below
    return field * cos - (up + down) if back else field * cos + (up + down)


def allowed_bias(scalars, group, first_row, rows, cols):
    first_len, second_len = scalars[2 * group], scalars[2 * group + 1]
    second_start = ((first_len + BLOCK - 1) // BLOCK) * BLOCK
    row = first_row + lax.broadcasted_iota(jnp.int32, (rows, 1), 0)
    in_second = (row >= second_start) & (row < second_start + second_len)
    start = jnp.where(row < first_len, 0, jnp.where(in_second, second_start, row))
    col = lax.broadcasted_iota(jnp.int32, (rows, cols), 1)
    return jnp.where((col >= start) & (col <= row), 0.0, neg_large)


def chunk_places(scalars, rows):
    me = scalars[4]
    return [pl.multiple_of((me ^ ((r % 2) * 2 + r // 2)) * rows, 64) for r in range(4)]


def head_mask(head):
    lane = lax.broadcasted_iota(jnp.int32, (1, LANES), 1)
    return jnp.where(lane // HEAD_DIM == head, 1.0, 0.0).astype(bf16)


def nt(left, right):
    return lax.dot_general(left, right, (((1,), (1,)), ((), ())), preferred_element_type=f32)


def nn(left, right):
    return jnp.dot(left, right, preferred_element_type=f32)


def tn(left, right):
    return lax.dot_general(left, right, (((0,), (0,)), ((), ())), preferred_element_type=f32)


def attention_kernel(
    scalars, mixed_ref, cos_ref, above_ref, below_ref, out_ref, kept_ref, sums_ref, held
):
    group = pl.program_id(0)
    rows = mixed_ref.shape[2]
    width = mixed_ref.shape[3] // 3
    total = 4 * rows
    places = chunk_places(scalars, rows)
    for r in range(4):
        at = pl.ds(places[r], rows)
        cos, above, below = cos_ref[0, at, :], above_ref[0, at, :], below_ref[0, at, :]
        for part in range(0, 2 * width, LANES):
            turned = turn(mixed_ref[r, 0, :, part : part + LANES], cos, above, below)
            if part < width:
                turned = turned.astype(bf16) * HEAD_DIM**-0.5
            kept_ref[0, at, part : part + LANES] = turned.astype(bf16)
        kept_ref[0, at, 2 * width :] = mixed_ref[r, 0, :, 2 * width :].astype(bf16)
    for first in range(0, total, TILE):
        cols = first + TILE
        bias = allowed_bias(scalars, group, first, TILE, cols)
        for pair in range(0, width, LANES):
            query = kept_ref[0, first:cols, pair : pair + LANES]
            key = kept_ref[0, :cols, width + pair : width + pair + LANES]
            value = kept_ref[0, :cols, 2 * width + pair : 2 * width + pair + LANES]
            result = None
            for head in range(LANES // HEAD_DIM):
                mask = head_mask(head)
                scores = nt(query * mask, key) + bias
                top = jnp.max(scores, axis=1, keepdims=True)
                expo = jnp.exp(scores - top)
                mass = jnp.sum(expo, axis=1, keepdims=True)
                probs16 = (expo * (1.0 / mass)).astype(bf16)
                mine = nn(probs16, value * mask)
                result = mine if result is None else result + mine
                at_head = pair // HEAD_DIM + head
                sums_ref[0, first:cols, at_head : at_head + 1] = top + jnp.log(mass)
            held[first:cols, pair : pair + LANES] = result.astype(bf16)
    for r in range(4):
        out_ref[r, 0] = held[pl.ds(places[r], rows), :]


def attention_back_kernel(
    scalars,
    kept_ref,
    sums_ref,
    grad_ref,
    cos_ref,
    above_ref,
    below_ref,
    out_ref,
    held,
    query_grad,
    key_grad,
    value_grad,
):
    group = pl.program_id(0)
    rows = grad_ref.shape[2]
    width = grad_ref.shape[3]
    total = 4 * rows
    places = chunk_places(scalars, rows)
    for r in range(4):
        held[pl.ds(places[r], rows), :] = grad_ref[r, 0]
    for first in reversed(range(0, total, TILE)):
        cols = first + TILE
        bias = allowed_bias(scalars, group, first, TILE, cols)
        for pair in range(0, width, LANES):
            lanes = slice(pair, pair + LANES)
            query = kept_ref[0, first:cols, pair : pair + LANES]
            key = kept_ref[0, :cols, width + pair : width + pair + LANES]
            value = kept_ref[0, :cols, 2 * width + pair : 2 * width + pair + LANES]
            grad = held[first:cols, lanes]
            grads = [None, None, None]
            for head in range(LANES // HEAD_DIM):
                mask = head_mask(head)
                at_head = pair // HEAD_DIM + head
                query_head, grad_head = query * mask, grad * mask
                scores = nt(query_head, key) + bias
                probs = jnp.exp(scores - sums_ref[0, first:cols, at_head : at_head + 1])
                prob_grad = nt(grad_head, value)
                mean = jnp.sum(probs * prob_grad, axis=1, keepdims=True)
                score_grad = (probs * (prob_grad - mean)).astype(bf16)
                mine = (
                    nn(score_grad, key * mask),
                    tn(score_grad, query_head),
                    tn(probs.astype(bf16), grad_head),
                )
                grads = [m if g is None else g + m for g, m in zip(grads, mine)]
            query_grad[first:cols, lanes] = grads[0]
            if cols == total:
                key_grad[:, lanes] = grads[1]
                value_grad[:, lanes] = grads[2]
            else:
                key_grad[:cols, lanes] += grads[1]
                value_grad[:cols, lanes] += grads[2]
    for r in range(4):
        at = pl.ds(places[r], rows)
        cos, above, below = cos_ref[0, at, :], above_ref[0, at, :], below_ref[0, at, :]
        for pair in range(0, width, LANES):
            query = turn(query_grad[at, pair : pair + LANES] * HEAD_DIM**-0.5, cos, above, below, True)
            key = turn(key_grad[at, pair : pair + LANES], cos, above, below, True)
            out_ref[r, 0, :, pair : pair + LANES] = query.astype(bf16)
            out_ref[r, 0, :, width + pair : width + pair + LANES] = key.astype(bf16)
        out_ref[r, 0, :, 2 * width :] = value_grad[at, :].astype(bf16)


def chunk_spec(rows, width):
    return pl.BlockSpec((4, 1, rows, width), lambda g, scalars: (0, g, 0, 0))


def group_spec(total, width):
    return pl.BlockSpec((1, total, width), lambda g, scalars: (g, 0, 0))


def attention_forward(mixed, tables, scalars, rows):
    width = mixed.shape[1] // 3
    total = 4 * rows
    attended, kept, sums = pl.pallas_call(
        attention_kernel,
        grid_spec=pltpu.PrefetchScalarGridSpec(
            num_scalar_prefetch=1,
            grid=(2,),
            in_specs=[chunk_spec(rows, 3 * width)] + [group_spec(total, LANES)] * 3,
            out_specs=[
                chunk_spec(rows, width),
                group_spec(total, 3 * width),
                group_spec(total, LANES),
            ],
            scratch_shapes=[pltpu.VMEM((total, width), bf16)],
        ),
        out_shape=[
            jax.ShapeDtypeStruct((4, 2, rows, width), bf16),
            jax.ShapeDtypeStruct((2, total, 3 * width), bf16),
            jax.ShapeDtypeStruct((2, total, LANES), f32),
        ],
        compiler_params=pltpu.CompilerParams(vmem_limit_bytes=40 << 20),
        cost_estimate=pl.CostEstimate(flops=0, bytes_accessed=0, transcendentals=0),
    )(scalars, mixed.reshape(4, 2, rows, 3 * width), *tables)
    return attended.reshape(8 * rows, width), kept, sums


def attention_backward(kept, sums, grad16, tables, scalars, rows):
    width = grad16.shape[1]
    total = 4 * rows
    mixed_grad = pl.pallas_call(
        attention_back_kernel,
        grid_spec=pltpu.PrefetchScalarGridSpec(
            num_scalar_prefetch=1,
            grid=(2,),
            in_specs=[
                group_spec(total, 3 * width),
                group_spec(total, LANES),
                chunk_spec(rows, width),
            ]
            + [group_spec(total, LANES)] * 3,
            out_specs=chunk_spec(rows, 3 * width),
            scratch_shapes=[pltpu.VMEM((total, width), bf16)]
            + [pltpu.VMEM((total, width), f32)] * 3,
        ),
        out_shape=jax.ShapeDtypeStruct((4, 2, rows, 3 * width), bf16),
        compiler_params=pltpu.CompilerParams(vmem_limit_bytes=40 << 20),
        cost_estimate=pl.CostEstimate(flops=0, bytes_accessed=0, transcendentals=0),
    )(scalars, kept, sums, grad16.reshape(4, 2, rows, width), *tables)
    return mixed_grad.reshape(8 * rows, 3 * width)


def call(kernel, args, grid, in_specs, out_specs, out_shape, scratch_shapes=(), scalars=0):
    return pl.pallas_call(
        kernel,
        grid_spec=pltpu.PrefetchScalarGridSpec(
            num_scalar_prefetch=scalars,
            grid=grid,
            in_specs=in_specs,
            out_specs=out_specs,
            scratch_shapes=scratch_shapes,
        ),
        out_shape=out_shape,
        compiler_params=pltpu.CompilerParams(vmem_limit_bytes=48 << 20),
        cost_estimate=pl.CostEstimate(flops=0, bytes_accessed=0, transcendentals=0),
    )(*args)


def mix_kernel(left_ref, right_ref, shift_ref, out_ref):
    out_ref[...] = nn(left_ref[...], right_ref[...]) + shift_ref[...]


def mix_product(normed, mixed_full, shift):
    rows, width = normed.shape
    cols = shift.shape[1]
    block = rows // 3
    return call(
        mix_kernel,
        (normed, mixed_full, shift.reshape(1, cols)),
        (3,),
        [
            pl.BlockSpec((block, width), lambda i: (i, 0)),
            pl.BlockSpec((width, cols), lambda i: (0, 0)),
            pl.BlockSpec((1, cols), lambda i: (0, 0)),
        ],
        pl.BlockSpec((block, cols), lambda i: (i, 0)),
        jax.ShapeDtypeStruct((rows, cols), f32),
    )


def hide_kernel(left_ref, right_ref, shift_ref, out_ref, slope_ref):
    value = nn(left_ref[...], right_ref[...]) + shift_ref[...]
    inner = math.sqrt(2.0 / math.pi)
    square = value * value
    bend = jnp.tanh(inner * value * (1.0 + 0.044715 * square))
    half = 0.5 * (1.0 + bend)
    out_ref[...] = (value * half).astype(bf16)
    slope = 0.5 * value * (1.0 - bend * bend) * (inner * (1.0 + 3.0 * 0.044715 * square))
    slope_ref[...] = (half + slope).astype(slope_ref.dtype)


def hide_product(normed, up_full, shift):
    rows, width = normed.shape
    cols = up_full.shape[1]
    block = rows // 6
    out = pl.BlockSpec((block, cols), lambda i: (i, 0))
    return call(
        hide_kernel,
        (normed, up_full, shift.reshape(1, cols)),
        (6,),
        [
            pl.BlockSpec((block, width), lambda i: (i, 0)),
            pl.BlockSpec((width, cols), lambda i: (0, 0)),
            pl.BlockSpec((1, cols), lambda i: (0, 0)),
        ],
        [out, out],
        [jax.ShapeDtypeStruct((rows, cols), dtype) for dtype in (bf16, f32)],
    )


def out_kernel(first_ref, second_ref, dense_ref, down_ref, out_ref):
    value = nt(first_ref[...], dense_ref[...]) + nn(second_ref[...], down_ref[...])
    out_ref[...] = value.astype(out_ref.dtype)


def out_product(attended, hidden, mixed_full, down_full, half, dtype):
    rows, width = attended.shape[0] // 2, down_full.shape[1]
    heads = attended.shape[1]
    return call(
        out_kernel,
        (attended, hidden, mixed_full, down_full),
        (width // 512,),
        [
            pl.BlockSpec((rows, heads), lambda j: (half, 0)),
            pl.BlockSpec((rows, hidden.shape[1]), lambda j: (half, 0)),
            pl.BlockSpec((512, heads), lambda j: (j, 3)),
            pl.BlockSpec((hidden.shape[1], 512), lambda j: (0, j)),
        ],
        pl.BlockSpec((rows, 512), lambda j: (0, j)),
        jax.ShapeDtypeStruct((rows, width), dtype),
    )


def nn_kernel(left_ref, right_ref, out_ref):
    out_ref[...] = nn(left_ref[...], right_ref[...]).astype(out_ref.dtype)


def nt_scaled_kernel(left_ref, right_ref, slope_ref, out_ref):
    value = nt(left_ref[...], right_ref[...]) * slope_ref[...].astype(f32)
    out_ref[...] = value.astype(out_ref.dtype)


def attended_back(grad16, mixed_full, heads):
    rows, width = grad16.shape
    block = rows // 3
    return call(
        nn_kernel,
        (grad16, mixed_full),
        (3,),
        [
            pl.BlockSpec((block, width), lambda i: (i, 0)),
            pl.BlockSpec((width, heads), lambda i: (0, 3)),
        ],
        pl.BlockSpec((block, heads), lambda i: (i, 0)),
        jax.ShapeDtypeStruct((rows, heads), bf16),
    )


def hidden_back(grad16, down_full, slope):
    rows, width = grad16.shape
    cols = slope.shape[1]
    block = rows // 2
    spec = pl.BlockSpec((block, 256), lambda i, j: (i, j))
    return call(
        nt_scaled_kernel,
        (grad16, down_full, slope),
        (2, cols // 256),
        [
            pl.BlockSpec((block, width), lambda i, j: (i, 0)),
            pl.BlockSpec((256, width), lambda i, j: (j, 0)),
            spec,
        ],
        spec,
        jax.ShapeDtypeStruct((rows, cols), bf16),
    )


def both_kernel(first_ref, second_ref, proj_ref, up_ref, out_ref):
    value = nt(first_ref[...], proj_ref[...]) + nt(second_ref[...], up_ref[...])
    out_ref[...] = value.astype(out_ref.dtype)


def normed_back(mixed_grad, pre_grad, mixed_full, up_full, half, dtype):
    rows, width = mixed_grad.shape[0] // 2, up_full.shape[0]
    return call(
        both_kernel,
        (mixed_grad, pre_grad, mixed_full, up_full),
        (width // 512,),
        [
            pl.BlockSpec((rows, mixed_grad.shape[1]), lambda j: (half, 0)),
            pl.BlockSpec((rows, pre_grad.shape[1]), lambda j: (half, 0)),
            pl.BlockSpec((512, mixed_grad.shape[1]), lambda j: (j, 0)),
            pl.BlockSpec((512, up_full.shape[1]), lambda j: (j, 0)),
        ],
        pl.BlockSpec((rows, 512), lambda j: (0, j)),
        jax.ShapeDtypeStruct((rows, width), dtype),
    )


def in_grad_kernel(left_ref, right_ref, *refs):
    value = tn(left_ref[...], right_ref[...])
    for ref in refs[:-1]:
        value = value + ref[...].astype(f32)
    refs[-1][...] = value.astype(bf16)


def in_grad(part, k, normed, grad, *others):
    rows, cols = grad.shape
    block = min(part, 256)
    steps = part // block
    spec = pl.BlockSpec((block, cols), lambda i: (i, 0))
    return call(
        in_grad_kernel,
        (normed, grad, *others),
        (steps,),
        [
            pl.BlockSpec((rows, block), lambda i: (0, k * steps + i)),
            pl.BlockSpec((rows, cols), lambda i: (0, 0)),
        ]
        + [spec] * len(others),
        spec,
        jax.ShapeDtypeStruct((part, cols), bf16),
    )


def down_grad(part, k, hidden, grad, *others):
    rows, height = hidden.shape
    block = min(part, 256)
    steps = part // block
    spec = pl.BlockSpec((height, block), lambda j: (0, j))
    return call(
        in_grad_kernel,
        (hidden, grad, *others),
        (steps,),
        [
            pl.BlockSpec((rows, height), lambda j: (0, 0)),
            pl.BlockSpec((rows, block), lambda j: (0, k * steps + j)),
        ]
        + [spec] * len(others),
        spec,
        jax.ShapeDtypeStruct((height, part), bf16),
    )


def mixed_grad_kernel(normed_ref, mixed_ref, grad_ref, attended_ref, *refs):
    split = mixed_ref.shape[1]
    values = (tn(normed_ref[...], mixed_ref[...]), tn(grad_ref[...], attended_ref[...]))
    for value, cols in zip(values, (slice(0, split), slice(split, None))):
        for ref in refs[:-1]:
            value = value + ref[:, cols].astype(f32)
        refs[-1][:, cols] = value.astype(bf16)


def mixed_weight_grad(part, k, normed, mixed_grad, grad, attended, *others):
    rows, heads = attended.shape
    width = mixed_grad.shape[1] + heads
    block = min(part, 256)
    steps = part // block
    spec = pl.BlockSpec((block, width), lambda i: (i, 0))
    slice_spec = pl.BlockSpec((rows, block), lambda i: (0, k * steps + i))
    return call(
        mixed_grad_kernel,
        (normed, mixed_grad, grad, attended, *others),
        (steps,),
        [
            slice_spec,
            pl.BlockSpec(mixed_grad.shape, lambda i: (0, 0)),
            slice_spec,
            pl.BlockSpec(attended.shape, lambda i: (0, 0)),
        ]
        + [spec] * len(others),
        spec,
        jax.ShapeDtypeStruct((part, width), bf16),
    )


def halves_kernel(axis, mid_ref, keep_ref, other_ref, *refs):
    out_ref, size = refs[-1], keep_ref.shape[axis]
    for part_ref, half in ((keep_ref, mid_ref[0]), (other_ref, 1 - mid_ref[0])):
        at = pl.ds(pl.multiple_of(half * size, LANES), size)
        if axis:
            out_ref[0, :, at] = part_ref[...].astype(f32)
        else:
            out_ref[0, at, :] = part_ref[...].astype(f32)


def place_halves(keep, other, mid, axis, layer, layers, before=None):
    rows, cols = keep.shape
    shape = (rows, 2 * cols) if axis else (2 * rows, cols)
    if cols % LANES or (axis == 0 and rows % LANES):
        line = jnp.concatenate([pick(keep, other, mid), pick(other, keep, mid)], axis=axis)
        line = line.astype(f32)[None]
        if before is None:
            return jnp.concatenate([jnp.zeros_like(line)] * layer + [line], axis=0)
        return jnp.concatenate([line, before[1:]], axis=0)
    spec = pl.BlockSpec((rows, cols), lambda i, mid_ref: (0, 0))
    given = [] if before is None else [before]
    return pl.pallas_call(
        partial(halves_kernel, axis),
        grid_spec=pltpu.PrefetchScalarGridSpec(
            num_scalar_prefetch=1,
            grid=(1,),
            in_specs=[spec, spec] + [pl.BlockSpec(memory_space=pl.ANY)] * len(given),
            out_specs=pl.BlockSpec((1, *shape), lambda i, mid_ref: (layer, 0, 0)),
        ),
        out_shape=jax.ShapeDtypeStruct((layers, *shape), f32),
        input_output_aliases={3: 0} if given else {},
        compiler_params=pltpu.CompilerParams(vmem_limit_bytes=32 << 20),
        cost_estimate=pl.CostEstimate(flops=0, bytes_accessed=0, transcendentals=0),
    )(mid.reshape(1), keep, other, *given)


def last_kernel(
    order_ref, low_ref, core_ref, x_ref, mid_ref, old_ref, shift_ref, out_ref, held
):
    branch = low_ref[...] + core_ref[...].astype(f32) + x_ref[...].astype(f32)
    held[...] = old_ref[...] + (branch + mid_ref[...].astype(f32)) + shift_ref[...]
    order_kernel(True, order_ref, held, out_ref)


def last_stream(order, low, core, x_low, mid, old, shift):
    rows, width = old.shape
    if width // order.shape[0] % LANES:
        branch = low[:rows] + core[:rows].astype(f32) + x_low.astype(f32) + mid.astype(f32)
        return reorder(old + branch + shift, order, f32, True)
    steps = row_steps(rows)
    row_spec = pl.BlockSpec((rows // steps, width), lambda i, order_ref: (i, 0))
    return call(
        last_kernel,
        (order, low, core, x_low, mid, old, shift),
        (steps,),
        [row_spec] * 5 + [pl.BlockSpec((1, width), lambda i, order_ref: (0, 0))],
        row_spec,
        jax.ShapeDtypeStruct((rows, width), f32),
        [pltpu.VMEM((rows // steps, width), f32)],
        scalars=1,
    )


def halves(value, half, axis):
    size = value.shape[axis] // 2
    return lax.dynamic_slice_in_dim(value, half * size, size, axis)


class Small:
    def __init__(self, seq, mine, tensor, mid, beside):
        self.seq, self.tensor = seq, tensor
        self.mine, self.beside = seq.settle(
            lambda mine: pair_up(mine, swap(mine, "dp", MID), mid, 0), mine[None], beside=beside
        )

    def second(self):
        def step(mine):
            for bit in side_bits():
                mine = jnp.concatenate([mine, swap(mine, "dp", bit)], axis=0)
            return mine[None]

        self.mine = self.seq.settle(step, self.mine)

    def finish(self, unpack):
        def step(mine):
            for bit in (0, 1):
                mine = pair_up(mine, swap(mine, "tensor", bit), (self.tensor >> bit) & 1, 0)
            return unpack(jnp.swapaxes(mine, 0, 1))

        return self.seq.settle(step, self.mine)


class SmallSums:
    def __init__(self, seq, norm_grads, in_bgrads, mid):
        self.seq, self.mid = seq, mid
        self.norm_grads, self.in_bgrads = norm_grads, in_bgrads
        self.layers, self.kinds = len(norm_grads), 3
        self.sides = side_bits()

    def halve(self, sums, biases, axis, half, move):
        keep, sent = halves(sums, half, axis), halves(sums, 1 - half, axis)
        split = biases.shape[0]
        received = move(jnp.concatenate([biases, sent.reshape(-1)]))
        return keep + received[split:].reshape(keep.shape), received[:split]

    def side(self, s, sums, biases):
        sums, other = self.halve(
            sums, biases, 1, 0, lambda value: swap(value, "dp", self.sides[s])
        )
        return sums, biases + other

    def first(self):
        tensor = lax.axis_index("tensor")

        def step(*values):
            sums = jnp.stack([value[: self.kinds] for value in values[: self.layers]])
            biases = jnp.concatenate(values[self.layers :])
            shape = (self.layers * self.kinds, 1 << len(self.sides), 2, lax.axis_size("tensor"), -1)
            sums, biases = self.side(len(self.sides) - 1, sums.reshape(shape), biases)
            none = biases[:0]
            for bit in (1, 0):
                sums, _ = self.halve(
                    sums, none, 3, (tensor >> bit) & 1, lambda value: swap(value, "tensor", bit)
                )
            return sums, biases

        values = [value for pair in self.in_bgrads for value in pair]
        self.sums, self.biases = self.seq.settle(step, *self.norm_grads, *values)

    def second(self):
        def step(sums, biases):
            sums, other = self.halve(
                sums, biases, 2, self.mid, lambda value: swap(value, "dp", MID)
            )
            pair = (pick(biases, other, self.mid), pick(other, biases, self.mid))
            return sums, jnp.concatenate(pair)

        self.sums, self.biases = self.seq.settle(step, self.sums, self.biases)

    def finish(self):
        def step(sums, biases):
            for s in reversed(range(len(self.sides) - 1)):
                sums, biases = self.side(s, sums, biases)
            return sums, biases

        sums, biases = self.seq.settle(step, self.sums, self.biases)
        return sums.reshape(self.layers, self.kinds, -1), biases.reshape(2, -1)


def shards(
    tokens_in,
    lengths,
    norm_gain,
    norm_bias,
    proj_weight,
    proj_bias,
    dense_weight,
    dense_bias,
    up_weight,
    up_bias,
    down_weight,
    down_bias,
    cotangent,
):
    rows, width = tokens_in.shape
    layer_count = proj_weight.shape[0]
    n_dp = lax.axis_size("dp")
    dp = lax.axis_index("dp")
    tensor = lax.axis_index("tensor")
    mid = (dp >> MID) & 1
    order = slice_order()
    seq = Sequence(lengths[0, 0].astype(f32), lengths[0, 0] > 0)

    def take_mixed(l, half, weight=proj_weight):
        proj = halves(weight[l], half, 2).reshape(weight.shape[1], -1)
        return jnp.concatenate([proj, halves(dense_weight[l], half, 0).T], axis=1)

    def take_up(l, half, weight=up_weight):
        return halves(weight[l], half, 1)

    def take_down(l, half, weight=down_weight):
        return halves(weight[l], half, 0)

    takes = ((take_mixed, 0), (take_up, 0), (take_down, 1))

    def set_out(l, i):
        weight = (proj_weight, up_weight, down_weight)[i]
        part = seq.run(lambda value: takes[i][0](l, 1 - mid, value), weight, apart=True)
        return seq.start(part, "dp", MID)

    def paired(l, i, moving):
        return joined(l, i, seq.wait(moving))

    def joined(l, i, received):
        take, axis = takes[i]
        block = seq.run(
            lambda other: pair_up(take(l, mid), other, mid, axis), received, apart=True
        )
        return Spread(seq, block, axis)

    moving = [set_out(0, 0), set_out(0, 1)]
    cot = seq.run(lambda value: reorder(value, order, bf16), cotangent)
    whole_lens = lengths.reshape(-1).astype(f32)
    coarse = jnp.floor(whole_lens / 8.0)
    small = Small(
        seq,
        jnp.concatenate(
            [
                value.reshape(-1)
                for value in (norm_gain, norm_bias, dense_bias, down_bias, proj_bias, up_bias)
            ]
            + [coarse.astype(bf16), (whole_lens - 8.0 * coarse).astype(bf16)]
        ),
        tensor,
        mid,
        lambda: swap(cot, "tensor", 1),
    )
    cot_across = small.beside
    small.second()
    m0 = paired(0, 0, moving[0])
    u0 = paired(0, 1, moving[1])
    m0.near()
    m0.far()
    each, proj_each, up_each = norm_gain.shape[1], proj_bias.shape[3], up_bias.shape[2]

    def unpack(everyone):
        pair_lens = lax.dynamic_index_in_dim(everyone[:2, :, -4:], tensor, 1, keepdims=False)
        pair_lens = pair_lens.astype(f32)
        pair_lens = (pair_lens[:, :2] * 8.0 + pair_lens[:, 2:]).astype(jnp.int32)
        lens = pick(pair_lens, pair_lens[::-1], mid)
        everyone = everyone[:, :, :-4]
        at = 4 * layer_count * each
        norm_parts = everyone[:, :, :at].reshape(n_dp, -1, 4 * layer_count, each)
        norm_parts = jnp.transpose(norm_parts, (2, 0, 1, 3)).reshape(4, layer_count, width)
        norm_parts = norm_parts.astype(f32)
        same_heads = lax.dynamic_index_in_dim(everyone[:, :, at:], tensor, 1, keepdims=False)
        same_heads = halves(same_heads[slice_places()], mid, 0).astype(f32)
        proj_at = layer_count * 3 * proj_each
        proj_shift = jnp.transpose(
            same_heads[:, :proj_at].reshape(-1, layer_count * 3, proj_each), (1, 0, 2)
        ).reshape(layer_count, -1)
        up_shift = jnp.transpose(
            same_heads[:, proj_at:].reshape(-1, layer_count, up_each), (1, 0, 2)
        ).reshape(layer_count, -1)
        gains, biases = norm_parts[0], norm_parts[1]
        shifts = norm_parts[2] + norm_parts[3]
        scalars = jnp.concatenate([lens.reshape(-1), tensor[None].astype(jnp.int32)])
        lines = [value[l] for value in (gains, biases, shifts) for l in range(layer_count)]
        lines += [value[l] for value in (proj_shift, up_shift) for l in range(layer_count)]
        return [line[None] for line in lines], lens, scalars.astype(jnp.int32)

    lines, lens, scalars = small.finish(unpack)
    gains, biases, out_shifts, proj_shift, up_shift = (
        lines[i * layer_count : (i + 1) * layer_count] for i in range(5)
    )

    def mix(l, normed, proj_full):
        return seq.run(mix_product, normed, proj_full, proj_shift[l])

    def attend(mixed):
        return seq.run(lambda value: attention_forward(value, tables, scalars, rows), mixed)

    def hide(l, normed, up_full):
        return seq.run(hide_product, normed, up_full, up_shift[l])

    def make_tables():
        return rotary_tables(jax.vmap(partial(layout, total=4 * rows, block=BLOCK))(lens))

    stream, own = seq.run(
        lambda value: norm_first(value, order, gains[0], biases[0]), tokens_in
    )
    tokens = Gather(seq, own, make_tables)
    token_parts, tables = tokens.parts, tokens.beside
    m0.near_wait()
    m0.far_wait()
    u0.far()
    m0.last()
    u0.near()
    sent = seq.run(lambda value: take_down(0, 1 - mid, value), down_weight, apart=True)

    def with_half(sent, own, mid, across, core_own, core_across):
        received, both = swap(sent, "dp", MID), swap(mid, "tensor", 1)
        received, both, mid = lax.optimization_barrier((received, both, mid))
        core_mid, core_both = swap(mid, "tensor", 0), swap(both, "tensor", 0)
        parts = (own, mid, across, both, core_own, core_mid, core_across, core_both)
        return received, assemble(parts, 0)

    received, normed = seq.settle(with_half, sent, *token_parts)
    d0 = joined(0, 2, received)
    u0.far_wait()
    seq.tick(3)
    u0.near_wait()
    m0.last_wait()
    u0.last()
    d0.far()
    mixed_full = m0.whole()
    mixed = mix(0, normed, mixed_full)
    d0.near()
    moving = [set_out(1, 0), set_out(1, 1)]
    attended, kept, sums = attend(mixed)
    u0.last_wait()
    up_full = u0.whole()
    hidden, slope = hide(0, normed, up_full)
    m1 = paired(1, 0, moving[0])
    u1 = paired(1, 1, moving[1])
    d0.far_wait()
    seq.tick(3)
    d0.near_wait()
    d0.last()
    cot_mid = seq.swap(cot, "dp", MID)
    m1.far()
    d0.last_wait()
    down_full = d0.whole()
    m1.near()
    moving = [set_out(1, 2)]
    saved = [(normed, kept, sums, slope, attended, hidden)]
    weights = [(mixed_full, up_full, down_full)]
    streams = [stream]

    branch = Scatter(seq, out_product, (attended, hidden, mixed_full, down_full), rows)
    branch.begin()
    branch.second()
    d1 = paired(1, 2, moving[0])
    m1.far_wait()
    seq.tick(2)
    m1.near_wait()
    m1.last()
    branch.third()
    u1.near()
    u1.far()
    stream, own = branch.finish(
        norm_after, stream, out_shifts[0], gains[1], biases[1]
    )
    streams.append(stream)

    def with_cores(mine, mid, cot, across):
        parts, both = gather_start_beside(mine, mid)
        *parts, cot, across = lax.optimization_barrier((*parts, cot, across))
        return parts, both, swap(cot, "tensor", 0), swap(across, "tensor", 0)

    parts, cot_both, cot_core_own, cot_core_across = seq.settle(
        with_cores, own, cot_mid, cot, cot_across
    )
    m1.last_wait()
    u1.near_wait()
    u1.far_wait()
    d1.near()
    d1.far()
    u1.last()
    grad16, normed, mixed_full = seq.settle(
        lambda *values: gather_finish_beside(values[:5], values[5:], m1.plain),
        *parts,
        cot,
        cot_mid,
        cot_across,
        cot_both,
        cot_core_own,
        cot_core_across,
    )
    mixed = mix(1, normed, mixed_full)
    d1.near_wait()
    u1.last_wait()
    attended, kept, sums = attend(mixed)
    up_full = u1.whole()
    hidden, slope = hide(1, normed, up_full)
    d1.far_wait()
    d1.last()
    saved.append((normed, kept, sums, slope, attended, hidden))
    weights.append((mixed_full, up_full, None))

    heads_width = attended.shape[1]
    parts = 1 << len(side_bits())
    norm_grads, in_bgrads = [None] * layer_count, [None] * layer_count

    part = width // parts

    def down_grads(l, grad16):
        return Reduce(seq, partial(down_grad, part), saved[l][5], grad16)

    def up_grads(l, grad):
        return Reduce(seq, partial(in_grad, part), saved[l][0], grad)

    def mixed_grads(l, grad, grad16):
        values = saved[l][0], grad, grad16, saved[l][4]
        return Reduce(seq, partial(mixed_weight_grad, part), *values)

    def attend_back(l, grad16):
        kept, sums = saved[l][1:3]
        mixed_full = weights[l][0]

        def step(value):
            grad = attended_back(value, mixed_full, heads_width)
            return attention_backward(kept, sums, grad, tables, scalars, rows)

        return seq.run(step, grad16)

    def hide_back(l, grad16):
        slope, down_full = saved[l][3], weights[l][2]
        return seq.run(lambda value: hidden_back(value, down_full, slope), grad16)

    def rows_back(l, mixed_grad, pre_grad):
        return Scatter(seq, normed_back, (mixed_grad, pre_grad, *weights[l][:2]), rows)

    def bias_back(mixed_grad, pre_grad):
        return jnp.sum(mixed_grad, axis=0, dtype=f32), jnp.sum(pre_grad, axis=0, dtype=f32)

    def own_start(total, axis):
        return halves(total, mid, axis), seq.start(halves(total, 1 - mid, axis), "dp", MID)

    def own_wait(pair):
        keep, moving = pair
        received = seq.wait(moving)
        return pick(keep, received, mid).astype(f32), pick(received, keep, mid).astype(f32)

    first, second = 0, 1
    early = len(side_bits()) == 2

    def send(reduce, which):
        reduce.send(reduce.near(which))

    def arrive(reduce, which):
        reduce.wait(reduce.near(which))

    def rest(reduce):
        for which in (first, second):
            reduce.make(reduce.near(which))
            send(reduce, which)
            arrive(reduce, which)
        reduce.make_far()
        reduce.send_far()
        reduce.wait_far()
        reduce.finish()

    down2 = down_grads(1, grad16)
    down2.make(down2.near(first))
    if early:
        send(down2, first)
    mixed_grad = attend_back(1, grad16)
    d1.last_wait()
    weights[1] = (mixed_full, up_full, d1.whole())
    if early:
        down2.make(down2.near(second))
        send(down2, second)
    pre_grad = hide_back(1, grad16)
    up2, mix2 = up_grads(1, pre_grad), mixed_grads(1, mixed_grad, grad16)
    back = rows_back(1, mixed_grad, pre_grad)
    back.begin()
    branch = Scatter(seq, out_product, (attended, hidden, *weights[1][::2]), rows)
    if early:
        arrive(down2, first)
        up2.make(up2.near(first))
        send(up2, first)
    made = back.second(
        lambda: (
            down2.plain(down2.far()) if early else (),
            up2.plain(up2.near(second)),
            mix2.plain(mix2.near(first)),
            mix2.plain(mix2.near(second)),
            bias_back(mixed_grad, pre_grad),
        )
    )
    in_bgrads[1] = made[4]
    if early:
        down2.take(down2.far(), made[0])
        up2.take(up2.near(second), made[1])
        mix2.take(mix2.near(first), made[2])
        mix2.take(mix2.near(second), made[3])
        arrive(down2, second)
        seq.tick(4)
        arrive(up2, first)
        send(up2, second)
    made = back.third(lambda: (up2.plain(up2.far()) if early else (), branch.plain()))
    branch.take(made[1])
    norm_grads[1], grad_stream, own = back.finish(
        norm_before, cot, streams[1], gains[1]
    )
    if early:
        up2.take(up2.far(), made[0])
        arrive(up2, second)
        send(mix2, first)
        down2.send_far()
    (branch.later, branch.x_high), coming = seq.settle(
        lambda own, low, core: gather_start_with(own, low, core, branch.sent_across),
        own,
        branch.low_part,
        branch.core,
    )
    if early:
        arrive(mix2, first)
        send(mix2, second)
        up2.send_far()
        grad16, made = seq.settle(gather_finish, *coming, beside=lambda: mix2.plain(mix2.far()))
        mix2.take(mix2.far(), made)
        mix2.send_far()
        down2.wait_far()
    else:
        grad16 = seq.settle(gather_finish, *coming)
        rest(down2)
        rest(up2)
        rest(mix2)

    results = {}

    def own_start(total, axis):
        keep, sent = seq.run(
            lambda value: (halves(value, mid, axis), halves(value, 1 - mid, axis)),
            total,
            apart=True,
        )
        return keep, seq.start(sent, "dp", MID)

    def own_finish(l, name, axis, pair):
        keep, moving = pair
        received = seq.wait(moving)
        before = results.get(name)
        given = () if before is None else (before,)
        results[name] = seq.run(
            lambda keep, other, *given: place_halves(
                keep, other, mid, axis, l, layer_count, *given
            ),
            keep,
            received,
            *given,
        )

    def mixed_finish(pair):
        keep, moving = pair
        received = seq.wait(moving)
        cols = 3 * heads_width

        def step(keep, other):
            pair = [pick(keep, other, mid).astype(f32), pick(other, keep, mid).astype(f32)]
            proj = [value[:, :cols].reshape(value.shape[0], 3, -1) for value in pair]
            dense = [value[:, cols:].T for value in pair]
            return jnp.concatenate(proj, axis=2), jnp.concatenate(dense, axis=0)

        return seq.run(step, keep, received, apart=True)

    down1 = down_grads(0, grad16)
    down1.make(down1.near(first))
    if early:
        send(down1, first)
        down2.make([0])
    sent = seq.run(branch.next, branch.low_part, branch.core, branch.x_high, apart=True)
    branch_mid = seq.start(sent, "dp", MID)
    mixed_grad = attend_back(0, grad16)
    if early:
        up2.wait_far()
        arrive(mix2, second)
    pre_grad = hide_back(0, grad16)
    up1, mix1 = up_grads(0, pre_grad), mixed_grads(0, mixed_grad, grad16)
    up1.make(up1.near(first))
    if early:
        send(up1, first)
        up2.make([0])
    branch.mid = seq.wait(branch_mid)
    if early:
        mix2.wait_far()
        seq.tick(2)
        arrive(down1, first)
        down1.make_far()
        down1.send_far()
    branch_low = seq.start(branch.later, "tensor", 1)
    up2_pair = own_start(up2.blocks[0], 0)
    up1.make(up1.near(second))
    mix1.make(mix1.near(first))
    down1.make(down1.near(second))
    if early:
        arrive(up1, first)
        up1.make_far()
        send(down1, second)
    branch.x_low = seq.wait(branch_low)
    down2_pair = own_start(down2.blocks[0], 1)
    back = rows_back(0, mixed_grad, pre_grad)
    back.begin()
    if early:
        down1.wait_far()
        up1.send_far()
    own_finish(1, "up", 1, up2_pair)
    if early:
        send(mix1, first)
    made = back.second(
        lambda: (
            mix1.plain(mix1.near(second)),
            bias_back(mixed_grad, pre_grad),
        )
    )
    mix1.take(mix1.near(second), made[0])
    in_bgrads[0] = made[1]
    own_finish(1, "down", 0, down2_pair)
    if early:
        seq.tick(2)
        arrive(down1, second)
        seq.tick(4)
        arrive(mix1, first)
        send(up1, second)
        send(mix1, second)
    made = back.third(
        lambda: (mix1.plain(mix1.far()), down1.plain([0]), mix2.plain([0])) if early else ()
    )
    norm_grads[0], grad_stream, own = back.finish(
        norm_before, grad_stream, streams[0], gains[0]
    )
    if early:
        mix1.take(mix1.far(), made[0])
        down1.take([0], made[1])
        mix2.take([0], made[2])
        up1.wait_far()
        seq.tick(7)
        arrive(up1, second)
        arrive(mix1, second)
        mix1.send_far()
    else:
        rest(down1)
        rest(up1)
        rest(mix1)
    mix2_pair = own_start(mix2.blocks[0], 0)
    down1_pair = own_start(down1.blocks[0], 1)
    if early:
        up1.make([0])
    up1_pair = own_start(up1.blocks[0], 0)
    small_sums = SmallSums(seq, norm_grads, in_bgrads, mid)
    small_sums.first()
    activations = branch.finish(partial(last_stream, order), streams[1], out_shifts[1])
    input_grad = seq.run(lambda value: reorder(value, order, f32, True), grad_stream)
    mix2_own = mixed_finish(mix2_pair)
    own_finish(0, "down", 0, down1_pair)
    small_sums.second()
    if early:
        mix1.wait_far()
        mix1.make([0])
    mix1_pair = own_start(mix1.blocks[0], 0)
    own_finish(0, "up", 1, up1_pair)
    seq.tick(6)
    norm_owned, bias_both = small_sums.finish()
    mix1_own = mixed_finish(mix1_pair)
    bias_both = bias_both + 0.0 * seq.scalar
    per_layer = bias_both.shape[1] // layer_count
    bias_both = bias_both.reshape(2, layer_count, per_layer)
    proj_b = jnp.transpose(
        bias_both[:, :, : 3 * heads_width].reshape(2, layer_count, 3, heads_width), (1, 2, 0, 3)
    ).reshape(layer_count, 3, 1, 2 * heads_width)
    up_b = jnp.transpose(bias_both[:, :, 3 * heads_width :], (1, 0, 2)).reshape(layer_count, 1, -1)
    return (
        activations,
        input_grad,
        norm_owned[:, 0],
        norm_owned[:, 1],
        jnp.stack([mix1_own[0], mix2_own[0]]),
        lax.dynamic_slice_in_dim(proj_b, dp * proj_each, proj_each, 3),
        jnp.stack([mix1_own[1], mix2_own[1]]),
        norm_owned[:, 2],
        results["up"],
        lax.dynamic_slice_in_dim(up_b, dp * up_each, up_each, 2),
        results["down"],
        norm_owned[:, 2],
    )


def solution(mesh):
    in_specs = (
        P(("dp", "tensor"), None),
        P("dp", None),
        P(None, ("dp", "tensor")),
        P(None, ("dp", "tensor")),
        P(None, "dp", None, "tensor"),
        P(None, None, "tensor", "dp"),
        P(None, "tensor", "dp"),
        P(None, ("dp", "tensor")),
        P(None, "dp", "tensor"),
        P(None, "tensor", "dp"),
        P(None, "tensor", "dp"),
        P(None, ("dp", "tensor")),
        P(("dp", "tensor"), None),
    )
    out_specs = (
        P(("dp", "tensor"), None),
        P(("dp", "tensor"), None),
        P(None, ("dp", "tensor")),
        P(None, ("dp", "tensor")),
        P(None, "dp", None, "tensor"),
        P(None, None, "tensor", "dp"),
        P(None, "tensor", "dp"),
        P(None, ("dp", "tensor")),
        P(None, "dp", "tensor"),
        P(None, "tensor", "dp"),
        P(None, "tensor", "dp"),
        P(None, ("dp", "tensor")),
    )
    return jax.shard_map(shards, mesh=mesh, in_specs=in_specs, out_specs=out_specs, check_vma=False)
```

```python
from functools import partial
import math

import jax
import jax.numpy as jnp
from jax import lax
from jax.experimental import pallas as pl
from jax.experimental.pallas import tpu as pltpu
from jax.sharding import PartitionSpec as P

HEAD_DIM = 64
ROT = 32
BLOCK = 128
LANES = 128
TILE = 256
MID = 1

TICK = 1_200_000_000

neg_large = -1e30
f32 = jnp.float32
bf16 = jnp.bfloat16


def swap(value, axis, bit):
    size = lax.axis_size(axis)
    return lax.ppermute(value, axis, [(i, i ^ (1 << bit)) for i in range(size)])


def tick_kernel(in_ref, out_ref):
    out_ref[0, 0] = in_ref[0, 0]


def tick(scalar, count):
    spec = pl.BlockSpec(memory_space=pltpu.SMEM)
    result = pl.pallas_call(
        tick_kernel,
        in_specs=[spec],
        out_specs=spec,
        out_shape=jax.ShapeDtypeStruct((1, 1), f32),
        cost_estimate=pl.CostEstimate(flops=count * TICK, bytes_accessed=0, transcendentals=0),
    )(scalar.reshape(1, 1))
    return result[0, 0]


class Sequence:
    def __init__(self, scalar, always):
        self.scalar = scalar
        self.always = always

    def gate(self, *values):
        *values, self.scalar = lax.optimization_barrier((*values, self.scalar))
        return values

    def run(self, step, *values, apart=False):
        values = self.gate(*values)
        if apart:
            shapes = jax.eval_shape(step, *values)

            def never(*others):
                return jax.tree.map(lambda shape: jnp.zeros(shape.shape, shape.dtype), shapes)

            result = lax.cond(self.always, step, never, *values)
        else:
            result = step(*values)
        leaves, tree = jax.tree.flatten(result)
        return jax.tree.unflatten(tree, self.gate(*leaves))

    def start(self, value, axis, bit):
        (value,) = self.gate(value)
        return swap(value, axis, bit)

    def wait(self, value):
        (value,) = self.gate(value)
        return value

    def settle(self, step, *values, beside=None):
        def both(*moved):
            return (step(*moved), beside()) if beside else step(*moved)

        return self.run(both, *values, apart=True)

    def tick(self, count):
        self.scalar = tick(self.scalar, count)

    def swap(self, value, axis, bit):
        return self.settle(lambda moved: swap(moved, axis, bit), value)


def side_bits():
    count = (lax.axis_size("dp") - 1).bit_length()
    return [bit for bit in range(count - 1, MID, -1)] + [0]


def slice_order():
    sides = side_bits()
    me = lax.axis_index("dp")
    base = me - (((me >> MID) & 1) << MID)
    order = []
    for k in range(1 << len(sides)):
        mask = sum(((k >> s) & 1) << bit for s, bit in enumerate(sides))
        for mid in range(2):
            order.append((base ^ mask) | (mid << MID))
    return jnp.stack(order).astype(jnp.int32)


def slice_places():
    sides = side_bits()
    every = jnp.arange(lax.axis_size("dp"), dtype=jnp.int32)
    apart = every ^ lax.axis_index("dp")
    place = (every >> MID) & 1
    for s, bit in enumerate(sides):
        place = place + (((apart >> bit) & 1) << (s + 1))
    return place


def pick(pair_first, pair_second, bit):
    return jnp.where(bit == 0, pair_first, pair_second)


def pair_up(keep, received, bit, axis):
    return jnp.concatenate(
        [pick(keep, received, bit), pick(received, keep, bit)], axis=axis
    )


class Spread:
    def __init__(self, seq, block, axis):
        self.seq, self.axis = seq, axis
        self.sides = side_bits()
        self.far_count = 1 << (len(self.sides) - 1)
        self.blocks = {0: block}

    def move(self, ks):
        for k in ks:
            if k != ks[0]:
                self.arrived(ks)
            s = k.bit_length() - 1
            self.blocks[k] = self.seq.start(self.blocks[k - (1 << s)], "dp", self.sides[s])

    def arrived(self, ks):
        last = max(k for k in ks if k in self.blocks)
        self.blocks[last] = self.seq.wait(self.blocks[last])

    def far(self):
        self.move(range(1, self.far_count))

    def far_wait(self):
        self.arrived(range(1, self.far_count))

    def near(self):
        self.move([self.far_count])

    def near_wait(self):
        self.arrived([self.far_count])

    def last(self):
        self.move(range(self.far_count + 1, 2 * self.far_count))

    def last_wait(self):
        self.arrived(range(self.far_count + 1, 2 * self.far_count))

    def plain(self, window=None):
        parts = [self.blocks[k] for k in sorted(self.blocks)]
        return assemble(parts, self.axis, window)

    def whole(self, window=None):
        parts = [self.blocks[k] for k in sorted(self.blocks)]
        return self.seq.run(lambda *values: assemble(values, self.axis, window), *parts)


class Reduce:
    def __init__(self, seq, product, *operands):
        self.seq, self.product, self.operands = seq, product, operands
        self.sides = side_bits()
        self.count = 1 << len(self.sides)
        self.blocks = {}
        self.arrived = [[] for _ in range(self.count)]
        self.moving = {}

    def make(self, ks):
        for k in ks:
            values = (*self.operands, *self.arrived[k])
            self.blocks[k] = self.seq.run(partial(self.product, k), *values)

    def plain(self, ks):
        return [self.product(k, *self.operands, *self.arrived[k]) for k in ks]

    def take(self, ks, made):
        self.blocks.update(zip(ks, made))

    def send(self, ks):
        for i, k in enumerate(ks):
            if i:
                self.wait([ks[i - 1]])
            s = k.bit_length() - 1
            self.moving[k] = self.seq.start(self.blocks[k], "dp", self.sides[s])

    def wait(self, ks):
        k = ks[-1]
        s = k.bit_length() - 1
        self.arrived[k - (1 << s)].append(self.seq.wait(self.moving[k]))

    def near(self, half):
        whole = list(reversed(range(self.count // 2, self.count)))
        middle = len(whole) // 2
        return whole[middle:] if half else whole[:middle]

    def far(self):
        return list(reversed(range(1, self.count // 2)))

    def make_far(self, near_done=True):
        ks = self.far()
        if ks[-1] in self.blocks or not (near_done or len(ks) == 1):
            return
        for k in ks[:-1]:
            self.make([k])
            self.send([k])
            self.wait([k])
        self.make(ks[-1:])

    def send_far(self):
        self.send(self.far()[-1:])

    def wait_far(self):
        self.wait(self.far()[-1:])

    def finish(self):
        self.make([0])
        return self.blocks[0]


def gather_start(own):
    mid, across = swap(own, "dp", MID), swap(own, "tensor", 1)
    own, mid, across = lax.optimization_barrier((own, mid, across))
    return own, mid, across, swap(own, "tensor", 0), swap(across, "tensor", 0)


def gather_start_with(own, low, core, sent):
    mid, across = swap(own, "dp", MID), swap(own, "tensor", 1)
    low, core, across = lax.optimization_barrier((low, core, across))
    later, x_high = sent(low, core)
    own, mid, across, x_high = lax.optimization_barrier((own, mid, across, x_high))
    core_parts = swap(own, "tensor", 0), swap(across, "tensor", 0)
    return (later, x_high), (own, mid, across, *core_parts)


def gather_finish(own, mid, across, core_own, core_across):
    both, core_mid = swap(mid, "tensor", 1), swap(mid, "tensor", 0)
    core_both = swap(both, "tensor", 0)
    parts = (own, mid, across, both, core_own, core_mid, core_across, core_both)
    return assemble(parts, 0)


class Gather:
    def __init__(self, seq, own, beside=None):
        self.seq = seq
        self.parts = seq.settle(gather_start, own, beside=beside)
        if beside:
            self.parts, self.beside = self.parts

    def finish(self, beside=None):
        return self.seq.settle(gather_finish, *self.parts, beside=beside)


def gather_start_beside(mine, mid):
    own, near, across = mine, swap(mine, "dp", MID), swap(mine, "tensor", 1)
    across, mid = lax.optimization_barrier((across, mid))
    both = swap(mid, "tensor", 1)
    own, near, across, both = lax.optimization_barrier((own, near, across, both))
    return (own, near, across, swap(own, "tensor", 0), swap(across, "tensor", 0)), both


def gather_finish_beside(parts, other, beside):
    own, mid, across, core_own, core_across = parts
    other_own, other_mid, other_across, other_both, other_core_own, other_core_across = other
    both, core_mid = swap(mid, "tensor", 1), swap(mid, "tensor", 0)
    core_mid, other_mid = lax.optimization_barrier((core_mid, other_mid))
    other_core_mid = swap(other_mid, "tensor", 0)
    other_core_mid, other_both = lax.optimization_barrier((other_core_mid, other_both))
    other_core_both = swap(other_both, "tensor", 0)
    others = (other_own, other_mid, other_across, other_both)
    others += (other_core_own, other_core_mid, other_core_across, other_core_both)
    whole, made = assemble(others, 0), beside()
    both, whole, made = lax.optimization_barrier((both, whole, made))
    core_both = swap(both, "tensor", 0)
    mine = (own, mid, across, both, core_own, core_mid, core_across, core_both)
    return whole, assemble(mine, 0), made


class Scatter:
    def __init__(self, seq, product, operands, rows):
        self.seq, self.product, self.operands, self.rows = seq, product, operands, rows

    def begin(self, beside=tuple):
        high = self.seq.run(lambda *values: self.product(*values, 1, bf16), *self.operands)
        self.core, (self.low_part, made) = self.seq.settle(
            lambda high: swap(high, "tensor", 0),
            high,
            beside=lambda: (self.product(*self.operands, 0, f32), beside()),
        )
        return made

    def plain(self):
        high = self.product(*self.operands, 1, bf16)
        return self.product(*self.operands, 0, f32), swap(high, "tensor", 0)

    def take(self, made):
        self.low_part, self.core = made

    def chunk(self, low, core, k, *others):
        at = slice(k * self.rows, (k + 1) * self.rows)
        part = low[at] + core[at].astype(f32)
        for value in others:
            part = part + value.astype(f32)
        return part

    def sent(self, low, core):
        return tuple(self.chunk(low, core, k).astype(bf16) for k in (2, 3))

    def next(self, low, core, other):
        return self.chunk(low, core, 1, other).astype(bf16)

    def second(self, beside=None):
        def step(low, core):
            later, first = self.sent(low, core)
            return later, swap(first, "tensor", 1)

        moved = self.seq.settle(step, self.low_part, self.core, beside=beside)
        if beside:
            moved, made = moved
        self.later, self.x_high = moved
        return made if beside else None

    def third_step(self, low, core, other, later):
        return swap(self.next(low, core, other), "dp", MID), swap(later, "tensor", 1)

    def third(self, beside=None):
        values = (self.low_part, self.core, self.x_high, self.later)
        moved = self.seq.settle(self.third_step, *values, beside=beside)
        if beside:
            moved, made = moved
        self.mid, self.x_low = moved
        return made if beside else None

    def sent_across(self, low, core):
        later, first = self.sent(low, core)
        return later, swap(first, "tensor", 1)

    def finish(self, step, *others):
        return self.seq.run(step, self.low_part, self.core, self.x_low, self.mid, *others)


def order_kernel(back, order_ref, in_ref, out_ref):
    count = order_ref.shape[0]
    part = in_ref.shape[1] // count
    for i in range(count):
        there = pl.ds(pl.multiple_of(order_ref[i] * part, LANES), part)
        here = slice(i * part, (i + 1) * part)
        if back:
            out_ref[:, there] = in_ref[:, here].astype(out_ref.dtype)
        else:
            out_ref[:, here] = in_ref[:, there].astype(out_ref.dtype)


def reorder(value, order, dtype, back=False):
    rows, width = value.shape
    count = order.shape[0]
    part = width // count
    if part % LANES:
        blocks = value.reshape(rows, count, part)
        index = slice_places() if back else order
        return jnp.take(blocks, index, axis=1).reshape(rows, width).astype(dtype)
    spec = pl.BlockSpec((rows, width), lambda i, order_ref: (0, 0))
    return pl.pallas_call(
        partial(order_kernel, back),
        grid_spec=pltpu.PrefetchScalarGridSpec(
            num_scalar_prefetch=1, grid=(1,), in_specs=[spec], out_specs=spec
        ),
        out_shape=jax.ShapeDtypeStruct((rows, width), dtype),
    )(order, value)


def assemble_kernel(axis, window, *refs):
    parts, out_ref, held, in_sems, out_sems = refs[:-4], refs[-4], refs[-3], refs[-2], refs[-1]
    copies, at = [], 0
    for i, part in enumerate(parts):
        size = window[1] if axis else part.shape[0]
        where = (pl.ds(at, size),) if axis == 0 else (slice(None), pl.ds(at, size))
        copies.append(
            (
                pltpu.make_async_copy(
                    part.at[:, pl.ds(*window)], held.at[where], in_sems.at[i]
                ),
                pltpu.make_async_copy(held.at[where], out_ref.at[where], out_sems.at[i]),
            )
        )
        at += size
    for come, go in copies:
        come.start()
    for come, go in copies:
        come.wait()
        go.start()
    for come, go in copies:
        go.wait()


def assemble(parts, axis, window=None):
    rows, width = parts[0].shape
    window = window or (0, width)
    count = len(parts)
    shape = (rows * count, window[1]) if axis == 0 else (rows, window[1] * count)
    if window[1] % LANES or window[0] % LANES:
        return jnp.concatenate(
            [part[:, window[0] : window[0] + window[1]] for part in parts], axis=axis
        )
    return pl.pallas_call(
        partial(assemble_kernel, axis, window),
        in_specs=[pl.BlockSpec(memory_space=pl.ANY)] * count,
        out_specs=pl.BlockSpec(memory_space=pl.ANY),
        out_shape=jax.ShapeDtypeStruct(shape, parts[0].dtype),
        scratch_shapes=[
            pltpu.VMEM(shape, parts[0].dtype),
            pltpu.SemaphoreType.DMA((count,)),
            pltpu.SemaphoreType.DMA((count,)),
        ],
        compiler_params=pltpu.CompilerParams(vmem_limit_bytes=16 << 20),
        cost_estimate=pl.CostEstimate(flops=0, bytes_accessed=0, transcendentals=0),
    )(*parts)


def norm_kernel(
    low_ref, core_ref, x_ref, mid_ref, old_ref, shift_ref, gain_ref, bias_ref, stream_ref, out_ref
):
    branch = low_ref[...] + core_ref[...].astype(f32) + x_ref[...].astype(f32)
    stream = old_ref[...] + (branch + mid_ref[...].astype(f32)) + shift_ref[...]
    stream_ref[...] = stream
    centre = stream - jnp.mean(stream, axis=1, keepdims=True)
    spread_of = jnp.mean(centre * centre, axis=1, keepdims=True)
    out_ref[...] = (
        centre * lax.rsqrt(spread_of + 1e-05) * gain_ref[...] + bias_ref[...]
    ).astype(bf16)


def norm_back_kernel(
    low_ref, core_ref, x_ref, mid_ref, grad_ref, old_ref, gain_ref, sums_ref, grad_out_ref, out_ref
):
    normed_grad = low_ref[...] + core_ref[...].astype(f32) + x_ref[...].astype(f32)
    normed_grad = normed_grad + mid_ref[...].astype(f32)
    grad, old = grad_ref[...].astype(f32), old_ref[...]
    centre = old - jnp.mean(old, axis=1, keepdims=True)
    root = lax.rsqrt(jnp.mean(centre * centre, axis=1, keepdims=True) + 1e-05)
    hat = centre * root
    scaled = normed_grad * gain_ref[...]
    back = scaled - jnp.mean(scaled, axis=1, keepdims=True)
    back = root * (back - hat * jnp.mean(scaled * hat, axis=1, keepdims=True))
    result = grad + back
    grad_out_ref[...] = result
    out_ref[...] = result.astype(bf16)

    @pl.when(pl.program_id(0) == 0)
    def clear():
        sums_ref[...] = jnp.zeros_like(sums_ref)

    sums_ref[0:1, :] += jnp.sum(normed_grad * hat, axis=0, keepdims=True)
    sums_ref[1:2, :] += jnp.sum(normed_grad, axis=0, keepdims=True)
    sums_ref[2:3, :] += jnp.sum(grad, axis=0, keepdims=True)


def norm_first_kernel(order_ref, in_ref, gain_ref, bias_ref, stream_ref, out_ref):
    order_kernel(False, order_ref, in_ref, stream_ref)
    stream = stream_ref[...]
    centre = stream - jnp.mean(stream, axis=1, keepdims=True)
    spread_of = jnp.mean(centre * centre, axis=1, keepdims=True)
    out_ref[...] = (
        centre * lax.rsqrt(spread_of + 1e-05) * gain_ref[...] + bias_ref[...]
    ).astype(bf16)


def norm_first(value, order, gain, bias):
    rows, width = value.shape
    if width // order.shape[0] % LANES:
        stream = reorder(value, order, f32)
        centre = stream - jnp.mean(stream, axis=1, keepdims=True)
        spread_of = jnp.mean(centre * centre, axis=1, keepdims=True)
        return stream, (centre * lax.rsqrt(spread_of + 1e-05) * gain + bias).astype(bf16)
    steps = row_steps(rows)
    row_spec = pl.BlockSpec((rows // steps, width), lambda i, order_ref: (i, 0))
    line_spec = pl.BlockSpec((1, width), lambda i, order_ref: (0, 0))
    return call(
        norm_first_kernel,
        (order, value, gain.reshape(1, width), bias.reshape(1, width)),
        (steps,),
        [row_spec, line_spec, line_spec],
        [row_spec, row_spec],
        [jax.ShapeDtypeStruct((rows, width), dtype) for dtype in (f32, bf16)],
        scalars=1,
    )


def row_steps(rows):
    return rows // 48 if rows % 48 == 0 else 1


def norm_call(kernel, rows, width, row_values, line_values, out_shapes):
    steps = row_steps(rows)
    row_spec = pl.BlockSpec((rows // steps, width), lambda i: (i, 0))
    line_spec = pl.BlockSpec((1, width), lambda i: (0, 0))
    sum_spec = pl.BlockSpec((8, width), lambda i: (0, 0))
    return pl.pallas_call(
        kernel,
        grid=(steps,),
        in_specs=[row_spec] * len(row_values) + [line_spec] * len(line_values),
        out_specs=[row_spec if shape.shape[0] == rows else sum_spec for shape in out_shapes],
        out_shape=out_shapes,
        compiler_params=pltpu.CompilerParams(vmem_limit_bytes=40 << 20),
        cost_estimate=pl.CostEstimate(flops=0, bytes_accessed=0, transcendentals=0),
    )(*row_values, *[value.reshape(1, width) for value in line_values])


def norm_after(low, core, x_low, mid, old, shift, gain, bias):
    rows, width = old.shape
    out = [jax.ShapeDtypeStruct((rows, width), dtype) for dtype in (f32, bf16)]
    return norm_call(
        norm_kernel, rows, width, (low, core, x_low, mid, old), (shift, gain, bias), out
    )


def norm_before(low, core, x_low, mid, grad, old, gain):
    rows, width = old.shape
    out = [jax.ShapeDtypeStruct((8, width), f32)]
    out += [jax.ShapeDtypeStruct((rows, width), dtype) for dtype in (f32, bf16)]
    return norm_call(norm_back_kernel, rows, width, (low, core, x_low, mid, grad, old), (gain,), out)


def layout(lens, total, block):
    steps_index = jnp.arange(total, dtype=jnp.int32)
    blocks_first = (lens[0] + block - 1) // block
    second_start = blocks_first * block
    in_first = steps_index < lens[0]
    in_second = (steps_index >= second_start) & (steps_index < second_start + lens[1])
    return jnp.where(in_first, steps_index, jnp.where(in_second, steps_index - second_start, 0))


def rotary_tables(position):
    half_rot = ROT // 2
    lane = jnp.arange(LANES, dtype=jnp.int32) % HEAD_DIM
    freqs = 10000.0 ** (-((lane % half_rot).astype(f32) * 2.0) / ROT)
    angles = position.astype(f32)[..., None] * freqs
    cosine, sine = jnp.cos(angles), jnp.sin(angles)
    return (
        jnp.where(lane < ROT, cosine, 1.0),
        jnp.where(lane < half_rot, -sine, 0.0),
        jnp.where((lane >= half_rot) & (lane < ROT), sine, 0.0),
    )


def turn(field, cos, above, below, back=False):
    up = pltpu.roll(field, LANES - ROT // 2, 1) * above
    down = pltpu.roll(field, ROT // 2, 1) * below
    return field * cos - (up + down) if back else field * cos + (up + down)


def allowed_bias(scalars, group, first_row, rows, cols):
    first_len, second_len = scalars[2 * group], scalars[2 * group + 1]
    second_start = ((first_len + BLOCK - 1) // BLOCK) * BLOCK
    row = first_row + lax.broadcasted_iota(jnp.int32, (rows, 1), 0)
    in_second = (row >= second_start) & (row < second_start + second_len)
    start = jnp.where(row < first_len, 0, jnp.where(in_second, second_start, row))
    col = lax.broadcasted_iota(jnp.int32, (rows, cols), 1)
    return jnp.where((col >= start) & (col <= row), 0.0, neg_large)


def chunk_places(scalars, rows):
    me = scalars[4]
    return [pl.multiple_of((me ^ ((r % 2) * 2 + r // 2)) * rows, 64) for r in range(4)]


def head_mask(head):
    lane = lax.broadcasted_iota(jnp.int32, (1, LANES), 1)
    return jnp.where(lane // HEAD_DIM == head, 1.0, 0.0).astype(bf16)


def nt(left, right):
    return lax.dot_general(left, right, (((1,), (1,)), ((), ())), preferred_element_type=f32)


def nn(left, right):
    return jnp.dot(left, right, preferred_element_type=f32)


def tn(left, right):
    return lax.dot_general(left, right, (((0,), (0,)), ((), ())), preferred_element_type=f32)


def attention_kernel(
    scalars, mixed_ref, cos_ref, above_ref, below_ref, out_ref, kept_ref, sums_ref, held
):
    group = pl.program_id(0)
    rows = mixed_ref.shape[2]
    width = mixed_ref.shape[3] // 3
    total = 4 * rows
    places = chunk_places(scalars, rows)
    for r in range(4):
        at = pl.ds(places[r], rows)
        cos, above, below = cos_ref[0, at, :], above_ref[0, at, :], below_ref[0, at, :]
        for part in range(0, 2 * width, LANES):
            turned = turn(mixed_ref[r, 0, :, part : part + LANES], cos, above, below)
            if part < width:
                turned = turned.astype(bf16) * HEAD_DIM**-0.5
            kept_ref[0, at, part : part + LANES] = turned.astype(bf16)
        kept_ref[0, at, 2 * width :] = mixed_ref[r, 0, :, 2 * width :].astype(bf16)
    for first in range(0, total, TILE):
        cols = first + TILE
        bias = allowed_bias(scalars, group, first, TILE, cols)
        for pair in range(0, width, LANES):
            query = kept_ref[0, first:cols, pair : pair + LANES]
            key = kept_ref[0, :cols, width + pair : width + pair + LANES]
            value = kept_ref[0, :cols, 2 * width + pair : 2 * width + pair + LANES]
            result = None
            for head in range(LANES // HEAD_DIM):
                mask = head_mask(head)
                scores = nt(query * mask, key) + bias
                top = jnp.max(scores, axis=1, keepdims=True)
                expo = jnp.exp(scores - top)
                mass = jnp.sum(expo, axis=1, keepdims=True)
                probs16 = (expo * (1.0 / mass)).astype(bf16)
                mine = nn(probs16, value * mask)
                result = mine if result is None else result + mine
                at_head = pair // HEAD_DIM + head
                sums_ref[0, first:cols, at_head : at_head + 1] = top + jnp.log(mass)
            held[first:cols, pair : pair + LANES] = result.astype(bf16)
    for r in range(4):
        out_ref[r, 0] = held[pl.ds(places[r], rows), :]


def attention_back_kernel(
    scalars,
    kept_ref,
    sums_ref,
    grad_ref,
    cos_ref,
    above_ref,
    below_ref,
    out_ref,
    held,
    query_grad,
    key_grad,
    value_grad,
):
    group = pl.program_id(0)
    rows = grad_ref.shape[2]
    width = grad_ref.shape[3]
    total = 4 * rows
    places = chunk_places(scalars, rows)
    for r in range(4):
        held[pl.ds(places[r], rows), :] = grad_ref[r, 0]
    for first in reversed(range(0, total, TILE)):
        cols = first + TILE
        bias = allowed_bias(scalars, group, first, TILE, cols)
        for pair in range(0, width, LANES):
            lanes = slice(pair, pair + LANES)
            query = kept_ref[0, first:cols, pair : pair + LANES]
            key = kept_ref[0, :cols, width + pair : width + pair + LANES]
            value = kept_ref[0, :cols, 2 * width + pair : 2 * width + pair + LANES]
            grad = held[first:cols, lanes]
            grads = [None, None, None]
            for head in range(LANES // HEAD_DIM):
                mask = head_mask(head)
                at_head = pair // HEAD_DIM + head
                query_head, grad_head = query * mask, grad * mask
                scores = nt(query_head, key) + bias
                probs = jnp.exp(scores - sums_ref[0, first:cols, at_head : at_head + 1])
                prob_grad = nt(grad_head, value)
                mean = jnp.sum(probs * prob_grad, axis=1, keepdims=True)
                score_grad = (probs * (prob_grad - mean)).astype(bf16)
                mine = (
                    nn(score_grad, key * mask),
                    tn(score_grad, query_head),
                    tn(probs.astype(bf16), grad_head),
                )
                grads = [m if g is None else g + m for g, m in zip(grads, mine)]
            query_grad[first:cols, lanes] = grads[0]
            if cols == total:
                key_grad[:, lanes] = grads[1]
                value_grad[:, lanes] = grads[2]
            else:
                key_grad[:cols, lanes] += grads[1]
                value_grad[:cols, lanes] += grads[2]
    for r in range(4):
        at = pl.ds(places[r], rows)
        cos, above, below = cos_ref[0, at, :], above_ref[0, at, :], below_ref[0, at, :]
        for pair in range(0, width, LANES):
            query = turn(query_grad[at, pair : pair + LANES] * HEAD_DIM**-0.5, cos, above, below, True)
            key = turn(key_grad[at, pair : pair + LANES], cos, above, below, True)
            out_ref[r, 0, :, pair : pair + LANES] = query.astype(bf16)
            out_ref[r, 0, :, width + pair : width + pair + LANES] = key.astype(bf16)
        out_ref[r, 0, :, 2 * width :] = value_grad[at, :].astype(bf16)


def chunk_spec(rows, width):
    return pl.BlockSpec((4, 1, rows, width), lambda g, scalars: (0, g, 0, 0))


def group_spec(total, width):
    return pl.BlockSpec((1, total, width), lambda g, scalars: (g, 0, 0))


def attention_forward(mixed, tables, scalars, rows):
    width = mixed.shape[1] // 3
    total = 4 * rows
    attended, kept, sums = pl.pallas_call(
        attention_kernel,
        grid_spec=pltpu.PrefetchScalarGridSpec(
            num_scalar_prefetch=1,
            grid=(2,),
            in_specs=[chunk_spec(rows, 3 * width)] + [group_spec(total, LANES)] * 3,
            out_specs=[
                chunk_spec(rows, width),
                group_spec(total, 3 * width),
                group_spec(total, LANES),
            ],
            scratch_shapes=[pltpu.VMEM((total, width), bf16)],
        ),
        out_shape=[
            jax.ShapeDtypeStruct((4, 2, rows, width), bf16),
            jax.ShapeDtypeStruct((2, total, 3 * width), bf16),
            jax.ShapeDtypeStruct((2, total, LANES), f32),
        ],
        compiler_params=pltpu.CompilerParams(vmem_limit_bytes=40 << 20),
        cost_estimate=pl.CostEstimate(flops=0, bytes_accessed=0, transcendentals=0),
    )(scalars, mixed.reshape(4, 2, rows, 3 * width), *tables)
    return attended.reshape(8 * rows, width), kept, sums


def attention_backward(kept, sums, grad16, tables, scalars, rows):
    width = grad16.shape[1]
    total = 4 * rows
    mixed_grad = pl.pallas_call(
        attention_back_kernel,
        grid_spec=pltpu.PrefetchScalarGridSpec(
            num_scalar_prefetch=1,
            grid=(2,),
            in_specs=[
                group_spec(total, 3 * width),
                group_spec(total, LANES),
                chunk_spec(rows, width),
            ]
            + [group_spec(total, LANES)] * 3,
            out_specs=chunk_spec(rows, 3 * width),
            scratch_shapes=[pltpu.VMEM((total, width), bf16)]
            + [pltpu.VMEM((total, width), f32)] * 3,
        ),
        out_shape=jax.ShapeDtypeStruct((4, 2, rows, 3 * width), bf16),
        compiler_params=pltpu.CompilerParams(vmem_limit_bytes=40 << 20),
        cost_estimate=pl.CostEstimate(flops=0, bytes_accessed=0, transcendentals=0),
    )(scalars, kept, sums, grad16.reshape(4, 2, rows, width), *tables)
    return mixed_grad.reshape(8 * rows, 3 * width)


def call(kernel, args, grid, in_specs, out_specs, out_shape, scratch_shapes=(), scalars=0):
    return pl.pallas_call(
        kernel,
        grid_spec=pltpu.PrefetchScalarGridSpec(
            num_scalar_prefetch=scalars,
            grid=grid,
            in_specs=in_specs,
            out_specs=out_specs,
            scratch_shapes=scratch_shapes,
        ),
        out_shape=out_shape,
        compiler_params=pltpu.CompilerParams(vmem_limit_bytes=48 << 20),
        cost_estimate=pl.CostEstimate(flops=0, bytes_accessed=0, transcendentals=0),
    )(*args)


def mix_kernel(left_ref, right_ref, shift_ref, out_ref):
    out_ref[...] = nn(left_ref[...], right_ref[...]) + shift_ref[...]


def mix_product(normed, mixed_full, shift):
    rows, width = normed.shape
    cols = shift.shape[1]
    block = rows // 3
    return call(
        mix_kernel,
        (normed, mixed_full, shift.reshape(1, cols)),
        (3,),
        [
            pl.BlockSpec((block, width), lambda i: (i, 0)),
            pl.BlockSpec((width, cols), lambda i: (0, 0)),
            pl.BlockSpec((1, cols), lambda i: (0, 0)),
        ],
        pl.BlockSpec((block, cols), lambda i: (i, 0)),
        jax.ShapeDtypeStruct((rows, cols), f32),
    )


def hide_kernel(left_ref, right_ref, shift_ref, out_ref, slope_ref):
    value = nn(left_ref[...], right_ref[...]) + shift_ref[...]
    inner = math.sqrt(2.0 / math.pi)
    square = value * value
    bend = jnp.tanh(inner * value * (1.0 + 0.044715 * square))
    half = 0.5 * (1.0 + bend)
    out_ref[...] = (value * half).astype(bf16)
    slope = 0.5 * value * (1.0 - bend * bend) * (inner * (1.0 + 3.0 * 0.044715 * square))
    slope_ref[...] = (half + slope).astype(slope_ref.dtype)


def hide_product(normed, up_full, shift):
    rows, width = normed.shape
    cols = up_full.shape[1]
    block = rows // 6
    out = pl.BlockSpec((block, cols), lambda i: (i, 0))
    return call(
        hide_kernel,
        (normed, up_full, shift.reshape(1, cols)),
        (6,),
        [
            pl.BlockSpec((block, width), lambda i: (i, 0)),
            pl.BlockSpec((width, cols), lambda i: (0, 0)),
            pl.BlockSpec((1, cols), lambda i: (0, 0)),
        ],
        [out, out],
        [jax.ShapeDtypeStruct((rows, cols), dtype) for dtype in (bf16, f32)],
    )


def out_kernel(first_ref, second_ref, dense_ref, down_ref, out_ref):
    value = nt(first_ref[...], dense_ref[...]) + nn(second_ref[...], down_ref[...])
    out_ref[...] = value.astype(out_ref.dtype)


def out_product(attended, hidden, mixed_full, down_full, half, dtype):
    rows, width = attended.shape[0] // 2, down_full.shape[1]
    heads = attended.shape[1]
    return call(
        out_kernel,
        (attended, hidden, mixed_full, down_full),
        (width // 512,),
        [
            pl.BlockSpec((rows, heads), lambda j: (half, 0)),
            pl.BlockSpec((rows, hidden.shape[1]), lambda j: (half, 0)),
            pl.BlockSpec((512, heads), lambda j: (j, 3)),
            pl.BlockSpec((hidden.shape[1], 512), lambda j: (0, j)),
        ],
        pl.BlockSpec((rows, 512), lambda j: (0, j)),
        jax.ShapeDtypeStruct((rows, width), dtype),
    )


def nn_kernel(left_ref, right_ref, out_ref):
    out_ref[...] = nn(left_ref[...], right_ref[...]).astype(out_ref.dtype)


def nt_scaled_kernel(left_ref, right_ref, slope_ref, out_ref):
    value = nt(left_ref[...], right_ref[...]) * slope_ref[...].astype(f32)
    out_ref[...] = value.astype(out_ref.dtype)


def attended_back(grad16, mixed_full, heads):
    rows, width = grad16.shape
    block = rows // 3
    return call(
        nn_kernel,
        (grad16, mixed_full),
        (3,),
        [
            pl.BlockSpec((block, width), lambda i: (i, 0)),
            pl.BlockSpec((width, heads), lambda i: (0, 3)),
        ],
        pl.BlockSpec((block, heads), lambda i: (i, 0)),
        jax.ShapeDtypeStruct((rows, heads), bf16),
    )


def hidden_back(grad16, down_full, slope):
    rows, width = grad16.shape
    cols = slope.shape[1]
    block = rows // 2
    spec = pl.BlockSpec((block, 256), lambda i, j: (i, j))
    return call(
        nt_scaled_kernel,
        (grad16, down_full, slope),
        (2, cols // 256),
        [
            pl.BlockSpec((block, width), lambda i, j: (i, 0)),
            pl.BlockSpec((256, width), lambda i, j: (j, 0)),
            spec,
        ],
        spec,
        jax.ShapeDtypeStruct((rows, cols), bf16),
    )


def both_kernel(first_ref, second_ref, proj_ref, up_ref, out_ref):
    value = nt(first_ref[...], proj_ref[...]) + nt(second_ref[...], up_ref[...])
    out_ref[...] = value.astype(out_ref.dtype)


def normed_back(mixed_grad, pre_grad, mixed_full, up_full, half, dtype):
    rows, width = mixed_grad.shape[0] // 2, up_full.shape[0]
    return call(
        both_kernel,
        (mixed_grad, pre_grad, mixed_full, up_full),
        (width // 512,),
        [
            pl.BlockSpec((rows, mixed_grad.shape[1]), lambda j: (half, 0)),
            pl.BlockSpec((rows, pre_grad.shape[1]), lambda j: (half, 0)),
            pl.BlockSpec((512, mixed_grad.shape[1]), lambda j: (j, 0)),
            pl.BlockSpec((512, up_full.shape[1]), lambda j: (j, 0)),
        ],
        pl.BlockSpec((rows, 512), lambda j: (0, j)),
        jax.ShapeDtypeStruct((rows, width), dtype),
    )


def in_grad_kernel(left_ref, right_ref, *refs):
    value = tn(left_ref[...], right_ref[...])
    for ref in refs[:-1]:
        value = value + ref[...].astype(f32)
    refs[-1][...] = value.astype(bf16)


def in_grad(part, k, normed, grad, *others):
    rows, cols = grad.shape
    block = min(part, 256)
    steps = part // block
    spec = pl.BlockSpec((block, cols), lambda i: (i, 0))
    return call(
        in_grad_kernel,
        (normed, grad, *others),
        (steps,),
        [
            pl.BlockSpec((rows, block), lambda i: (0, k * steps + i)),
            pl.BlockSpec((rows, cols), lambda i: (0, 0)),
        ]
        + [spec] * len(others),
        spec,
        jax.ShapeDtypeStruct((part, cols), bf16),
    )


def down_grad(part, k, hidden, grad, *others):
    rows, height = hidden.shape
    block = min(part, 256)
    steps = part // block
    spec = pl.BlockSpec((height, block), lambda j: (0, j))
    return call(
        in_grad_kernel,
        (hidden, grad, *others),
        (steps,),
        [
            pl.BlockSpec((rows, height), lambda j: (0, 0)),
            pl.BlockSpec((rows, block), lambda j: (0, k * steps + j)),
        ]
        + [spec] * len(others),
        spec,
        jax.ShapeDtypeStruct((height, part), bf16),
    )


def mixed_grad_kernel(normed_ref, mixed_ref, grad_ref, attended_ref, *refs):
    split = mixed_ref.shape[1]
    values = (tn(normed_ref[...], mixed_ref[...]), tn(grad_ref[...], attended_ref[...]))
    for value, cols in zip(values, (slice(0, split), slice(split, None))):
        for ref in refs[:-1]:
            value = value + ref[:, cols].astype(f32)
        refs[-1][:, cols] = value.astype(bf16)


def mixed_weight_grad(part, k, normed, mixed_grad, grad, attended, *others):
    rows, heads = attended.shape
    width = mixed_grad.shape[1] + heads
    block = min(part, 256)
    steps = part // block
    spec = pl.BlockSpec((block, width), lambda i: (i, 0))
    slice_spec = pl.BlockSpec((rows, block), lambda i: (0, k * steps + i))
    return call(
        mixed_grad_kernel,
        (normed, mixed_grad, grad, attended, *others),
        (steps,),
        [
            slice_spec,
            pl.BlockSpec(mixed_grad.shape, lambda i: (0, 0)),
            slice_spec,
            pl.BlockSpec(attended.shape, lambda i: (0, 0)),
        ]
        + [spec] * len(others),
        spec,
        jax.ShapeDtypeStruct((part, width), bf16),
    )


def halves_kernel(axis, mid_ref, keep_ref, other_ref, *refs):
    out_ref, size = refs[-1], keep_ref.shape[axis]
    for part_ref, half in ((keep_ref, mid_ref[0]), (other_ref, 1 - mid_ref[0])):
        at = pl.ds(pl.multiple_of(half * size, LANES), size)
        if axis:
            out_ref[0, :, at] = part_ref[...].astype(f32)
        else:
            out_ref[0, at, :] = part_ref[...].astype(f32)


def place_halves(keep, other, mid, axis, layer, layers, before=None):
    rows, cols = keep.shape
    shape = (rows, 2 * cols) if axis else (2 * rows, cols)
    if cols % LANES or (axis == 0 and rows % LANES):
        line = jnp.concatenate([pick(keep, other, mid), pick(other, keep, mid)], axis=axis)
        line = line.astype(f32)[None]
        if before is None:
            return jnp.concatenate([jnp.zeros_like(line)] * layer + [line], axis=0)
        return jnp.concatenate([line, before[1:]], axis=0)
    spec = pl.BlockSpec((rows, cols), lambda i, mid_ref: (0, 0))
    given = [] if before is None else [before]
    return pl.pallas_call(
        partial(halves_kernel, axis),
        grid_spec=pltpu.PrefetchScalarGridSpec(
            num_scalar_prefetch=1,
            grid=(1,),
            in_specs=[spec, spec] + [pl.BlockSpec(memory_space=pl.ANY)] * len(given),
            out_specs=pl.BlockSpec((1, *shape), lambda i, mid_ref: (layer, 0, 0)),
        ),
        out_shape=jax.ShapeDtypeStruct((layers, *shape), f32),
        input_output_aliases={3: 0} if given else {},
        compiler_params=pltpu.CompilerParams(vmem_limit_bytes=32 << 20),
        cost_estimate=pl.CostEstimate(flops=0, bytes_accessed=0, transcendentals=0),
    )(mid.reshape(1), keep, other, *given)


def last_kernel(
    order_ref, low_ref, core_ref, x_ref, mid_ref, old_ref, shift_ref, out_ref, held
):
    branch = low_ref[...] + core_ref[...].astype(f32) + x_ref[...].astype(f32)
    held[...] = old_ref[...] + (branch + mid_ref[...].astype(f32)) + shift_ref[...]
    order_kernel(True, order_ref, held, out_ref)


def last_stream(order, low, core, x_low, mid, old, shift):
    rows, width = old.shape
    if width // order.shape[0] % LANES:
        branch = low[:rows] + core[:rows].astype(f32) + x_low.astype(f32) + mid.astype(f32)
        return reorder(old + branch + shift, order, f32, True)
    steps = row_steps(rows)
    row_spec = pl.BlockSpec((rows // steps, width), lambda i, order_ref: (i, 0))
    return call(
        last_kernel,
        (order, low, core, x_low, mid, old, shift),
        (steps,),
        [row_spec] * 5 + [pl.BlockSpec((1, width), lambda i, order_ref: (0, 0))],
        row_spec,
        jax.ShapeDtypeStruct((rows, width), f32),
        [pltpu.VMEM((rows // steps, width), f32)],
        scalars=1,
    )


def halves(value, half, axis):
    size = value.shape[axis] // 2
    return lax.dynamic_slice_in_dim(value, half * size, size, axis)


class Small:
    def __init__(self, seq, mine, tensor, mid, beside):
        self.seq, self.tensor = seq, tensor
        self.mine, self.beside = seq.settle(
            lambda mine: pair_up(mine, swap(mine, "dp", MID), mid, 0), mine[None], beside=beside
        )

    def second(self):
        def step(mine):
            for bit in side_bits():
                mine = jnp.concatenate([mine, swap(mine, "dp", bit)], axis=0)
            return mine[None]

        self.mine = self.seq.settle(step, self.mine)

    def finish(self, unpack):
        def step(mine):
            for bit in (0, 1):
                mine = pair_up(mine, swap(mine, "tensor", bit), (self.tensor >> bit) & 1, 0)
            return unpack(jnp.swapaxes(mine, 0, 1))

        return self.seq.settle(step, self.mine)


class SmallSums:
    def __init__(self, seq, norm_grads, in_bgrads, mid):
        self.seq, self.mid = seq, mid
        self.norm_grads, self.in_bgrads = norm_grads, in_bgrads
        self.layers, self.kinds = len(norm_grads), 3
        self.sides = side_bits()

    def halve(self, sums, biases, axis, half, move):
        keep, sent = halves(sums, half, axis), halves(sums, 1 - half, axis)
        split = biases.shape[0]
        received = move(jnp.concatenate([biases, sent.reshape(-1)]))
        return keep + received[split:].reshape(keep.shape), received[:split]

    def side(self, s, sums, biases):
        sums, other = self.halve(
            sums, biases, 1, 0, lambda value: swap(value, "dp", self.sides[s])
        )
        return sums, biases + other

    def first(self):
        tensor = lax.axis_index("tensor")

        def step(*values):
            sums = jnp.stack([value[: self.kinds] for value in values[: self.layers]])
            biases = jnp.concatenate(values[self.layers :])
            shape = (self.layers * self.kinds, 1 << len(self.sides), 2, lax.axis_size("tensor"), -1)
            sums, biases = self.side(len(self.sides) - 1, sums.reshape(shape), biases)
            none = biases[:0]
            for bit in (1, 0):
                sums, _ = self.halve(
                    sums, none, 3, (tensor >> bit) & 1, lambda value: swap(value, "tensor", bit)
                )
            return sums, biases

        values = [value for pair in self.in_bgrads for value in pair]
        self.sums, self.biases = self.seq.settle(step, *self.norm_grads, *values)

    def second(self):
        def step(sums, biases):
            sums, other = self.halve(
                sums, biases, 2, self.mid, lambda value: swap(value, "dp", MID)
            )
            pair = (pick(biases, other, self.mid), pick(other, biases, self.mid))
            return sums, jnp.concatenate(pair)

        self.sums, self.biases = self.seq.settle(step, self.sums, self.biases)

    def finish(self):
        def step(sums, biases):
            for s in reversed(range(len(self.sides) - 1)):
                sums, biases = self.side(s, sums, biases)
            return sums, biases

        sums, biases = self.seq.settle(step, self.sums, self.biases)
        return sums.reshape(self.layers, self.kinds, -1), biases.reshape(2, -1)


def shards(
    tokens_in,
    lengths,
    norm_gain,
    norm_bias,
    proj_weight,
    proj_bias,
    dense_weight,
    dense_bias,
    up_weight,
    up_bias,
    down_weight,
    down_bias,
    cotangent,
):
    rows, width = tokens_in.shape
    layer_count = proj_weight.shape[0]
    n_dp = lax.axis_size("dp")
    dp = lax.axis_index("dp")
    tensor = lax.axis_index("tensor")
    mid = (dp >> MID) & 1
    order = slice_order()
    seq = Sequence(lengths[0, 0].astype(f32), lengths[0, 0] > 0)

    def take_mixed(l, half, weight=proj_weight):
        proj = halves(weight[l], half, 2).reshape(weight.shape[1], -1)
        return jnp.concatenate([proj, halves(dense_weight[l], half, 0).T], axis=1)

    def take_up(l, half, weight=up_weight):
        return halves(weight[l], half, 1)

    def take_down(l, half, weight=down_weight):
        return halves(weight[l], half, 0)

    takes = ((take_mixed, 0), (take_up, 0), (take_down, 1))

    def set_out(l, i):
        weight = (proj_weight, up_weight, down_weight)[i]
        part = seq.run(lambda value: takes[i][0](l, 1 - mid, value), weight, apart=True)
        return seq.start(part, "dp", MID)

    def paired(l, i, moving):
        return joined(l, i, seq.wait(moving))

    def joined(l, i, received):
        take, axis = takes[i]
        block = seq.run(
            lambda other: pair_up(take(l, mid), other, mid, axis), received, apart=True
        )
        return Spread(seq, block, axis)

    moving = [set_out(0, 0), set_out(0, 1)]
    cot = seq.run(lambda value: reorder(value, order, bf16), cotangent)
    whole_lens = lengths.reshape(-1).astype(f32)
    coarse = jnp.floor(whole_lens / 8.0)
    small = Small(
        seq,
        jnp.concatenate(
            [
                value.reshape(-1)
                for value in (norm_gain, norm_bias, dense_bias, down_bias, proj_bias, up_bias)
            ]
            + [coarse.astype(bf16), (whole_lens - 8.0 * coarse).astype(bf16)]
        ),
        tensor,
        mid,
        lambda: swap(cot, "tensor", 1),
    )
    cot_across = small.beside
    small.second()
    m0 = paired(0, 0, moving[0])
    u0 = paired(0, 1, moving[1])
    m0.near()
    m0.far()
    sent = seq.run(lambda value: take_down(0, 1 - mid, value), down_weight, apart=True)
    each, proj_each, up_each = norm_gain.shape[1], proj_bias.shape[3], up_bias.shape[2]

    def unpack(everyone):
        pair_lens = lax.dynamic_index_in_dim(everyone[:2, :, -4:], tensor, 1, keepdims=False)
        pair_lens = pair_lens.astype(f32)
        pair_lens = (pair_lens[:, :2] * 8.0 + pair_lens[:, 2:]).astype(jnp.int32)
        lens = pick(pair_lens, pair_lens[::-1], mid)
        everyone = everyone[:, :, :-4]
        at = 4 * layer_count * each
        norm_parts = everyone[:, :, :at].reshape(n_dp, -1, 4 * layer_count, each)
        norm_parts = jnp.transpose(norm_parts, (2, 0, 1, 3)).reshape(4, layer_count, width)
        norm_parts = norm_parts.astype(f32)
        same_heads = lax.dynamic_index_in_dim(everyone[:, :, at:], tensor, 1, keepdims=False)
        same_heads = halves(same_heads[slice_places()], mid, 0).astype(f32)
        proj_at = layer_count * 3 * proj_each
        proj_shift = jnp.transpose(
            same_heads[:, :proj_at].reshape(-1, layer_count * 3, proj_each), (1, 0, 2)
        ).reshape(layer_count, -1)
        up_shift = jnp.transpose(
            same_heads[:, proj_at:].reshape(-1, layer_count, up_each), (1, 0, 2)
        ).reshape(layer_count, -1)
        gains, biases = norm_parts[0], norm_parts[1]
        shifts = norm_parts[2] + norm_parts[3]
        scalars = jnp.concatenate([lens.reshape(-1), tensor[None].astype(jnp.int32)])
        lines = [value[l] for value in (gains, biases, shifts) for l in range(layer_count)]
        lines += [value[l] for value in (proj_shift, up_shift) for l in range(layer_count)]
        return [line[None] for line in lines], lens, scalars.astype(jnp.int32)

    lines, lens, scalars = small.finish(unpack)
    gains, biases, out_shifts, proj_shift, up_shift = (
        lines[i * layer_count : (i + 1) * layer_count] for i in range(5)
    )

    def mix(l, normed, proj_full):
        return seq.run(mix_product, normed, proj_full, proj_shift[l])

    def attend(mixed):
        return seq.run(lambda value: attention_forward(value, tables, scalars, rows), mixed)

    def hide(l, normed, up_full):
        return seq.run(hide_product, normed, up_full, up_shift[l])

    def make_tables():
        return rotary_tables(jax.vmap(partial(layout, total=4 * rows, block=BLOCK))(lens))

    stream, own = seq.run(
        lambda value: norm_first(value, order, gains[0], biases[0]), tokens_in
    )
    mid_rows, across = seq.start(own, "dp", MID), seq.start(own, "tensor", 1)
    moving = seq.start(sent, "dp", MID)
    tables = seq.run(make_tables, apart=True)
    across = seq.wait(across)
    m0.near_wait()
    m0.far_wait()
    m0.last()
    u0.far()
    core_parts = seq.settle(
        lambda *values: tuple(swap(value, "tensor", 0) for value in values), own, across
    )
    u0.near()
    token_parts = (own, seq.wait(mid_rows), across, *core_parts)

    def finish_first(own, mid, across, core_own, core_across):
        both = swap(mid, "tensor", 1)
        both, mid = lax.optimization_barrier((both, mid))
        core_both = swap(both, "tensor", 0)
        core_both, mid = lax.optimization_barrier((core_both, mid))
        core_mid = swap(mid, "tensor", 0)
        parts = (own, mid, across, both, core_own, core_mid, core_across, core_both)
        return assemble(parts, 0)

    normed = seq.settle(finish_first, *token_parts)
    received = seq.wait(moving)
    seq.tick(7)
    d0 = joined(0, 2, received)
    m0.last_wait()
    u0.far_wait()
    seq.tick(1)
    u0.near_wait()
    u0.last()
    d0.far()
    d0.near()
    mixed_full = m0.whole()
    mixed = mix(0, normed, mixed_full)
    attended, kept, sums = attend(mixed)
    u0.last_wait()
    seq.tick(1)
    up_full = u0.whole()
    hidden, slope = hide(0, normed, up_full)
    d0.far_wait()
    seq.tick(3)
    d0.near_wait()
    d0.last()
    m1 = paired(1, 0, set_out(1, 0))
    m1.far()
    moving = set_out(1, 1)
    cot_mid = seq.start(cot, "dp", MID)
    d0.last_wait()
    down_full = d0.whole()
    m1.near()
    saved = [(normed, kept, sums, slope, attended, hidden)]
    weights = [(mixed_full, up_full, down_full)]
    streams = [stream]

    branch = Scatter(seq, out_product, (attended, hidden, mixed_full, down_full), rows)
    branch.begin()
    u1 = paired(1, 1, moving)
    moving = set_out(1, 2)
    branch.second()
    cot_mid = seq.wait(cot_mid)
    d1 = paired(1, 2, moving)
    m1.far_wait()
    seq.tick(2)
    m1.near_wait()
    m1.last()
    branch.third()
    u1.near()
    u1.far()
    stream, own = branch.finish(
        norm_after, stream, out_shifts[0], gains[1], biases[1]
    )
    streams.append(stream)

    def with_cores(mine, mid, cot, across):
        parts, both = gather_start_beside(mine, mid)
        *parts, cot, across = lax.optimization_barrier((*parts, cot, across))
        return parts, both, swap(cot, "tensor", 0), swap(across, "tensor", 0)

    parts, cot_both, cot_core_own, cot_core_across = seq.settle(
        with_cores, own, cot_mid, cot, cot_across
    )
    m1.last_wait()
    u1.near_wait()
    u1.far_wait()
    d1.near()
    d1.far()
    u1.last()
    grad16, normed, mixed_full = seq.settle(
        lambda *values: gather_finish_beside(values[:5], values[5:], m1.plain),
        *parts,
        cot,
        cot_mid,
        cot_across,
        cot_both,
        cot_core_own,
        cot_core_across,
    )
    mixed = mix(1, normed, mixed_full)
    d1.near_wait()
    u1.last_wait()
    attended, kept, sums = attend(mixed)
    up_full = u1.whole()
    hidden, slope = hide(1, normed, up_full)
    d1.far_wait()
    d1.last()
    saved.append((normed, kept, sums, slope, attended, hidden))
    weights.append((mixed_full, up_full, None))

    heads_width = attended.shape[1]
    parts = 1 << len(side_bits())
    norm_grads, in_bgrads = [None] * layer_count, [None] * layer_count

    part = width // parts

    def down_grads(l, grad16):
        return Reduce(seq, partial(down_grad, part), saved[l][5], grad16)

    def up_grads(l, grad):
        return Reduce(seq, partial(in_grad, part), saved[l][0], grad)

    def mixed_grads(l, grad, grad16):
        values = saved[l][0], grad, grad16, saved[l][4]
        return Reduce(seq, partial(mixed_weight_grad, part), *values)

    def attend_back(l, grad16):
        kept, sums = saved[l][1:3]
        mixed_full = weights[l][0]

        def step(value):
            grad = attended_back(value, mixed_full, heads_width)
            return attention_backward(kept, sums, grad, tables, scalars, rows)

        return seq.run(step, grad16)

    def hide_back(l, grad16):
        slope, down_full = saved[l][3], weights[l][2]
        return seq.run(lambda value: hidden_back(value, down_full, slope), grad16)

    def rows_back(l, mixed_grad, pre_grad):
        return Scatter(seq, normed_back, (mixed_grad, pre_grad, *weights[l][:2]), rows)

    def bias_back(mixed_grad, pre_grad):
        return jnp.sum(mixed_grad, axis=0, dtype=f32), jnp.sum(pre_grad, axis=0, dtype=f32)

    def own_start(total, axis):
        return halves(total, mid, axis), seq.start(halves(total, 1 - mid, axis), "dp", MID)

    def own_wait(pair):
        keep, moving = pair
        received = seq.wait(moving)
        return pick(keep, received, mid).astype(f32), pick(received, keep, mid).astype(f32)

    first, second = 0, 1
    early = len(side_bits()) == 2

    def send(reduce, which):
        reduce.send(reduce.near(which))

    def arrive(reduce, which):
        reduce.wait(reduce.near(which))

    def rest(reduce):
        for which in (first, second):
            reduce.make(reduce.near(which))
            send(reduce, which)
            arrive(reduce, which)
        reduce.make_far()
        reduce.send_far()
        reduce.wait_far()
        reduce.finish()

    down2 = down_grads(1, grad16)
    down2.make(down2.near(first))
    if early:
        send(down2, first)
    mixed_grad = attend_back(1, grad16)
    d1.last_wait()
    weights[1] = (mixed_full, up_full, d1.whole())
    if early:
        down2.make(down2.near(second))
        send(down2, second)
    pre_grad = hide_back(1, grad16)
    up2, mix2 = up_grads(1, pre_grad), mixed_grads(1, mixed_grad, grad16)
    back = rows_back(1, mixed_grad, pre_grad)
    back.begin()
    branch = Scatter(seq, out_product, (attended, hidden, *weights[1][::2]), rows)
    if early:
        arrive(down2, first)
        up2.make(up2.near(first))
        send(up2, first)
    made = back.second(
        lambda: (
            down2.plain(down2.far()) if early else (),
            up2.plain(up2.near(second)),
            mix2.plain(mix2.near(first)),
            mix2.plain(mix2.near(second)),
            bias_back(mixed_grad, pre_grad),
        )
    )
    in_bgrads[1] = made[4]
    if early:
        down2.take(down2.far(), made[0])
        up2.take(up2.near(second), made[1])
        mix2.take(mix2.near(first), made[2])
        mix2.take(mix2.near(second), made[3])
        arrive(down2, second)
        seq.tick(4)
        arrive(up2, first)
        send(up2, second)
    made = back.third(lambda: (up2.plain(up2.far()) if early else (), branch.plain()))
    branch.take(made[1])
    norm_grads[1], grad_stream, own = back.finish(
        norm_before, cot, streams[1], gains[1]
    )
    if early:
        up2.take(up2.far(), made[0])
        arrive(up2, second)
        send(mix2, first)
        down2.send_far()
    (branch.later, branch.x_high), coming = seq.settle(
        lambda own, low, core: gather_start_with(own, low, core, branch.sent_across),
        own,
        branch.low_part,
        branch.core,
    )
    if early:
        arrive(mix2, first)
        send(mix2, second)
        up2.send_far()
        grad16, made = seq.settle(gather_finish, *coming, beside=lambda: mix2.plain(mix2.far()))
        mix2.take(mix2.far(), made)
        mix2.send_far()
        down2.wait_far()
    else:
        grad16 = seq.settle(gather_finish, *coming)
        rest(down2)
        rest(up2)
        rest(mix2)

    results = {}

    def own_start(total, axis):
        keep, sent = seq.run(
            lambda value: (halves(value, mid, axis), halves(value, 1 - mid, axis)),
            total,
            apart=True,
        )
        return keep, seq.start(sent, "dp", MID)

    def own_finish(l, name, axis, pair):
        keep, moving = pair
        received = seq.wait(moving)
        before = results.get(name)
        given = () if before is None else (before,)
        results[name] = seq.run(
            lambda keep, other, *given: place_halves(
                keep, other, mid, axis, l, layer_count, *given
            ),
            keep,
            received,
            *given,
        )

    def mixed_finish(pair):
        keep, moving = pair
        received = seq.wait(moving)
        cols = 3 * heads_width

        def step(keep, other):
            pair = [pick(keep, other, mid).astype(f32), pick(other, keep, mid).astype(f32)]
            proj = [value[:, :cols].reshape(value.shape[0], 3, -1) for value in pair]
            dense = [value[:, cols:].T for value in pair]
            return jnp.concatenate(proj, axis=2), jnp.concatenate(dense, axis=0)

        return seq.run(step, keep, received, apart=True)

    down1 = down_grads(0, grad16)
    down1.make(down1.near(first))
    if early:
        send(down1, first)
        down2.make([0])
    sent = seq.run(branch.next, branch.low_part, branch.core, branch.x_high, apart=True)
    branch_mid = seq.start(sent, "dp", MID)
    mixed_grad = attend_back(0, grad16)
    if early:
        up2.wait_far()
        arrive(mix2, second)
    pre_grad = hide_back(0, grad16)
    up1, mix1 = up_grads(0, pre_grad), mixed_grads(0, mixed_grad, grad16)
    up1.make(up1.near(first))
    if early:
        send(up1, first)
        up2.make([0])
    branch.mid = seq.wait(branch_mid)
    if early:
        mix2.wait_far()
        seq.tick(2)
        arrive(down1, first)
        down1.make_far()
        down1.send_far()
    branch_low = seq.start(branch.later, "tensor", 1)
    up2_pair = own_start(up2.blocks[0], 0)
    up1.make(up1.near(second))
    mix1.make(mix1.near(first))
    down1.make(down1.near(second))
    if early:
        arrive(up1, first)
        up1.make_far()
        send(down1, second)
    branch.x_low = seq.wait(branch_low)
    down2_pair = own_start(down2.blocks[0], 1)
    back = rows_back(0, mixed_grad, pre_grad)
    back.begin()
    if early:
        down1.wait_far()
        up1.send_far()
    own_finish(1, "up", 1, up2_pair)
    if early:
        send(mix1, first)
    made = back.second(
        lambda: (
            mix1.plain(mix1.near(second)),
            bias_back(mixed_grad, pre_grad),
        )
    )
    mix1.take(mix1.near(second), made[0])
    in_bgrads[0] = made[1]
    own_finish(1, "down", 0, down2_pair)
    if early:
        seq.tick(2)
        arrive(down1, second)
        seq.tick(4)
        arrive(mix1, first)
        send(up1, second)
        send(mix1, second)
    made = back.third(
        lambda: (mix1.plain(mix1.far()), down1.plain([0]), mix2.plain([0])) if early else ()
    )
    norm_grads[0], grad_stream, own = back.finish(
        norm_before, grad_stream, streams[0], gains[0]
    )
    if early:
        mix1.take(mix1.far(), made[0])
        down1.take([0], made[1])
        mix2.take([0], made[2])
        up1.wait_far()
        seq.tick(7)
        arrive(up1, second)
        arrive(mix1, second)
        mix1.send_far()
    else:
        rest(down1)
        rest(up1)
        rest(mix1)
    mix2_pair = own_start(mix2.blocks[0], 0)
    down1_pair = own_start(down1.blocks[0], 1)
    if early:
        up1.make([0])
    up1_pair = own_start(up1.blocks[0], 0)
    small_sums = SmallSums(seq, norm_grads, in_bgrads, mid)
    small_sums.first()
    activations = branch.finish(partial(last_stream, order), streams[1], out_shifts[1])
    input_grad = seq.run(lambda value: reorder(value, order, f32, True), grad_stream)
    mix2_own = mixed_finish(mix2_pair)
    own_finish(0, "down", 0, down1_pair)
    small_sums.second()
    if early:
        mix1.wait_far()
        mix1.make([0])
    mix1_pair = own_start(mix1.blocks[0], 0)
    own_finish(0, "up", 1, up1_pair)
    seq.tick(6)
    norm_owned, bias_both = small_sums.finish()
    mix1_own = mixed_finish(mix1_pair)
    bias_both = bias_both + 0.0 * seq.scalar
    per_layer = bias_both.shape[1] // layer_count
    bias_both = bias_both.reshape(2, layer_count, per_layer)
    proj_b = jnp.transpose(
        bias_both[:, :, : 3 * heads_width].reshape(2, layer_count, 3, heads_width), (1, 2, 0, 3)
    ).reshape(layer_count, 3, 1, 2 * heads_width)
    up_b = jnp.transpose(bias_both[:, :, 3 * heads_width :], (1, 0, 2)).reshape(layer_count, 1, -1)
    return (
        activations,
        input_grad,
        norm_owned[:, 0],
        norm_owned[:, 1],
        jnp.stack([mix1_own[0], mix2_own[0]]),
        lax.dynamic_slice_in_dim(proj_b, dp * proj_each, proj_each, 3),
        jnp.stack([mix1_own[1], mix2_own[1]]),
        norm_owned[:, 2],
        results["up"],
        lax.dynamic_slice_in_dim(up_b, dp * up_each, up_each, 2),
        results["down"],
        norm_owned[:, 2],
    )


def solution(mesh):
    in_specs = (
        P(("dp", "tensor"), None),
        P("dp", None),
        P(None, ("dp", "tensor")),
        P(None, ("dp", "tensor")),
        P(None, "dp", None, "tensor"),
        P(None, None, "tensor", "dp"),
        P(None, "tensor", "dp"),
        P(None, ("dp", "tensor")),
        P(None, "dp", "tensor"),
        P(None, "tensor", "dp"),
        P(None, "tensor", "dp"),
        P(None, ("dp", "tensor")),
        P(("dp", "tensor"), None),
    )
    out_specs = (
        P(("dp", "tensor"), None),
        P(("dp", "tensor"), None),
        P(None, ("dp", "tensor")),
        P(None, ("dp", "tensor")),
        P(None, "dp", None, "tensor"),
        P(None, None, "tensor", "dp"),
        P(None, "tensor", "dp"),
        P(None, ("dp", "tensor")),
        P(None, "dp", "tensor"),
        P(None, "tensor", "dp"),
        P(None, "tensor", "dp"),
        P(None, ("dp", "tensor")),
    )
    return jax.shard_map(shards, mesh=mesh, in_specs=in_specs, out_specs=out_specs, check_vma=False)
```

```python
from functools import partial
import math

import jax
import jax.numpy as jnp
from jax import lax
from jax.experimental import pallas as pl
from jax.experimental.pallas import tpu as pltpu
from jax.sharding import PartitionSpec as P

HEAD_DIM = 64
ROT = 32
BLOCK = 128
LANES = 128
TILE = 256
MID = 1

TICK = 1_200_000_000

neg_large = -1e30
f32 = jnp.float32
bf16 = jnp.bfloat16


def swap(value, axis, bit):
    size = lax.axis_size(axis)
    return lax.ppermute(value, axis, [(i, i ^ (1 << bit)) for i in range(size)])


def tick_kernel(in_ref, out_ref):
    out_ref[0, 0] = in_ref[0, 0]


def tick(scalar, count):
    spec = pl.BlockSpec(memory_space=pltpu.SMEM)
    result = pl.pallas_call(
        tick_kernel,
        in_specs=[spec],
        out_specs=spec,
        out_shape=jax.ShapeDtypeStruct((1, 1), f32),
        cost_estimate=pl.CostEstimate(flops=count * TICK, bytes_accessed=0, transcendentals=0),
    )(scalar.reshape(1, 1))
    return result[0, 0]


class Sequence:
    def __init__(self, scalar, always):
        self.scalar = scalar
        self.always = always

    def gate(self, *values):
        *values, self.scalar = lax.optimization_barrier((*values, self.scalar))
        return values

    def run(self, step, *values, apart=False):
        values = self.gate(*values)
        if apart:
            shapes = jax.eval_shape(step, *values)

            def never(*others):
                return jax.tree.map(lambda shape: jnp.zeros(shape.shape, shape.dtype), shapes)

            result = lax.cond(self.always, step, never, *values)
        else:
            result = step(*values)
        leaves, tree = jax.tree.flatten(result)
        return jax.tree.unflatten(tree, self.gate(*leaves))

    def start(self, value, axis, bit):
        (value,) = self.gate(value)
        return swap(value, axis, bit)

    def wait(self, value):
        (value,) = self.gate(value)
        return value

    def settle(self, step, *values, beside=None):
        def both(*moved):
            return (step(*moved), beside()) if beside else step(*moved)

        return self.run(both, *values, apart=True)

    def tick(self, count):
        self.scalar = tick(self.scalar, count)

    def swap(self, value, axis, bit):
        return self.settle(lambda moved: swap(moved, axis, bit), value)


def side_bits():
    count = (lax.axis_size("dp") - 1).bit_length()
    return [bit for bit in range(count - 1, MID, -1)] + [0]


def slice_order():
    sides = side_bits()
    me = lax.axis_index("dp")
    base = me - (((me >> MID) & 1) << MID)
    order = []
    for k in range(1 << len(sides)):
        mask = sum(((k >> s) & 1) << bit for s, bit in enumerate(sides))
        for mid in range(2):
            order.append((base ^ mask) | (mid << MID))
    return jnp.stack(order).astype(jnp.int32)


def slice_places():
    sides = side_bits()
    every = jnp.arange(lax.axis_size("dp"), dtype=jnp.int32)
    apart = every ^ lax.axis_index("dp")
    place = (every >> MID) & 1
    for s, bit in enumerate(sides):
        place = place + (((apart >> bit) & 1) << (s + 1))
    return place


def pick(pair_first, pair_second, bit):
    return jnp.where(bit == 0, pair_first, pair_second)


def pair_up(keep, received, bit, axis):
    return jnp.concatenate(
        [pick(keep, received, bit), pick(received, keep, bit)], axis=axis
    )


class Spread:
    def __init__(self, seq, block, axis):
        self.seq, self.axis = seq, axis
        self.sides = side_bits()
        self.far_count = 1 << (len(self.sides) - 1)
        self.blocks = {0: block}

    def move(self, ks):
        for k in ks:
            if k != ks[0]:
                self.arrived(ks)
            s = k.bit_length() - 1
            self.blocks[k] = self.seq.start(self.blocks[k - (1 << s)], "dp", self.sides[s])

    def arrived(self, ks):
        last = max(k for k in ks if k in self.blocks)
        self.blocks[last] = self.seq.wait(self.blocks[last])

    def far(self):
        self.move(range(1, self.far_count))

    def far_wait(self):
        self.arrived(range(1, self.far_count))

    def near(self):
        self.move([self.far_count])

    def near_wait(self):
        self.arrived([self.far_count])

    def last(self):
        self.move(range(self.far_count + 1, 2 * self.far_count))

    def last_wait(self):
        self.arrived(range(self.far_count + 1, 2 * self.far_count))

    def plain(self, window=None):
        parts = [self.blocks[k] for k in sorted(self.blocks)]
        return assemble(parts, self.axis, window)

    def whole(self, window=None):
        parts = [self.blocks[k] for k in sorted(self.blocks)]
        return self.seq.run(lambda *values: assemble(values, self.axis, window), *parts)


class Reduce:
    def __init__(self, seq, product, *operands):
        self.seq, self.product, self.operands = seq, product, operands
        self.sides = side_bits()
        self.count = 1 << len(self.sides)
        self.blocks = {}
        self.arrived = [[] for _ in range(self.count)]
        self.moving = {}

    def make(self, ks):
        for k in ks:
            values = (*self.operands, *self.arrived[k])
            self.blocks[k] = self.seq.run(partial(self.product, k), *values)

    def plain(self, ks):
        return [self.product(k, *self.operands, *self.arrived[k]) for k in ks]

    def take(self, ks, made):
        self.blocks.update(zip(ks, made))

    def send(self, ks):
        for i, k in enumerate(ks):
            if i:
                self.wait([ks[i - 1]])
            s = k.bit_length() - 1
            self.moving[k] = self.seq.start(self.blocks[k], "dp", self.sides[s])

    def wait(self, ks):
        k = ks[-1]
        s = k.bit_length() - 1
        self.arrived[k - (1 << s)].append(self.seq.wait(self.moving[k]))

    def near(self, half):
        whole = list(reversed(range(self.count // 2, self.count)))
        middle = len(whole) // 2
        return whole[middle:] if half else whole[:middle]

    def far(self):
        return list(reversed(range(1, self.count // 2)))

    def make_far(self, near_done=True):
        ks = self.far()
        if ks[-1] in self.blocks or not (near_done or len(ks) == 1):
            return
        for k in ks[:-1]:
            self.make([k])
            self.send([k])
            self.wait([k])
        self.make(ks[-1:])

    def send_far(self):
        self.send(self.far()[-1:])

    def wait_far(self):
        self.wait(self.far()[-1:])

    def finish(self):
        self.make([0])
        return self.blocks[0]


def gather_start(own):
    mid, across = swap(own, "dp", MID), swap(own, "tensor", 1)
    own, mid, across = lax.optimization_barrier((own, mid, across))
    return own, mid, across, swap(own, "tensor", 0), swap(across, "tensor", 0)


def gather_start_with(own, low, core, sent):
    mid, across = swap(own, "dp", MID), swap(own, "tensor", 1)
    low, core, across = lax.optimization_barrier((low, core, across))
    later, x_high = sent(low, core)
    own, mid, across, x_high = lax.optimization_barrier((own, mid, across, x_high))
    core_parts = swap(own, "tensor", 0), swap(across, "tensor", 0)
    return (later, x_high), (own, mid, across, *core_parts)


def gather_finish(own, mid, across, core_own, core_across):
    both, core_mid = swap(mid, "tensor", 1), swap(mid, "tensor", 0)
    core_both = swap(both, "tensor", 0)
    parts = (own, mid, across, both, core_own, core_mid, core_across, core_both)
    return assemble(parts, 0)


class Gather:
    def __init__(self, seq, own, beside=None):
        self.seq = seq
        self.parts = seq.settle(gather_start, own, beside=beside)
        if beside:
            self.parts, self.beside = self.parts

    def finish(self, beside=None):
        return self.seq.settle(gather_finish, *self.parts, beside=beside)


def gather_start_beside(mine, mid):
    own, near, across = mine, swap(mine, "dp", MID), swap(mine, "tensor", 1)
    across, mid = lax.optimization_barrier((across, mid))
    both = swap(mid, "tensor", 1)
    own, near, across, both = lax.optimization_barrier((own, near, across, both))
    return (own, near, across, swap(own, "tensor", 0), swap(across, "tensor", 0)), both


def gather_finish_beside(parts, other, beside):
    own, mid, across, core_own, core_across = parts
    other_own, other_mid, other_across, other_both, other_core_own, other_core_across = other
    both, core_mid = swap(mid, "tensor", 1), swap(mid, "tensor", 0)
    core_mid, other_mid = lax.optimization_barrier((core_mid, other_mid))
    other_core_mid = swap(other_mid, "tensor", 0)
    other_core_mid, other_both = lax.optimization_barrier((other_core_mid, other_both))
    other_core_both = swap(other_both, "tensor", 0)
    others = (other_own, other_mid, other_across, other_both)
    others += (other_core_own, other_core_mid, other_core_across, other_core_both)
    whole, made = assemble(others, 0), beside()
    both, whole, made = lax.optimization_barrier((both, whole, made))
    core_both = swap(both, "tensor", 0)
    mine = (own, mid, across, both, core_own, core_mid, core_across, core_both)
    return whole, assemble(mine, 0), made


class Scatter:
    def __init__(self, seq, product, operands, rows):
        self.seq, self.product, self.operands, self.rows = seq, product, operands, rows

    def begin(self, beside=tuple):
        high = self.seq.run(lambda *values: self.product(*values, 1, bf16), *self.operands)
        self.core, (self.low_part, made) = self.seq.settle(
            lambda high: swap(high, "tensor", 0),
            high,
            beside=lambda: (self.product(*self.operands, 0, f32), beside()),
        )
        return made

    def plain(self):
        high = self.product(*self.operands, 1, bf16)
        return self.product(*self.operands, 0, f32), swap(high, "tensor", 0)

    def take(self, made):
        self.low_part, self.core = made

    def chunk(self, low, core, k, *others):
        at = slice(k * self.rows, (k + 1) * self.rows)
        part = low[at] + core[at].astype(f32)
        for value in others:
            part = part + value.astype(f32)
        return part

    def sent(self, low, core):
        return tuple(self.chunk(low, core, k).astype(bf16) for k in (2, 3))

    def next(self, low, core, other):
        return self.chunk(low, core, 1, other).astype(bf16)

    def second(self, beside=None):
        def step(low, core):
            later, first = self.sent(low, core)
            return later, swap(first, "tensor", 1)

        moved = self.seq.settle(step, self.low_part, self.core, beside=beside)
        if beside:
            moved, made = moved
        self.later, self.x_high = moved
        return made if beside else None

    def third_step(self, low, core, other, later):
        return swap(self.next(low, core, other), "dp", MID), swap(later, "tensor", 1)

    def third(self, beside=None):
        values = (self.low_part, self.core, self.x_high, self.later)
        moved = self.seq.settle(self.third_step, *values, beside=beside)
        if beside:
            moved, made = moved
        self.mid, self.x_low = moved
        return made if beside else None

    def sent_across(self, low, core):
        later, first = self.sent(low, core)
        return later, swap(first, "tensor", 1)

    def finish(self, step, *others):
        return self.seq.run(step, self.low_part, self.core, self.x_low, self.mid, *others)


def order_kernel(back, order_ref, in_ref, out_ref):
    count = order_ref.shape[0]
    part = in_ref.shape[1] // count
    for i in range(count):
        there = pl.ds(pl.multiple_of(order_ref[i] * part, LANES), part)
        here = slice(i * part, (i + 1) * part)
        if back:
            out_ref[:, there] = in_ref[:, here].astype(out_ref.dtype)
        else:
            out_ref[:, here] = in_ref[:, there].astype(out_ref.dtype)


def reorder(value, order, dtype, back=False):
    rows, width = value.shape
    count = order.shape[0]
    part = width // count
    if part % LANES:
        blocks = value.reshape(rows, count, part)
        index = slice_places() if back else order
        return jnp.take(blocks, index, axis=1).reshape(rows, width).astype(dtype)
    spec = pl.BlockSpec((rows, width), lambda i, order_ref: (0, 0))
    return pl.pallas_call(
        partial(order_kernel, back),
        grid_spec=pltpu.PrefetchScalarGridSpec(
            num_scalar_prefetch=1, grid=(1,), in_specs=[spec], out_specs=spec
        ),
        out_shape=jax.ShapeDtypeStruct((rows, width), dtype),
    )(order, value)


def assemble_kernel(axis, window, *refs):
    parts, out_ref, held, in_sems, out_sems = refs[:-4], refs[-4], refs[-3], refs[-2], refs[-1]
    copies, at = [], 0
    for i, part in enumerate(parts):
        size = window[1] if axis else part.shape[0]
        where = (pl.ds(at, size),) if axis == 0 else (slice(None), pl.ds(at, size))
        copies.append(
            (
                pltpu.make_async_copy(
                    part.at[:, pl.ds(*window)], held.at[where], in_sems.at[i]
                ),
                pltpu.make_async_copy(held.at[where], out_ref.at[where], out_sems.at[i]),
            )
        )
        at += size
    for come, go in copies:
        come.start()
    for come, go in copies:
        come.wait()
        go.start()
    for come, go in copies:
        go.wait()


def assemble(parts, axis, window=None):
    rows, width = parts[0].shape
    window = window or (0, width)
    count = len(parts)
    shape = (rows * count, window[1]) if axis == 0 else (rows, window[1] * count)
    if window[1] % LANES or window[0] % LANES:
        return jnp.concatenate(
            [part[:, window[0] : window[0] + window[1]] for part in parts], axis=axis
        )
    return pl.pallas_call(
        partial(assemble_kernel, axis, window),
        in_specs=[pl.BlockSpec(memory_space=pl.ANY)] * count,
        out_specs=pl.BlockSpec(memory_space=pl.ANY),
        out_shape=jax.ShapeDtypeStruct(shape, parts[0].dtype),
        scratch_shapes=[
            pltpu.VMEM(shape, parts[0].dtype),
            pltpu.SemaphoreType.DMA((count,)),
            pltpu.SemaphoreType.DMA((count,)),
        ],
        compiler_params=pltpu.CompilerParams(vmem_limit_bytes=16 << 20),
        cost_estimate=pl.CostEstimate(flops=0, bytes_accessed=0, transcendentals=0),
    )(*parts)


def norm_kernel(
    low_ref, core_ref, x_ref, mid_ref, old_ref, shift_ref, gain_ref, bias_ref, stream_ref, out_ref
):
    branch = low_ref[...] + core_ref[...].astype(f32) + x_ref[...].astype(f32)
    stream = old_ref[...] + (branch + mid_ref[...].astype(f32)) + shift_ref[...]
    stream_ref[...] = stream
    centre = stream - jnp.mean(stream, axis=1, keepdims=True)
    spread_of = jnp.mean(centre * centre, axis=1, keepdims=True)
    out_ref[...] = (
        centre * lax.rsqrt(spread_of + 1e-05) * gain_ref[...] + bias_ref[...]
    ).astype(bf16)


def norm_back_kernel(
    low_ref, core_ref, x_ref, mid_ref, grad_ref, old_ref, gain_ref, sums_ref, grad_out_ref, out_ref
):
    normed_grad = low_ref[...] + core_ref[...].astype(f32) + x_ref[...].astype(f32)
    normed_grad = normed_grad + mid_ref[...].astype(f32)
    grad, old = grad_ref[...].astype(f32), old_ref[...]
    centre = old - jnp.mean(old, axis=1, keepdims=True)
    root = lax.rsqrt(jnp.mean(centre * centre, axis=1, keepdims=True) + 1e-05)
    hat = centre * root
    scaled = normed_grad * gain_ref[...]
    back = scaled - jnp.mean(scaled, axis=1, keepdims=True)
    back = root * (back - hat * jnp.mean(scaled * hat, axis=1, keepdims=True))
    result = grad + back
    grad_out_ref[...] = result
    out_ref[...] = result.astype(bf16)

    @pl.when(pl.program_id(0) == 0)
    def clear():
        sums_ref[...] = jnp.zeros_like(sums_ref)

    sums_ref[0:1, :] += jnp.sum(normed_grad * hat, axis=0, keepdims=True)
    sums_ref[1:2, :] += jnp.sum(normed_grad, axis=0, keepdims=True)
    sums_ref[2:3, :] += jnp.sum(grad, axis=0, keepdims=True)


def norm_first_kernel(order_ref, in_ref, gain_ref, bias_ref, stream_ref, out_ref):
    order_kernel(False, order_ref, in_ref, stream_ref)
    stream = stream_ref[...]
    centre = stream - jnp.mean(stream, axis=1, keepdims=True)
    spread_of = jnp.mean(centre * centre, axis=1, keepdims=True)
    out_ref[...] = (
        centre * lax.rsqrt(spread_of + 1e-05) * gain_ref[...] + bias_ref[...]
    ).astype(bf16)


def norm_first(value, order, gain, bias):
    rows, width = value.shape
    if width // order.shape[0] % LANES:
        stream = reorder(value, order, f32)
        centre = stream - jnp.mean(stream, axis=1, keepdims=True)
        spread_of = jnp.mean(centre * centre, axis=1, keepdims=True)
        return stream, (centre * lax.rsqrt(spread_of + 1e-05) * gain + bias).astype(bf16)
    steps = row_steps(rows)
    row_spec = pl.BlockSpec((rows // steps, width), lambda i, order_ref: (i, 0))
    line_spec = pl.BlockSpec((1, width), lambda i, order_ref: (0, 0))
    return call(
        norm_first_kernel,
        (order, value, gain.reshape(1, width), bias.reshape(1, width)),
        (steps,),
        [row_spec, line_spec, line_spec],
        [row_spec, row_spec],
        [jax.ShapeDtypeStruct((rows, width), dtype) for dtype in (f32, bf16)],
        scalars=1,
    )


def row_steps(rows):
    return rows // 48 if rows % 48 == 0 else 1


def norm_call(kernel, rows, width, row_values, line_values, out_shapes):
    steps = row_steps(rows)
    row_spec = pl.BlockSpec((rows // steps, width), lambda i: (i, 0))
    line_spec = pl.BlockSpec((1, width), lambda i: (0, 0))
    sum_spec = pl.BlockSpec((8, width), lambda i: (0, 0))
    return pl.pallas_call(
        kernel,
        grid=(steps,),
        in_specs=[row_spec] * len(row_values) + [line_spec] * len(line_values),
        out_specs=[row_spec if shape.shape[0] == rows else sum_spec for shape in out_shapes],
        out_shape=out_shapes,
        compiler_params=pltpu.CompilerParams(vmem_limit_bytes=40 << 20),
        cost_estimate=pl.CostEstimate(flops=0, bytes_accessed=0, transcendentals=0),
    )(*row_values, *[value.reshape(1, width) for value in line_values])


def norm_after(low, core, x_low, mid, old, shift, gain, bias):
    rows, width = old.shape
    out = [jax.ShapeDtypeStruct((rows, width), dtype) for dtype in (f32, bf16)]
    return norm_call(
        norm_kernel, rows, width, (low, core, x_low, mid, old), (shift, gain, bias), out
    )


def norm_before(low, core, x_low, mid, grad, old, gain):
    rows, width = old.shape
    out = [jax.ShapeDtypeStruct((8, width), f32)]
    out += [jax.ShapeDtypeStruct((rows, width), dtype) for dtype in (f32, bf16)]
    return norm_call(norm_back_kernel, rows, width, (low, core, x_low, mid, grad, old), (gain,), out)


def layout(lens, total, block):
    steps_index = jnp.arange(total, dtype=jnp.int32)
    blocks_first = (lens[0] + block - 1) // block
    second_start = blocks_first * block
    in_first = steps_index < lens[0]
    in_second = (steps_index >= second_start) & (steps_index < second_start + lens[1])
    return jnp.where(in_first, steps_index, jnp.where(in_second, steps_index - second_start, 0))


def rotary_tables(position):
    half_rot = ROT // 2
    lane = jnp.arange(LANES, dtype=jnp.int32) % HEAD_DIM
    freqs = 10000.0 ** (-((lane % half_rot).astype(f32) * 2.0) / ROT)
    angles = position.astype(f32)[..., None] * freqs
    cosine, sine = jnp.cos(angles), jnp.sin(angles)
    return (
        jnp.where(lane < ROT, cosine, 1.0),
        jnp.where(lane < half_rot, -sine, 0.0),
        jnp.where((lane >= half_rot) & (lane < ROT), sine, 0.0),
    )


def turn(field, cos, above, below, back=False):
    up = pltpu.roll(field, LANES - ROT // 2, 1) * above
    down = pltpu.roll(field, ROT // 2, 1) * below
    return field * cos - (up + down) if back else field * cos + (up + down)


def allowed_bias(scalars, group, first_row, rows, cols):
    first_len, second_len = scalars[2 * group], scalars[2 * group + 1]
    second_start = ((first_len + BLOCK - 1) // BLOCK) * BLOCK
    row = first_row + lax.broadcasted_iota(jnp.int32, (rows, 1), 0)
    in_second = (row >= second_start) & (row < second_start + second_len)
    start = jnp.where(row < first_len, 0, jnp.where(in_second, second_start, row))
    col = lax.broadcasted_iota(jnp.int32, (rows, cols), 1)
    return jnp.where((col >= start) & (col <= row), 0.0, neg_large)


def chunk_places(scalars, rows):
    me = scalars[4]
    return [pl.multiple_of((me ^ ((r % 2) * 2 + r // 2)) * rows, 64) for r in range(4)]


def head_mask(head):
    lane = lax.broadcasted_iota(jnp.int32, (1, LANES), 1)
    return jnp.where(lane // HEAD_DIM == head, 1.0, 0.0).astype(bf16)


def nt(left, right):
    return lax.dot_general(left, right, (((1,), (1,)), ((), ())), preferred_element_type=f32)


def nn(left, right):
    return jnp.dot(left, right, preferred_element_type=f32)


def tn(left, right):
    return lax.dot_general(left, right, (((0,), (0,)), ((), ())), preferred_element_type=f32)


def attention_kernel(
    scalars, mixed_ref, cos_ref, above_ref, below_ref, out_ref, kept_ref, sums_ref, held
):
    group = pl.program_id(0)
    rows = mixed_ref.shape[2]
    width = mixed_ref.shape[3] // 3
    total = 4 * rows
    places = chunk_places(scalars, rows)
    for r in range(4):
        at = pl.ds(places[r], rows)
        cos, above, below = cos_ref[0, at, :], above_ref[0, at, :], below_ref[0, at, :]
        for part in range(0, 2 * width, LANES):
            turned = turn(mixed_ref[r, 0, :, part : part + LANES], cos, above, below)
            if part < width:
                turned = turned.astype(bf16) * HEAD_DIM**-0.5
            kept_ref[0, at, part : part + LANES] = turned.astype(bf16)
        kept_ref[0, at, 2 * width :] = mixed_ref[r, 0, :, 2 * width :].astype(bf16)
    for first in range(0, total, TILE):
        cols = first + TILE
        bias = allowed_bias(scalars, group, first, TILE, cols)
        for pair in range(0, width, LANES):
            query = kept_ref[0, first:cols, pair : pair + LANES]
            key = kept_ref[0, :cols, width + pair : width + pair + LANES]
            value = kept_ref[0, :cols, 2 * width + pair : 2 * width + pair + LANES]
            result = None
            for head in range(LANES // HEAD_DIM):
                mask = head_mask(head)
                scores = nt(query * mask, key) + bias
                top = jnp.max(scores, axis=1, keepdims=True)
                expo = jnp.exp(scores - top)
                mass = jnp.sum(expo, axis=1, keepdims=True)
                probs16 = (expo * (1.0 / mass)).astype(bf16)
                mine = nn(probs16, value * mask)
                result = mine if result is None else result + mine
                at_head = pair // HEAD_DIM + head
                sums_ref[0, first:cols, at_head : at_head + 1] = top + jnp.log(mass)
            held[first:cols, pair : pair + LANES] = result.astype(bf16)
    for r in range(4):
        out_ref[r, 0] = held[pl.ds(places[r], rows), :]


def attention_back_kernel(
    scalars,
    kept_ref,
    sums_ref,
    grad_ref,
    cos_ref,
    above_ref,
    below_ref,
    out_ref,
    held,
    query_grad,
    key_grad,
    value_grad,
):
    group = pl.program_id(0)
    rows = grad_ref.shape[2]
    width = grad_ref.shape[3]
    total = 4 * rows
    places = chunk_places(scalars, rows)
    for r in range(4):
        held[pl.ds(places[r], rows), :] = grad_ref[r, 0]
    for first in reversed(range(0, total, TILE)):
        cols = first + TILE
        bias = allowed_bias(scalars, group, first, TILE, cols)
        for pair in range(0, width, LANES):
            lanes = slice(pair, pair + LANES)
            query = kept_ref[0, first:cols, pair : pair + LANES]
            key = kept_ref[0, :cols, width + pair : width + pair + LANES]
            value = kept_ref[0, :cols, 2 * width + pair : 2 * width + pair + LANES]
            grad = held[first:cols, lanes]
            grads = [None, None, None]
            for head in range(LANES // HEAD_DIM):
                mask = head_mask(head)
                at_head = pair // HEAD_DIM + head
                query_head, grad_head = query * mask, grad * mask
                scores = nt(query_head, key) + bias
                probs = jnp.exp(scores - sums_ref[0, first:cols, at_head : at_head + 1])
                prob_grad = nt(grad_head, value)
                mean = jnp.sum(probs * prob_grad, axis=1, keepdims=True)
                score_grad = (probs * (prob_grad - mean)).astype(bf16)
                mine = (
                    nn(score_grad, key * mask),
                    tn(score_grad, query_head),
                    tn(probs.astype(bf16), grad_head),
                )
                grads = [m if g is None else g + m for g, m in zip(grads, mine)]
            query_grad[first:cols, lanes] = grads[0]
            if cols == total:
                key_grad[:, lanes] = grads[1]
                value_grad[:, lanes] = grads[2]
            else:
                key_grad[:cols, lanes] += grads[1]
                value_grad[:cols, lanes] += grads[2]
    for r in range(4):
        at = pl.ds(places[r], rows)
        cos, above, below = cos_ref[0, at, :], above_ref[0, at, :], below_ref[0, at, :]
        for pair in range(0, width, LANES):
            query = turn(query_grad[at, pair : pair + LANES] * HEAD_DIM**-0.5, cos, above, below, True)
            key = turn(key_grad[at, pair : pair + LANES], cos, above, below, True)
            out_ref[r, 0, :, pair : pair + LANES] = query.astype(bf16)
            out_ref[r, 0, :, width + pair : width + pair + LANES] = key.astype(bf16)
        out_ref[r, 0, :, 2 * width :] = value_grad[at, :].astype(bf16)


def chunk_spec(rows, width):
    return pl.BlockSpec((4, 1, rows, width), lambda g, scalars: (0, g, 0, 0))


def group_spec(total, width):
    return pl.BlockSpec((1, total, width), lambda g, scalars: (g, 0, 0))


def attention_forward(mixed, tables, scalars, rows):
    width = mixed.shape[1] // 3
    total = 4 * rows
    attended, kept, sums = pl.pallas_call(
        attention_kernel,
        grid_spec=pltpu.PrefetchScalarGridSpec(
            num_scalar_prefetch=1,
            grid=(2,),
            in_specs=[chunk_spec(rows, 3 * width)] + [group_spec(total, LANES)] * 3,
            out_specs=[
                chunk_spec(rows, width),
                group_spec(total, 3 * width),
                group_spec(total, LANES),
            ],
            scratch_shapes=[pltpu.VMEM((total, width), bf16)],
        ),
        out_shape=[
            jax.ShapeDtypeStruct((4, 2, rows, width), bf16),
            jax.ShapeDtypeStruct((2, total, 3 * width), bf16),
            jax.ShapeDtypeStruct((2, total, LANES), f32),
        ],
        compiler_params=pltpu.CompilerParams(vmem_limit_bytes=40 << 20),
        cost_estimate=pl.CostEstimate(flops=0, bytes_accessed=0, transcendentals=0),
    )(scalars, mixed.reshape(4, 2, rows, 3 * width), *tables)
    return attended.reshape(8 * rows, width), kept, sums


def attention_backward(kept, sums, grad16, tables, scalars, rows):
    width = grad16.shape[1]
    total = 4 * rows
    mixed_grad = pl.pallas_call(
        attention_back_kernel,
        grid_spec=pltpu.PrefetchScalarGridSpec(
            num_scalar_prefetch=1,
            grid=(2,),
            in_specs=[
                group_spec(total, 3 * width),
                group_spec(total, LANES),
                chunk_spec(rows, width),
            ]
            + [group_spec(total, LANES)] * 3,
            out_specs=chunk_spec(rows, 3 * width),
            scratch_shapes=[pltpu.VMEM((total, width), bf16)]
            + [pltpu.VMEM((total, width), f32)] * 3,
        ),
        out_shape=jax.ShapeDtypeStruct((4, 2, rows, 3 * width), bf16),
        compiler_params=pltpu.CompilerParams(vmem_limit_bytes=40 << 20),
        cost_estimate=pl.CostEstimate(flops=0, bytes_accessed=0, transcendentals=0),
    )(scalars, kept, sums, grad16.reshape(4, 2, rows, width), *tables)
    return mixed_grad.reshape(8 * rows, 3 * width)


def call(kernel, args, grid, in_specs, out_specs, out_shape, scratch_shapes=(), scalars=0):
    return pl.pallas_call(
        kernel,
        grid_spec=pltpu.PrefetchScalarGridSpec(
            num_scalar_prefetch=scalars,
            grid=grid,
            in_specs=in_specs,
            out_specs=out_specs,
            scratch_shapes=scratch_shapes,
        ),
        out_shape=out_shape,
        compiler_params=pltpu.CompilerParams(vmem_limit_bytes=48 << 20),
        cost_estimate=pl.CostEstimate(flops=0, bytes_accessed=0, transcendentals=0),
    )(*args)


def mix_kernel(left_ref, right_ref, shift_ref, out_ref):
    out_ref[...] = nn(left_ref[...], right_ref[...]) + shift_ref[...]


def mix_product(normed, mixed_full, shift):
    rows, width = normed.shape
    cols = shift.shape[1]
    block = rows // 3
    return call(
        mix_kernel,
        (normed, mixed_full, shift.reshape(1, cols)),
        (3,),
        [
            pl.BlockSpec((block, width), lambda i: (i, 0)),
            pl.BlockSpec((width, cols), lambda i: (0, 0)),
            pl.BlockSpec((1, cols), lambda i: (0, 0)),
        ],
        pl.BlockSpec((block, cols), lambda i: (i, 0)),
        jax.ShapeDtypeStruct((rows, cols), f32),
    )


def hide_kernel(left_ref, right_ref, shift_ref, out_ref, slope_ref):
    value = nn(left_ref[...], right_ref[...]) + shift_ref[...]
    inner = math.sqrt(2.0 / math.pi)
    square = value * value
    bend = jnp.tanh(inner * value * (1.0 + 0.044715 * square))
    half = 0.5 * (1.0 + bend)
    out_ref[...] = (value * half).astype(bf16)
    slope = 0.5 * value * (1.0 - bend * bend) * (inner * (1.0 + 3.0 * 0.044715 * square))
    slope_ref[...] = (half + slope).astype(slope_ref.dtype)


def hide_product(normed, up_full, shift):
    rows, width = normed.shape
    cols = up_full.shape[1]
    block = rows // 6
    out = pl.BlockSpec((block, cols), lambda i: (i, 0))
    return call(
        hide_kernel,
        (normed, up_full, shift.reshape(1, cols)),
        (6,),
        [
            pl.BlockSpec((block, width), lambda i: (i, 0)),
            pl.BlockSpec((width, cols), lambda i: (0, 0)),
            pl.BlockSpec((1, cols), lambda i: (0, 0)),
        ],
        [out, out],
        [jax.ShapeDtypeStruct((rows, cols), dtype) for dtype in (bf16, f32)],
    )


def out_kernel(first_ref, second_ref, dense_ref, down_ref, out_ref):
    value = nt(first_ref[...], dense_ref[...]) + nn(second_ref[...], down_ref[...])
    out_ref[...] = value.astype(out_ref.dtype)


def out_product(attended, hidden, mixed_full, down_full, half, dtype):
    rows, width = attended.shape[0] // 2, down_full.shape[1]
    heads = attended.shape[1]
    return call(
        out_kernel,
        (attended, hidden, mixed_full, down_full),
        (width // 512,),
        [
            pl.BlockSpec((rows, heads), lambda j: (half, 0)),
            pl.BlockSpec((rows, hidden.shape[1]), lambda j: (half, 0)),
            pl.BlockSpec((512, heads), lambda j: (j, 3)),
            pl.BlockSpec((hidden.shape[1], 512), lambda j: (0, j)),
        ],
        pl.BlockSpec((rows, 512), lambda j: (0, j)),
        jax.ShapeDtypeStruct((rows, width), dtype),
    )


def nn_kernel(left_ref, right_ref, out_ref):
    out_ref[...] = nn(left_ref[...], right_ref[...]).astype(out_ref.dtype)


def nt_scaled_kernel(left_ref, right_ref, slope_ref, out_ref):
    value = nt(left_ref[...], right_ref[...]) * slope_ref[...].astype(f32)
    out_ref[...] = value.astype(out_ref.dtype)


def attended_back(grad16, mixed_full, heads):
    rows, width = grad16.shape
    block = rows // 3
    return call(
        nn_kernel,
        (grad16, mixed_full),
        (3,),
        [
            pl.BlockSpec((block, width), lambda i: (i, 0)),
            pl.BlockSpec((width, heads), lambda i: (0, 3)),
        ],
        pl.BlockSpec((block, heads), lambda i: (i, 0)),
        jax.ShapeDtypeStruct((rows, heads), bf16),
    )


def hidden_back(grad16, down_full, slope):
    rows, width = grad16.shape
    cols = slope.shape[1]
    block = rows // 2
    spec = pl.BlockSpec((block, 256), lambda i, j: (i, j))
    return call(
        nt_scaled_kernel,
        (grad16, down_full, slope),
        (2, cols // 256),
        [
            pl.BlockSpec((block, width), lambda i, j: (i, 0)),
            pl.BlockSpec((256, width), lambda i, j: (j, 0)),
            spec,
        ],
        spec,
        jax.ShapeDtypeStruct((rows, cols), bf16),
    )


def both_kernel(first_ref, second_ref, proj_ref, up_ref, out_ref):
    value = nt(first_ref[...], proj_ref[...]) + nt(second_ref[...], up_ref[...])
    out_ref[...] = value.astype(out_ref.dtype)


def normed_back(mixed_grad, pre_grad, mixed_full, up_full, half, dtype):
    rows, width = mixed_grad.shape[0] // 2, up_full.shape[0]
    return call(
        both_kernel,
        (mixed_grad, pre_grad, mixed_full, up_full),
        (width // 512,),
        [
            pl.BlockSpec((rows, mixed_grad.shape[1]), lambda j: (half, 0)),
            pl.BlockSpec((rows, pre_grad.shape[1]), lambda j: (half, 0)),
            pl.BlockSpec((512, mixed_grad.shape[1]), lambda j: (j, 0)),
            pl.BlockSpec((512, up_full.shape[1]), lambda j: (j, 0)),
        ],
        pl.BlockSpec((rows, 512), lambda j: (0, j)),
        jax.ShapeDtypeStruct((rows, width), dtype),
    )


def in_grad_kernel(left_ref, right_ref, *refs):
    value = tn(left_ref[...], right_ref[...])
    for ref in refs[:-1]:
        value = value + ref[...].astype(f32)
    refs[-1][...] = value.astype(bf16)


def in_grad(part, k, normed, grad, *others):
    rows, cols = grad.shape
    block = min(part, 256)
    steps = part // block
    spec = pl.BlockSpec((block, cols), lambda i: (i, 0))
    return call(
        in_grad_kernel,
        (normed, grad, *others),
        (steps,),
        [
            pl.BlockSpec((rows, block), lambda i: (0, k * steps + i)),
            pl.BlockSpec((rows, cols), lambda i: (0, 0)),
        ]
        + [spec] * len(others),
        spec,
        jax.ShapeDtypeStruct((part, cols), bf16),
    )


def down_grad(part, k, hidden, grad, *others):
    rows, height = hidden.shape
    block = min(part, 256)
    steps = part // block
    spec = pl.BlockSpec((height, block), lambda j: (0, j))
    return call(
        in_grad_kernel,
        (hidden, grad, *others),
        (steps,),
        [
            pl.BlockSpec((rows, height), lambda j: (0, 0)),
            pl.BlockSpec((rows, block), lambda j: (0, k * steps + j)),
        ]
        + [spec] * len(others),
        spec,
        jax.ShapeDtypeStruct((height, part), bf16),
    )


def mixed_grad_kernel(normed_ref, mixed_ref, grad_ref, attended_ref, *refs):
    split = mixed_ref.shape[1]
    values = (tn(normed_ref[...], mixed_ref[...]), tn(grad_ref[...], attended_ref[...]))
    for value, cols in zip(values, (slice(0, split), slice(split, None))):
        for ref in refs[:-1]:
            value = value + ref[:, cols].astype(f32)
        refs[-1][:, cols] = value.astype(bf16)


def mixed_weight_grad(part, k, normed, mixed_grad, grad, attended, *others):
    rows, heads = attended.shape
    width = mixed_grad.shape[1] + heads
    block = min(part, 256)
    steps = part // block
    spec = pl.BlockSpec((block, width), lambda i: (i, 0))
    slice_spec = pl.BlockSpec((rows, block), lambda i: (0, k * steps + i))
    return call(
        mixed_grad_kernel,
        (normed, mixed_grad, grad, attended, *others),
        (steps,),
        [
            slice_spec,
            pl.BlockSpec(mixed_grad.shape, lambda i: (0, 0)),
            slice_spec,
            pl.BlockSpec(attended.shape, lambda i: (0, 0)),
        ]
        + [spec] * len(others),
        spec,
        jax.ShapeDtypeStruct((part, width), bf16),
    )


def halves_kernel(axis, mid_ref, keep_ref, other_ref, *refs):
    out_ref, size = refs[-1], keep_ref.shape[axis]
    for part_ref, half in ((keep_ref, mid_ref[0]), (other_ref, 1 - mid_ref[0])):
        at = pl.ds(pl.multiple_of(half * size, LANES), size)
        if axis:
            out_ref[0, :, at] = part_ref[...].astype(f32)
        else:
            out_ref[0, at, :] = part_ref[...].astype(f32)


def place_halves(keep, other, mid, axis, layer, layers, before=None):
    rows, cols = keep.shape
    shape = (rows, 2 * cols) if axis else (2 * rows, cols)
    if cols % LANES or (axis == 0 and rows % LANES):
        line = jnp.concatenate([pick(keep, other, mid), pick(other, keep, mid)], axis=axis)
        line = line.astype(f32)[None]
        if before is None:
            return jnp.concatenate([jnp.zeros_like(line)] * layer + [line], axis=0)
        return jnp.concatenate([line, before[1:]], axis=0)
    spec = pl.BlockSpec((rows, cols), lambda i, mid_ref: (0, 0))
    given = [] if before is None else [before]
    return pl.pallas_call(
        partial(halves_kernel, axis),
        grid_spec=pltpu.PrefetchScalarGridSpec(
            num_scalar_prefetch=1,
            grid=(1,),
            in_specs=[spec, spec] + [pl.BlockSpec(memory_space=pl.ANY)] * len(given),
            out_specs=pl.BlockSpec((1, *shape), lambda i, mid_ref: (layer, 0, 0)),
        ),
        out_shape=jax.ShapeDtypeStruct((layers, *shape), f32),
        input_output_aliases={3: 0} if given else {},
        compiler_params=pltpu.CompilerParams(vmem_limit_bytes=32 << 20),
        cost_estimate=pl.CostEstimate(flops=0, bytes_accessed=0, transcendentals=0),
    )(mid.reshape(1), keep, other, *given)


def last_kernel(
    order_ref, low_ref, core_ref, x_ref, mid_ref, old_ref, shift_ref, out_ref, held
):
    branch = low_ref[...] + core_ref[...].astype(f32) + x_ref[...].astype(f32)
    held[...] = old_ref[...] + (branch + mid_ref[...].astype(f32)) + shift_ref[...]
    order_kernel(True, order_ref, held, out_ref)


def last_stream(order, low, core, x_low, mid, old, shift):
    rows, width = old.shape
    if width // order.shape[0] % LANES:
        branch = low[:rows] + core[:rows].astype(f32) + x_low.astype(f32) + mid.astype(f32)
        return reorder(old + branch + shift, order, f32, True)
    steps = row_steps(rows)
    row_spec = pl.BlockSpec((rows // steps, width), lambda i, order_ref: (i, 0))
    return call(
        last_kernel,
        (order, low, core, x_low, mid, old, shift),
        (steps,),
        [row_spec] * 5 + [pl.BlockSpec((1, width), lambda i, order_ref: (0, 0))],
        row_spec,
        jax.ShapeDtypeStruct((rows, width), f32),
        [pltpu.VMEM((rows // steps, width), f32)],
        scalars=1,
    )


def halves(value, half, axis):
    size = value.shape[axis] // 2
    return lax.dynamic_slice_in_dim(value, half * size, size, axis)


class Small:
    def __init__(self, seq, mine, tensor, mid, beside):
        self.seq, self.tensor = seq, tensor
        self.mine, self.beside = seq.settle(
            lambda mine: pair_up(mine, swap(mine, "dp", MID), mid, 0), mine[None], beside=beside
        )

    def second(self):
        def step(mine):
            for bit in side_bits():
                mine = jnp.concatenate([mine, swap(mine, "dp", bit)], axis=0)
            return mine[None]

        self.mine = self.seq.settle(step, self.mine)

    def finish(self, unpack):
        def step(mine):
            for bit in (0, 1):
                mine = pair_up(mine, swap(mine, "tensor", bit), (self.tensor >> bit) & 1, 0)
            return unpack(jnp.swapaxes(mine, 0, 1))

        return self.seq.settle(step, self.mine)


class SmallSums:
    def __init__(self, seq, norm_grads, in_bgrads, mid):
        self.seq, self.mid = seq, mid
        self.norm_grads, self.in_bgrads = norm_grads, in_bgrads
        self.layers, self.kinds = len(norm_grads), 3
        self.sides = side_bits()

    def halve(self, sums, biases, axis, half, move):
        keep, sent = halves(sums, half, axis), halves(sums, 1 - half, axis)
        split = biases.shape[0]
        received = move(jnp.concatenate([biases, sent.reshape(-1)]))
        return keep + received[split:].reshape(keep.shape), received[:split]

    def side(self, s, sums, biases):
        sums, other = self.halve(
            sums, biases, 1, 0, lambda value: swap(value, "dp", self.sides[s])
        )
        return sums, biases + other

    def first(self):
        tensor = lax.axis_index("tensor")

        def step(*values):
            sums = jnp.stack([value[: self.kinds] for value in values[: self.layers]])
            biases = jnp.concatenate(values[self.layers :])
            shape = (self.layers * self.kinds, 1 << len(self.sides), 2, lax.axis_size("tensor"), -1)
            sums, biases = self.side(len(self.sides) - 1, sums.reshape(shape), biases)
            none = biases[:0]
            for bit in (1, 0):
                sums, _ = self.halve(
                    sums, none, 3, (tensor >> bit) & 1, lambda value: swap(value, "tensor", bit)
                )
            return sums, biases

        values = [value for pair in self.in_bgrads for value in pair]
        self.sums, self.biases = self.seq.settle(step, *self.norm_grads, *values)

    def second(self):
        def step(sums, biases):
            for s in reversed(range(len(self.sides) - 1)):
                sums, biases = self.side(s, sums, biases)
            return sums, biases

        self.sums, self.biases = self.seq.settle(step, self.sums, self.biases)

    def finish(self):
        def step(sums, biases):
            sums, other = self.halve(
                sums, biases, 2, self.mid, lambda value: swap(value, "dp", MID)
            )
            pair = (pick(biases, other, self.mid), pick(other, biases, self.mid))
            return sums, jnp.concatenate(pair)

        sums, biases = self.seq.settle(step, self.sums, self.biases)
        return sums.reshape(self.layers, self.kinds, -1), biases.reshape(2, -1)


def shards(
    tokens_in,
    lengths,
    norm_gain,
    norm_bias,
    proj_weight,
    proj_bias,
    dense_weight,
    dense_bias,
    up_weight,
    up_bias,
    down_weight,
    down_bias,
    cotangent,
):
    rows, width = tokens_in.shape
    layer_count = proj_weight.shape[0]
    n_dp = lax.axis_size("dp")
    dp = lax.axis_index("dp")
    tensor = lax.axis_index("tensor")
    mid = (dp >> MID) & 1
    order = slice_order()
    seq = Sequence(lengths[0, 0].astype(f32), lengths[0, 0] > 0)

    def take_mixed(l, half, weight=proj_weight):
        proj = halves(weight[l], half, 2).reshape(weight.shape[1], -1)
        return jnp.concatenate([proj, halves(dense_weight[l], half, 0).T], axis=1)

    def take_up(l, half, weight=up_weight):
        return halves(weight[l], half, 1)

    def take_down(l, half, weight=down_weight):
        return halves(weight[l], half, 0)

    takes = ((take_mixed, 0), (take_up, 0), (take_down, 1))

    def set_out(l, i):
        weight = (proj_weight, up_weight, down_weight)[i]
        part = seq.run(lambda value: takes[i][0](l, 1 - mid, value), weight, apart=True)
        return seq.start(part, "dp", MID)

    def paired(l, i, moving):
        return joined(l, i, seq.wait(moving))

    def joined(l, i, received):
        take, axis = takes[i]
        block = seq.run(
            lambda other: pair_up(take(l, mid), other, mid, axis), received, apart=True
        )
        return Spread(seq, block, axis)

    moving = [set_out(0, 0), set_out(0, 1)]
    cot = seq.run(lambda value: reorder(value, order, bf16), cotangent)
    whole_lens = lengths.reshape(-1).astype(f32)
    coarse = jnp.floor(whole_lens / 8.0)
    small = Small(
        seq,
        jnp.concatenate(
            [
                value.reshape(-1)
                for value in (norm_gain, norm_bias, dense_bias, down_bias, proj_bias, up_bias)
            ]
            + [coarse.astype(bf16), (whole_lens - 8.0 * coarse).astype(bf16)]
        ),
        tensor,
        mid,
        lambda: swap(cot, "tensor", 1),
    )
    cot_across = small.beside
    small.second()
    m0 = paired(0, 0, moving[0])
    u0 = paired(0, 1, moving[1])
    m0.near()
    m0.far()
    sent = seq.run(lambda value: take_down(0, 1 - mid, value), down_weight, apart=True)
    each, proj_each, up_each = norm_gain.shape[1], proj_bias.shape[3], up_bias.shape[2]

    def unpack(everyone):
        pair_lens = lax.dynamic_index_in_dim(everyone[:2, :, -4:], tensor, 1, keepdims=False)
        pair_lens = pair_lens.astype(f32)
        pair_lens = (pair_lens[:, :2] * 8.0 + pair_lens[:, 2:]).astype(jnp.int32)
        lens = pick(pair_lens, pair_lens[::-1], mid)
        everyone = everyone[:, :, :-4]
        at = 4 * layer_count * each
        norm_parts = everyone[:, :, :at].reshape(n_dp, -1, 4 * layer_count, each)
        norm_parts = jnp.transpose(norm_parts, (2, 0, 1, 3)).reshape(4, layer_count, width)
        norm_parts = norm_parts.astype(f32)
        same_heads = lax.dynamic_index_in_dim(everyone[:, :, at:], tensor, 1, keepdims=False)
        same_heads = halves(same_heads[slice_places()], mid, 0).astype(f32)
        proj_at = layer_count * 3 * proj_each
        proj_shift = jnp.transpose(
            same_heads[:, :proj_at].reshape(-1, layer_count * 3, proj_each), (1, 0, 2)
        ).reshape(layer_count, -1)
        up_shift = jnp.transpose(
            same_heads[:, proj_at:].reshape(-1, layer_count, up_each), (1, 0, 2)
        ).reshape(layer_count, -1)
        gains, biases = norm_parts[0], norm_parts[1]
        shifts = norm_parts[2] + norm_parts[3]
        scalars = jnp.concatenate([lens.reshape(-1), tensor[None].astype(jnp.int32)])
        lines = [value[l] for value in (gains, biases, shifts) for l in range(layer_count)]
        lines += [value[l] for value in (proj_shift, up_shift) for l in range(layer_count)]
        return [line[None] for line in lines], lens, scalars.astype(jnp.int32)

    lines, lens, scalars = small.finish(unpack)
    gains, biases, out_shifts, proj_shift, up_shift = (
        lines[i * layer_count : (i + 1) * layer_count] for i in range(5)
    )

    def mix(l, normed, proj_full):
        return seq.run(mix_product, normed, proj_full, proj_shift[l])

    def attend(mixed):
        return seq.run(lambda value: attention_forward(value, tables, scalars, rows), mixed)

    def hide(l, normed, up_full):
        return seq.run(hide_product, normed, up_full, up_shift[l])

    def make_tables():
        return rotary_tables(jax.vmap(partial(layout, total=4 * rows, block=BLOCK))(lens))

    stream, own = seq.run(
        lambda value: norm_first(value, order, gains[0], biases[0]), tokens_in
    )
    mid_rows, across = seq.start(own, "dp", MID), seq.start(own, "tensor", 1)
    moving = seq.start(sent, "dp", MID)
    tables = seq.run(make_tables, apart=True)
    across = seq.wait(across)
    m0.near_wait()
    m0.far_wait()
    m0.last()
    u0.far()
    core_parts = seq.settle(
        lambda *values: tuple(swap(value, "tensor", 0) for value in values), own, across
    )
    u0.near()
    token_parts = (own, seq.wait(mid_rows), across, *core_parts)

    def finish_first(own, mid, across, core_own, core_across):
        both = swap(mid, "tensor", 1)
        both, mid = lax.optimization_barrier((both, mid))
        core_both = swap(both, "tensor", 0)
        core_both, mid = lax.optimization_barrier((core_both, mid))
        core_mid = swap(mid, "tensor", 0)
        parts = (own, mid, across, both, core_own, core_mid, core_across, core_both)
        return assemble(parts, 0)

    normed = seq.settle(finish_first, *token_parts)
    received = seq.wait(moving)
    seq.tick(7)
    d0 = joined(0, 2, received)
    m0.last_wait()
    u0.far_wait()
    seq.tick(1)
    u0.near_wait()
    u0.last()
    d0.far()
    d0.near()
    mixed_full = m0.whole()
    mixed = mix(0, normed, mixed_full)
    attended, kept, sums = attend(mixed)
    u0.last_wait()
    seq.tick(1)
    up_full = u0.whole()
    hidden, slope = hide(0, normed, up_full)
    d0.far_wait()
    seq.tick(3)
    d0.near_wait()
    d0.last()
    m1 = paired(1, 0, set_out(1, 0))
    m1.far()
    moving = set_out(1, 1)
    cot_mid = seq.start(cot, "dp", MID)
    d0.last_wait()
    down_full = d0.whole()
    m1.near()
    saved = [(normed, kept, sums, slope, attended, hidden)]
    weights = [(mixed_full, up_full, down_full)]
    streams = [stream]

    branch = Scatter(seq, out_product, (attended, hidden, mixed_full, down_full), rows)
    branch.begin()
    u1 = paired(1, 1, moving)
    moving = set_out(1, 2)
    branch.second()
    cot_mid = seq.wait(cot_mid)
    d1 = paired(1, 2, moving)
    m1.far_wait()
    seq.tick(2)
    m1.near_wait()
    m1.last()
    branch.third()
    u1.near()
    u1.far()
    stream, own = branch.finish(
        norm_after, stream, out_shifts[0], gains[1], biases[1]
    )
    streams.append(stream)

    def with_cores(mine, mid, cot, across):
        parts, both = gather_start_beside(mine, mid)
        *parts, cot, across = lax.optimization_barrier((*parts, cot, across))
        return parts, both, swap(cot, "tensor", 0), swap(across, "tensor", 0)

    parts, cot_both, cot_core_own, cot_core_across = seq.settle(
        with_cores, own, cot_mid, cot, cot_across
    )
    m1.last_wait()
    u1.near_wait()
    u1.far_wait()
    d1.near()
    d1.far()
    u1.last()
    grad16, normed, mixed_full = seq.settle(
        lambda *values: gather_finish_beside(values[:5], values[5:], m1.plain),
        *parts,
        cot,
        cot_mid,
        cot_across,
        cot_both,
        cot_core_own,
        cot_core_across,
    )
    mixed = mix(1, normed, mixed_full)
    d1.near_wait()
    u1.last_wait()
    attended, kept, sums = attend(mixed)
    up_full = u1.whole()
    hidden, slope = hide(1, normed, up_full)
    d1.far_wait()
    d1.last()
    saved.append((normed, kept, sums, slope, attended, hidden))
    weights.append((mixed_full, up_full, None))

    heads_width = attended.shape[1]
    parts = 1 << len(side_bits())
    norm_grads, in_bgrads = [None] * layer_count, [None] * layer_count

    part = width // parts

    def down_grads(l, grad16):
        return Reduce(seq, partial(down_grad, part), saved[l][5], grad16)

    def up_grads(l, grad):
        return Reduce(seq, partial(in_grad, part), saved[l][0], grad)

    def mixed_grads(l, grad, grad16):
        values = saved[l][0], grad, grad16, saved[l][4]
        return Reduce(seq, partial(mixed_weight_grad, part), *values)

    def attend_back(l, grad16):
        kept, sums = saved[l][1:3]
        mixed_full = weights[l][0]

        def step(value):
            grad = attended_back(value, mixed_full, heads_width)
            return attention_backward(kept, sums, grad, tables, scalars, rows)

        return seq.run(step, grad16)

    def hide_back(l, grad16):
        slope, down_full = saved[l][3], weights[l][2]
        return seq.run(lambda value: hidden_back(value, down_full, slope), grad16)

    def rows_back(l, mixed_grad, pre_grad):
        return Scatter(seq, normed_back, (mixed_grad, pre_grad, *weights[l][:2]), rows)

    def bias_back(mixed_grad, pre_grad):
        return jnp.sum(mixed_grad, axis=0, dtype=f32), jnp.sum(pre_grad, axis=0, dtype=f32)

    def own_start(total, axis):
        return halves(total, mid, axis), seq.start(halves(total, 1 - mid, axis), "dp", MID)

    def own_wait(pair):
        keep, moving = pair
        received = seq.wait(moving)
        return pick(keep, received, mid).astype(f32), pick(received, keep, mid).astype(f32)

    first, second = 0, 1
    early = len(side_bits()) == 2

    def send(reduce, which):
        reduce.send(reduce.near(which))

    def arrive(reduce, which):
        reduce.wait(reduce.near(which))

    def rest(reduce):
        for which in (first, second):
            reduce.make(reduce.near(which))
            send(reduce, which)
            arrive(reduce, which)
        reduce.make_far()
        reduce.send_far()
        reduce.wait_far()
        reduce.finish()

    down2 = down_grads(1, grad16)
    down2.make(down2.near(first))
    if early:
        send(down2, first)
    mixed_grad = attend_back(1, grad16)
    d1.last_wait()
    weights[1] = (mixed_full, up_full, d1.whole())
    if early:
        down2.make(down2.near(second))
        send(down2, second)
    pre_grad = hide_back(1, grad16)
    up2, mix2 = up_grads(1, pre_grad), mixed_grads(1, mixed_grad, grad16)
    back = rows_back(1, mixed_grad, pre_grad)
    back.begin()
    branch = Scatter(seq, out_product, (attended, hidden, *weights[1][::2]), rows)
    if early:
        arrive(down2, first)
        up2.make(up2.near(first))
        send(up2, first)
    made = back.second(
        lambda: (
            down2.plain(down2.far()) if early else (),
            up2.plain(up2.near(second)),
            mix2.plain(mix2.near(first)),
            mix2.plain(mix2.near(second)),
            bias_back(mixed_grad, pre_grad),
        )
    )
    in_bgrads[1] = made[4]
    if early:
        down2.take(down2.far(), made[0])
        up2.take(up2.near(second), made[1])
        mix2.take(mix2.near(first), made[2])
        mix2.take(mix2.near(second), made[3])
        arrive(down2, second)
        seq.tick(4)
        arrive(up2, first)
        send(up2, second)
    made = back.third(lambda: (up2.plain(up2.far()) if early else (), branch.plain()))
    branch.take(made[1])
    norm_grads[1], grad_stream, own = back.finish(
        norm_before, cot, streams[1], gains[1]
    )
    if early:
        up2.take(up2.far(), made[0])
        arrive(up2, second)
        send(mix2, first)
        down2.send_far()
    (branch.later, branch.x_high), coming = seq.settle(
        lambda own, low, core: gather_start_with(own, low, core, branch.sent_across),
        own,
        branch.low_part,
        branch.core,
    )
    if early:
        arrive(mix2, first)
        send(mix2, second)
        up2.send_far()
        grad16, made = seq.settle(gather_finish, *coming, beside=lambda: mix2.plain(mix2.far()))
        mix2.take(mix2.far(), made)
        mix2.send_far()
        down2.wait_far()
    else:
        grad16 = seq.settle(gather_finish, *coming)
        rest(down2)
        rest(up2)
        rest(mix2)

    results = {}

    def own_start(total, axis):
        keep, sent = seq.run(
            lambda value: (halves(value, mid, axis), halves(value, 1 - mid, axis)),
            total,
            apart=True,
        )
        return keep, seq.start(sent, "dp", MID)

    def own_finish(l, name, axis, pair):
        keep, moving = pair
        received = seq.wait(moving)
        before = results.get(name)
        given = () if before is None else (before,)
        results[name] = seq.run(
            lambda keep, other, *given: place_halves(
                keep, other, mid, axis, l, layer_count, *given
            ),
            keep,
            received,
            *given,
        )

    def mixed_finish(pair):
        keep, moving = pair
        received = seq.wait(moving)
        cols = 3 * heads_width

        def step(keep, other):
            pair = [pick(keep, other, mid).astype(f32), pick(other, keep, mid).astype(f32)]
            proj = [value[:, :cols].reshape(value.shape[0], 3, -1) for value in pair]
            dense = [value[:, cols:].T for value in pair]
            return jnp.concatenate(proj, axis=2), jnp.concatenate(dense, axis=0)

        return seq.run(step, keep, received, apart=True)

    down1 = down_grads(0, grad16)
    down1.make(down1.near(first))
    if early:
        send(down1, first)
        down2.make([0])
    sent = seq.run(branch.next, branch.low_part, branch.core, branch.x_high, apart=True)
    branch_mid = seq.start(sent, "dp", MID)
    mixed_grad = attend_back(0, grad16)
    if early:
        up2.wait_far()
        arrive(mix2, second)
    pre_grad = hide_back(0, grad16)
    up1, mix1 = up_grads(0, pre_grad), mixed_grads(0, mixed_grad, grad16)
    up1.make(up1.near(first))
    if early:
        send(up1, first)
        up2.make([0])
    branch.mid = seq.wait(branch_mid)
    if early:
        mix2.wait_far()
        seq.tick(2)
        arrive(down1, first)
        down1.make_far()
        down1.send_far()
    branch_low = seq.start(branch.later, "tensor", 1)
    up2_pair = own_start(up2.blocks[0], 0)
    up1.make(up1.near(second))
    mix1.make(mix1.near(first))
    down1.make(down1.near(second))
    if early:
        arrive(up1, first)
        up1.make_far()
        send(down1, second)
    branch.x_low = seq.wait(branch_low)
    down2_pair = own_start(down2.blocks[0], 1)
    back = rows_back(0, mixed_grad, pre_grad)
    back.begin()
    if early:
        down1.wait_far()
        up1.send_far()
    own_finish(1, "up", 1, up2_pair)
    if early:
        send(mix1, first)
    made = back.second(
        lambda: (
            mix1.plain(mix1.near(second)),
            bias_back(mixed_grad, pre_grad),
        )
    )
    mix1.take(mix1.near(second), made[0])
    in_bgrads[0] = made[1]
    own_finish(1, "down", 0, down2_pair)
    if early:
        seq.tick(2)
        arrive(down1, second)
        seq.tick(4)
        arrive(mix1, first)
        send(up1, second)
        send(mix1, second)
    made = back.third(
        lambda: (mix1.plain(mix1.far()), down1.plain([0]), mix2.plain([0])) if early else ()
    )
    norm_grads[0], grad_stream, own = back.finish(
        norm_before, grad_stream, streams[0], gains[0]
    )
    if early:
        mix1.take(mix1.far(), made[0])
        down1.take([0], made[1])
        mix2.take([0], made[2])
        up1.wait_far()
        seq.tick(7)
        arrive(up1, second)
        arrive(mix1, second)
        mix1.send_far()
    else:
        rest(down1)
        rest(up1)
        rest(mix1)
    mix2_pair = own_start(mix2.blocks[0], 0)
    down1_pair = own_start(down1.blocks[0], 1)
    if early:
        up1.make([0])
    up1_pair = own_start(up1.blocks[0], 0)
    small_sums = SmallSums(seq, norm_grads, in_bgrads, mid)
    small_sums.first()
    activations = branch.finish(partial(last_stream, order), streams[1], out_shifts[1])
    input_grad = seq.run(lambda value: reorder(value, order, f32, True), grad_stream)
    mix2_own = mixed_finish(mix2_pair)
    if early:
        mix1.wait_far()
        mix1.make([0])
    mix1_pair = own_start(mix1.blocks[0], 0)
    small_sums.second()
    own_finish(0, "down", 0, down1_pair)
    own_finish(0, "up", 1, up1_pair)
    seq.tick(1)
    norm_owned, bias_both = small_sums.finish()
    mix1_own = mixed_finish(mix1_pair)
    bias_both = bias_both + 0.0 * seq.scalar
    per_layer = bias_both.shape[1] // layer_count
    bias_both = bias_both.reshape(2, layer_count, per_layer)
    proj_b = jnp.transpose(
        bias_both[:, :, : 3 * heads_width].reshape(2, layer_count, 3, heads_width), (1, 2, 0, 3)
    ).reshape(layer_count, 3, 1, 2 * heads_width)
    up_b = jnp.transpose(bias_both[:, :, 3 * heads_width :], (1, 0, 2)).reshape(layer_count, 1, -1)
    return (
        activations,
        input_grad,
        norm_owned[:, 0],
        norm_owned[:, 1],
        jnp.stack([mix1_own[0], mix2_own[0]]),
        lax.dynamic_slice_in_dim(proj_b, dp * proj_each, proj_each, 3),
        jnp.stack([mix1_own[1], mix2_own[1]]),
        norm_owned[:, 2],
        results["up"],
        lax.dynamic_slice_in_dim(up_b, dp * up_each, up_each, 2),
        results["down"],
        norm_owned[:, 2],
    )


def solution(mesh):
    in_specs = (
        P(("dp", "tensor"), None),
        P("dp", None),
        P(None, ("dp", "tensor")),
        P(None, ("dp", "tensor")),
        P(None, "dp", None, "tensor"),
        P(None, None, "tensor", "dp"),
        P(None, "tensor", "dp"),
        P(None, ("dp", "tensor")),
        P(None, "dp", "tensor"),
        P(None, "tensor", "dp"),
        P(None, "tensor", "dp"),
        P(None, ("dp", "tensor")),
        P(("dp", "tensor"), None),
    )
    out_specs = (
        P(("dp", "tensor"), None),
        P(("dp", "tensor"), None),
        P(None, ("dp", "tensor")),
        P(None, ("dp", "tensor")),
        P(None, "dp", None, "tensor"),
        P(None, None, "tensor", "dp"),
        P(None, "tensor", "dp"),
        P(None, ("dp", "tensor")),
        P(None, "dp", "tensor"),
        P(None, "tensor", "dp"),
        P(None, "tensor", "dp"),
        P(None, ("dp", "tensor")),
    )
    return jax.shard_map(shards, mesh=mesh, in_specs=in_specs, out_specs=out_specs, check_vma=False)
```
